32 devices in a mesh: grp: 2 (over x), cell: 16 (over z, y, core).
Axes of the slice: x: 2, y: 2, z: 4, core: 2. Of those that a mesh axis runs over, the one named last changes fastest.
Arguments:
- jac_blocks: bfloat16 [448, 640, 640], P(('grp', 'cell')), parts along dimension 0, may hold values from -0.3125 to 0.3125
- modes: bfloat16 [81920, 256], P(('grp', 'cell')), parts along dimension 0, may hold values from -1.5 to 1.5
- neighbours: int32 [448, 2], P(('grp', 'cell')), parts along dimension 0, may hold values from -1 to 63, as said below
Outputs:
- projected: float32 [512, 256], P(('grp', 'cell')), parts along dimension 0
The draws below stay inside these ranges and needn't reach their ends.
There are 2 independent parts, one for each index of `grp`. The reference program is written for one: setup_inputs(seed, part) draws one part's arguments, and reference() takes and returns one part's arrays. A program takes and returns all parts, laid end to end along the dimension named above; each array names one. Nothing has to cross between parts.
Inputs may be any that keep to these rules, and one draw needn't show every extreme that they name: `neighbours`: slot j < 4 of each device is its diagonal block (j, d * 4 + j). Every other live slot (r, c) of device d has c = d * 4 + r - 1 or c = d * 4 + r + 1, so it couples a block row only to the block just before or after it, which may be the last block of the previous device or the first of the next. Column and row are both -1 or both live. Counts of live slots differ from device to device; some device has all 14 slots live.
All inputs are finite; a program needn't handle non-finite values.
Results may differ from the reference program's by a relative error of at most 0.0003.
Values may be sent and summed in bfloat16 or wider, within the bound.
No kernel may reach another device: no remote copies, remote signals or barrier semaphores. Data moves between devices by JAX's collectives and lax.ppermute only.
A program may use at most 128 MiB of HBM per device.

```python
import jax
import jax.numpy as jnp
from jax import lax

BW = 640
MODES = 256
B_DEV = 4
NNZ_DEV = 14
NB = 64
NNZ = 224
ROWS = 40960
N_CELL = 16


def draw_neighbours(key, part):
    key = jax.random.fold_in(key, 7)
    key_rows, key_sides, key_count, key_full = jax.random.split(key, 4)
    extra = 2 * B_DEV
    device = jnp.arange(N_CELL, dtype=jnp.int32)[:, None]
    rand_rows = jax.random.randint(key_rows, (N_CELL, extra), 0, B_DEV).astype(jnp.int32)
    sides = jax.random.randint(key_sides, (N_CELL, extra), 0, 2).astype(jnp.int32) * 2 - 1
    count = jax.random.randint(key_count, (N_CELL,), 0, extra + 1).astype(jnp.int32)
    fullest = jax.random.randint(key_full, (), 1, N_CELL - 1).astype(jnp.int32)
    count = jnp.where(jnp.arange(N_CELL, dtype=jnp.int32) == fullest, extra, count)
    diag_rows = jnp.broadcast_to(jnp.arange(B_DEV, dtype=jnp.int32)[None, :], (N_CELL, B_DEV))
    diag_cols = device * B_DEV + diag_rows
    face_rows = jnp.broadcast_to(jnp.array([0, B_DEV - 1], jnp.int32)[None, :], (N_CELL, 2))
    face_cols = jnp.concatenate([device * B_DEV - 1, device * B_DEV + B_DEV], 1)
    rand_cols = device * B_DEV + rand_rows + sides
    slot_rows = jnp.concatenate([diag_rows, face_rows, rand_rows], 1)
    slot_cols = jnp.concatenate([diag_cols, face_cols, rand_cols], 1)
    position = jnp.arange(NNZ_DEV, dtype=jnp.int32)[None, :]
    valid = (slot_cols >= 0) & (slot_cols < NB) & (position < B_DEV + 2 + count[:, None])
    slot_rows = jnp.where(valid, slot_rows, -1)
    slot_cols = jnp.where(valid, slot_cols, -1)
    return jnp.stack([slot_rows, slot_cols], -1).reshape(NNZ, 2).astype(jnp.int32)


def raised(values, key, source, target, shards_of, factor):
    owner, partner = [(jnp.arange(values.shape[dim]) // (values.shape[dim] // shards_of)).reshape([-1 if axis == dim else 1 for axis in range(values.ndim)]) for dim in (source, target)]
    chosen = jax.random.permutation(key, shards_of)[partner]
    strong = (owner == chosen) | (owner == (partner + shards_of // 2) % shards_of)
    return jnp.where(strong, factor * values, values)


def shard_levels(own_key, shape, cuts, least, high):
    def one(dim, blocks):
        draws = jax.random.uniform(jax.random.fold_in(jax.random.fold_in(own_key, 6), dim), (blocks,), jnp.float32, least / len(cuts), high / len(cuts))
        return jnp.repeat(jnp.exp(draws), shape[dim] // blocks).reshape((-1,) + (1,) * (len(shape) - dim - 1))

    loudness = one(*cuts[0])
    for cut in cuts[1:]:
        loudness = loudness * one(*cut)
    return loudness


def bell_draw(stream_key, shape, deviation, bound, cuts=(), held_as=jnp.bfloat16):
    entries = deviation * jax.random.normal(stream_key, shape, jnp.float32)
    if cuts:
        entries = entries * shard_levels(stream_key, shape, cuts, -0.22, 0.18)
    return jnp.clip(entries, -bound, bound).astype(held_as)


def bell_draw_with(stream_key, shape, width, most, pieces, heavy, held_as=jnp.bfloat16):
    result = width * jax.random.normal(stream_key, shape, jnp.float32)
    if pieces:
        result = result * shard_levels(stream_key, shape, pieces, -0.22, 0.18)
    return jnp.clip(raised(result, jax.random.fold_in(stream_key, 3), *heavy), -most, most).astype(held_as)


def setup_inputs(seed: int = 0, part: int = 0) -> dict:
    seeds = jax.random.split(jax.random.key(seed), 4)
    part_keys = jax.random.split(jax.random.fold_in(seeds[3], part), 4)
    return {
        "jac_blocks": bell_draw(part_keys[0], (NNZ, BW, BW), ((BW * 3) ** -0.5), 0.3125, ((0, 16),)),
        "modes": bell_draw_with(part_keys[1], (ROWS, MODES), (ROWS ** -0.25), 1.5, ((0, 16),), (0, 1, 16, 2.0)),
        "neighbours": draw_neighbours(jax.random.fold_in(jax.random.fold_in(seeds[3], part), 71), part),
    }


def reference(jac_blocks, modes, neighbours):
    n_devs = NB // B_DEV
    mode_blocks = modes.reshape(NB, BW, MODES)
    jac_dev = jac_blocks.reshape(n_devs, NNZ_DEV, BW, BW)
    lists_dev = neighbours.reshape(n_devs, NNZ_DEV, 2)
    mode_dev = modes.reshape(n_devs, B_DEV, BW, MODES)

    def one_device(total, inputs):
        jac_here, list_here, mode_here = inputs
        slot_rows = list_here[:, 0]
        slot_cols = jnp.clip(list_here[:, 1], 0, NB - 1).astype(jnp.int32)
        picked = mode_blocks[slot_cols].astype(jnp.float32)
        products = jnp.einsum("sij,sjm->sim", jac_here.astype(jnp.float32), picked,
                              precision=lax.Precision.HIGHEST)
        selector = (slot_rows[None, :] == jnp.arange(B_DEV, dtype=jnp.int32)[:, None]).astype(jnp.float32)
        jv_rows = jnp.einsum("rs,sim->rim", selector, products, precision=lax.Precision.HIGHEST)
        part = jnp.einsum("rim,rin->mn", mode_here.astype(jnp.float32), jv_rows,
                          precision=lax.Precision.HIGHEST)
        return total + part, None

    start = jnp.zeros((MODES, MODES), jnp.float32)
    total, unused = lax.scan(one_device, start, (jac_dev, lists_dev, mode_dev))
    return total
```

```python
import functools

import jax
import jax.numpy as jnp
from jax import lax
from jax.experimental import pallas as pl
from jax.experimental.pallas import tpu as pltpu
from jax.sharding import PartitionSpec as P

OWN_VMEM = 54 * 2**20
JOIN_VMEM = 8 * 2**20


def dot(a, b):
    return jnp.dot(a, b, preferred_element_type=jnp.float32)


def halves(value):
    upper = value.astype(jnp.bfloat16)
    return upper, (value - upper.astype(jnp.float32)).astype(jnp.bfloat16)


def own_kernel(blocks, nb_ref, jac_hbm, modes_hbm, p_ref, t_ref, jac, modes, turned, jv, face, sems, mode_sem):
    slots, width, _ = jac_hbm.shape
    load_modes = pltpu.make_async_copy(modes_hbm, modes, mode_sem)
    load_modes.start()
    for s in range(slots):
        pltpu.make_async_copy(jac_hbm.at[s], jac.at[s], sems.at[s]).start()
    face[...] = jnp.zeros_like(face)
    load_modes.wait()
    for k in range(blocks):
        turned[k] = modes[pl.ds(k * width, width), :].T
    base = nb_ref[1, 0]
    for s in range(blocks):
        pltpu.make_async_copy(jac_hbm.at[s], jac.at[s], sems.at[s]).wait()
        jv[s] = dot(jac[s], modes[pl.ds(s * width, width), :])

    def step(s, carry):
        pltpu.make_async_copy(jac_hbm.at[s], jac.at[s], sems.at[s]).wait()
        r = nb_ref[0, s]
        c = nb_ref[1, s] - base
        live = r >= 0

        @pl.when(live & (c >= 0) & (c < blocks))
        def _():
            rows = pl.ds(pl.multiple_of(c * width, width), width)
            jv[r] += dot(jac[s], modes[rows, :])

        @pl.when(live & (c < 0))
        def _():
            face[0] += dot(turned[0], jac[s])

        @pl.when(live & (c >= blocks))
        def _():
            face[1] += dot(turned[blocks - 1], jac[s])

        return carry

    lax.fori_loop(blocks, slots, step, 0)
    total = jnp.zeros(p_ref.shape, jnp.float32)
    for k in range(blocks):
        upper, lower = halves(jv[k])
        total += dot(turned[k], upper) + dot(turned[k], lower)
    p_ref[...] = total
    for side in range(2):
        upper, lower = halves(face[side])
        t_ref[side, 0] = upper
        t_ref[side, 1] = lower


def own_part(neighbours, jac_blocks, modes):
    slots, width, _ = jac_blocks.shape
    rows, n_modes = modes.shape
    blocks = rows // width
    flops = 2 * n_modes * width * width * slots + 4 * rows * n_modes * n_modes
    return pl.pallas_call(
        functools.partial(own_kernel, blocks),
        out_shape=(
            jax.ShapeDtypeStruct((n_modes, n_modes), jnp.float32),
            jax.ShapeDtypeStruct((2, 2, n_modes, width), jnp.bfloat16),
        ),
        in_specs=[
            pl.BlockSpec(memory_space=pltpu.SMEM),
            pl.BlockSpec(memory_space=pl.ANY),
            pl.BlockSpec(memory_space=pl.ANY),
        ],
        out_specs=(pl.BlockSpec(memory_space=pltpu.VMEM), pl.BlockSpec(memory_space=pltpu.VMEM)),
        scratch_shapes=[
            pltpu.VMEM((slots, width, width), jnp.bfloat16),
            pltpu.VMEM((rows, n_modes), jnp.bfloat16),
            pltpu.VMEM((blocks, n_modes, width), jnp.bfloat16),
            pltpu.VMEM((blocks, width, n_modes), jnp.float32),
            pltpu.VMEM((2, n_modes, width), jnp.float32),
            pltpu.SemaphoreType.DMA((slots,)),
            pltpu.SemaphoreType.DMA,
        ],
        compiler_params=pltpu.CompilerParams(vmem_limit_bytes=OWN_VMEM),
        cost_estimate=pl.CostEstimate(
            flops=flops, bytes_accessed=slots * width * width * 2 + rows * n_modes * 2, transcendentals=0
        ),
        name="own_part",
    )(neighbours, jac_blocks, modes)


def join_kernel(p_ref, t_ref, before_ref, after_ref, out_ref):
    total = p_ref[...]
    for side, halo in enumerate((before_ref, after_ref)):
        for part in range(2):
            total += dot(t_ref[side, part], halo[...])
    out_ref[...] = total


def join(p, t, before, after):
    return pl.pallas_call(
        join_kernel,
        out_shape=jax.ShapeDtypeStruct(p.shape, jnp.float32),
        in_specs=[pl.BlockSpec(memory_space=pltpu.VMEM)] * 4,
        out_specs=pl.BlockSpec(memory_space=pltpu.VMEM),
        compiler_params=pltpu.CompilerParams(vmem_limit_bytes=JOIN_VMEM),
        name="join",
    )(p, t, before, after)


def per_device(jac_blocks, modes, neighbours):
    width = jac_blocks.shape[1]
    rows, n_modes = modes.shape
    count = lax.axis_size("cell")
    ends = count - 1
    before = lax.ppermute(modes[rows - width :], "cell", [(i, i + 1) for i in range(ends)])
    after = lax.ppermute(modes[:width], "cell", [(i + 1, i) for i in range(ends)])
    p, t = own_part(neighbours.T, jac_blocks, modes)
    total = join(p, t, before, after)
    parts = lax.all_to_all(total.reshape(count, n_modes // count, n_modes), "cell", 0, 0)
    return jnp.sum(parts, axis=0)


def solution(mesh):
    placed = (P(("grp", "cell"), None, None), P(("grp", "cell"), None), P(("grp", "cell"), None))
    return jax.shard_map(
        per_device, mesh=mesh, in_specs=placed, out_specs=P(("grp", "cell"), None), check_vma=False
    )
```

```python
import functools

import jax
import jax.numpy as jnp
from jax import lax
from jax.experimental import pallas as pl
from jax.experimental.pallas import tpu as pltpu
from jax.sharding import PartitionSpec as P

OWN_VMEM = 48 * 2**20
JOIN_VMEM = 8 * 2**20


def dot(a, b):
    return jnp.dot(a, b, preferred_element_type=jnp.float32)


def halves(value):
    upper = value.astype(jnp.bfloat16)
    return upper, (value - upper.astype(jnp.float32)).astype(jnp.bfloat16)


def own_kernel(blocks, nb_ref, jac_hbm, modes, p_ref, t_ref, jac, turned, jv, parts, face, sems):
    slots, width, _ = jac_hbm.shape
    n_modes = modes.shape[1]

    def load(s):
        return pltpu.make_async_copy(jac_hbm.at[s], jac.at[s], sems.at[s])

    for s in range(slots):
        load(s).start()
    face[...] = jnp.zeros_like(face)
    for s in range(blocks):
        rows = pl.ds(s * width, width)
        load(s).wait()
        jv[rows, :] = dot(jac[s], modes[rows, :])
        turned[:, rows] = modes[rows, :].T
    base = nb_ref[1, 0]
    last = (blocks - 1) * width

    def step(s, carry):
        load(s).wait()
        r = nb_ref[0, s]
        c = nb_ref[1, s] - base
        live = r >= 0

        @pl.when(live & (c >= 0) & (c < blocks))
        def _():
            rows = pl.ds(pl.multiple_of(r * width, width), width)
            picked = pl.ds(pl.multiple_of(c * width, width), width)
            jv[rows, :] += dot(jac[s], modes[picked, :])

        @pl.when(live & (c < 0))
        def _():
            face[0] += dot(turned[:, :width], jac[s])

        @pl.when(live & (c >= blocks))
        def _():
            face[1] += dot(turned[:, last:], jac[s])

        return carry

    lax.fori_loop(blocks, slots, step, 0)
    for side in range(2):
        upper, lower = halves(face[side])
        t_ref[side, 0] = upper
        t_ref[side, 1] = lower
    for s in range(blocks):
        rows = pl.ds(s * width, width)
        upper, lower = halves(jv[rows, :])
        parts[rows, :n_modes] = upper
        parts[rows, n_modes:] = lower
    both = dot(turned[...], parts[...])
    p_ref[...] = both[:, :n_modes] + both[:, n_modes:]


def own_part(neighbours, jac_blocks, modes):
    slots, width, _ = jac_blocks.shape
    rows, n_modes = modes.shape
    blocks = rows // width
    flops = 2 * n_modes * width * width * slots + 4 * rows * n_modes * n_modes
    return pl.pallas_call(
        functools.partial(own_kernel, blocks),
        out_shape=(
            jax.ShapeDtypeStruct((n_modes, n_modes), jnp.float32),
            jax.ShapeDtypeStruct((2, 2, n_modes, width), jnp.bfloat16),
        ),
        in_specs=[
            pl.BlockSpec(memory_space=pltpu.SMEM),
            pl.BlockSpec(memory_space=pl.ANY),
            pl.BlockSpec(memory_space=pltpu.VMEM),
        ],
        out_specs=(pl.BlockSpec(memory_space=pltpu.VMEM), pl.BlockSpec(memory_space=pltpu.VMEM)),
        scratch_shapes=[
            pltpu.VMEM((slots, width, width), jnp.bfloat16),
            pltpu.VMEM((n_modes, rows), jnp.bfloat16),
            pltpu.VMEM((rows, n_modes), jnp.float32),
            pltpu.VMEM((rows, 2 * n_modes), jnp.bfloat16),
            pltpu.VMEM((2, n_modes, width), jnp.float32),
            pltpu.SemaphoreType.DMA((slots,)),
        ],
        compiler_params=pltpu.CompilerParams(vmem_limit_bytes=OWN_VMEM),
        cost_estimate=pl.CostEstimate(
            flops=flops, bytes_accessed=slots * width * width * 2 + rows * n_modes * 2, transcendentals=0
        ),
        name="own_part",
    )(neighbours, jac_blocks, modes)


def join_kernel(p_ref, t_ref, before_ref, after_ref, out_ref):
    total = p_ref[...]
    for side, halo in enumerate((before_ref, after_ref)):
        for part in range(2):
            total += dot(t_ref[side, part], halo[...])
    out_ref[...] = total


def join(p, t, before, after):
    return pl.pallas_call(
        join_kernel,
        out_shape=jax.ShapeDtypeStruct(p.shape, jnp.float32),
        in_specs=[pl.BlockSpec(memory_space=pltpu.VMEM)] * 4,
        out_specs=pl.BlockSpec(memory_space=pltpu.VMEM),
        compiler_params=pltpu.CompilerParams(vmem_limit_bytes=JOIN_VMEM),
        name="join",
    )(p, t, before, after)


def per_device(jac_blocks, modes, neighbours):
    width = jac_blocks.shape[1]
    rows, n_modes = modes.shape
    count = lax.axis_size("cell")
    ends = count - 1
    before = lax.ppermute(modes[rows - width :], "cell", [(i, i + 1) for i in range(ends)])
    after = lax.ppermute(modes[:width], "cell", [(i + 1, i) for i in range(ends)])
    p, t = own_part(neighbours.T, jac_blocks, modes)
    total = join(p, t, before, after)
    parts = lax.all_to_all(total.reshape(count, n_modes // count, n_modes), "cell", 0, 0)
    return jnp.sum(parts, axis=0)


def solution(mesh):
    placed = (P(("grp", "cell"), None, None), P(("grp", "cell"), None), P(("grp", "cell"), None))
    return jax.shard_map(
        per_device, mesh=mesh, in_specs=placed, out_specs=P(("grp", "cell"), None), check_vma=False
    )
```

```python
import functools

import jax
import jax.numpy as jnp
from jax import lax
from jax.experimental import pallas as pl
from jax.experimental.pallas import tpu as pltpu
from jax.sharding import PartitionSpec as P

OWN_VMEM = 48 * 2**20
JOIN_VMEM = 8 * 2**20


def dot(a, b):
    return jnp.dot(a, b, preferred_element_type=jnp.float32)


def halves(value):
    upper = value.astype(jnp.bfloat16)
    return upper, (value - upper.astype(jnp.float32)).astype(jnp.bfloat16)


def own_kernel(blocks, nb_ref, jac_hbm, modes, p_ref, t_ref, jac, turned, jv, parts, face, sems):
    slots, width, _ = jac_hbm.shape
    n_modes = modes.shape[1]

    def load(s):
        return pltpu.make_async_copy(jac_hbm.at[s], jac.at[s], sems.at[s])

    for s in range(slots):
        load(s).start()
    face[...] = jnp.zeros_like(face)
    for s in range(blocks):
        rows = pl.ds(s * width, width)
        load(s).wait()
        jv[rows, :] = dot(jac[s], modes[rows, :])
        turned[:, rows] = modes[rows, :].T
    base = nb_ref[1, 0]
    last = (blocks - 1) * width

    def step(s, carry):
        load(s).wait()
        r = nb_ref[0, s]
        c = nb_ref[1, s] - base
        live = r >= 0

        @pl.when(live & (c >= 0) & (c < blocks))
        def _():
            rows = pl.ds(pl.multiple_of(r * width, width), width)
            picked = pl.ds(pl.multiple_of(c * width, width), width)
            jv[rows, :] += dot(jac[s], modes[picked, :])

        @pl.when(live & (c < 0))
        def _():
            face[0] += dot(turned[:, :width], jac[s])

        @pl.when(live & (c >= blocks))
        def _():
            face[1] += dot(turned[:, last:], jac[s])

        return carry

    lax.fori_loop(blocks, slots, step, 0)
    for side in range(2):
        upper, lower = halves(face[side])
        t_ref[side, 0] = upper
        t_ref[side, 1] = lower
    for s in range(blocks):
        rows = pl.ds(s * width, width)
        upper, lower = halves(jv[rows, :])
        parts[rows, :n_modes] = upper
        parts[rows, n_modes:] = lower
    both = dot(turned[...], parts[...])
    p_ref[...] = both[:, :n_modes] + both[:, n_modes:]


def own_part(neighbours, jac_blocks, modes):
    slots, width, _ = jac_blocks.shape
    rows, n_modes = modes.shape
    blocks = rows // width
    flops = 2 * n_modes * width * width * slots + 4 * rows * n_modes * n_modes
    return pl.pallas_call(
        functools.partial(own_kernel, blocks),
        out_shape=(
            jax.ShapeDtypeStruct((n_modes, n_modes), jnp.float32),
            jax.ShapeDtypeStruct((2, 2, n_modes, width), jnp.bfloat16),
        ),
        in_specs=[
            pl.BlockSpec(memory_space=pltpu.SMEM),
            pl.BlockSpec(memory_space=pl.ANY),
            pl.BlockSpec(memory_space=pltpu.VMEM),
        ],
        out_specs=(pl.BlockSpec(memory_space=pltpu.VMEM), pl.BlockSpec(memory_space=pltpu.VMEM)),
        scratch_shapes=[
            pltpu.VMEM((slots, width, width), jnp.bfloat16),
            pltpu.VMEM((n_modes, rows), jnp.bfloat16),
            pltpu.VMEM((rows, n_modes), jnp.float32),
            pltpu.VMEM((rows, 2 * n_modes), jnp.bfloat16),
            pltpu.VMEM((2, n_modes, width), jnp.float32),
            pltpu.SemaphoreType.DMA((slots,)),
        ],
        compiler_params=pltpu.CompilerParams(vmem_limit_bytes=OWN_VMEM),
        cost_estimate=pl.CostEstimate(
            flops=flops, bytes_accessed=slots * width * width * 2 + rows * n_modes * 2, transcendentals=0
        ),
        name="own_part",
    )(neighbours, jac_blocks, modes)


def join_kernel(rows, p_ref, t_ref, before_ref, after_ref, keep_ref, give_ref):
    total = p_ref[...]
    for side, halo in enumerate((before_ref, after_ref)):
        for part in range(2):
            total += dot(t_ref[side, part], halo[...])
    first = lax.rem(lax.axis_index("cell"), 2) == 0
    for chip in range(total.shape[0] // (2 * rows)):
        even = total[2 * chip * rows : (2 * chip + 1) * rows]
        odd = total[(2 * chip + 1) * rows : (2 * chip + 2) * rows]
        place = slice(chip * rows, (chip + 1) * rows)
        keep_ref[place, :] = jnp.where(first, even, odd)
        give_ref[place, :] = jnp.where(first, odd, even)


def join(rows, p, t, before, after):
    half = jax.ShapeDtypeStruct((p.shape[0] // 2, p.shape[1]), jnp.float32)
    return pl.pallas_call(
        functools.partial(join_kernel, rows),
        out_shape=(half, half),
        in_specs=[pl.BlockSpec(memory_space=pltpu.VMEM)] * 4,
        out_specs=(pl.BlockSpec(memory_space=pltpu.VMEM),) * 2,
        compiler_params=pltpu.CompilerParams(vmem_limit_bytes=JOIN_VMEM),
        name="join",
    )(p, t, before, after)


def per_device(jac_blocks, modes, neighbours):
    width = jac_blocks.shape[1]
    rows, n_modes = modes.shape
    count = lax.axis_size("cell")
    ends = count - 1
    before = lax.ppermute(modes[rows - width :], "cell", [(i, i + 1) for i in range(ends)])
    after = lax.ppermute(modes[:width], "cell", [(i + 1, i) for i in range(ends)])
    p, t = own_part(neighbours.T, jac_blocks, modes)
    keep, give = join(n_modes // count, p, t, before, after)
    got = lax.ppermute(give, "cell", [(i, i ^ 1) for i in range(count)])
    pair = (keep + got).reshape(count // 2, n_modes // count, n_modes)
    same_core = [list(range(core, count, 2)) for core in range(2)]
    parts = lax.all_to_all(pair, "cell", 0, 0, axis_index_groups=same_core)
    return jnp.sum(parts, axis=0)


def solution(mesh):
    placed = (P(("grp", "cell"), None, None), P(("grp", "cell"), None), P(("grp", "cell"), None))
    return jax.shard_map(
        per_device, mesh=mesh, in_specs=placed, out_specs=P(("grp", "cell"), None), check_vma=False
    )
```

```python
import functools

import jax
import jax.numpy as jnp
from jax import lax
from jax.experimental import pallas as pl
from jax.experimental.pallas import tpu as pltpu
from jax.sharding import PartitionSpec as P

OWN_VMEM = 48 * 2**20
JOIN_VMEM = 8 * 2**20


def dot(a, b):
    return jnp.dot(a, b, preferred_element_type=jnp.float32)


def halves(value):
    upper = value.astype(jnp.bfloat16)
    return upper, (value - upper.astype(jnp.float32)).astype(jnp.bfloat16)


def own_kernel(blocks, nb_ref, jac_hbm, modes, p_ref, t_ref, jac, turned, jv, parts, face, sems):
    slots, width, _ = jac_hbm.shape
    n_modes = modes.shape[1]

    def load(s):
        return pltpu.make_async_copy(jac_hbm.at[s], jac.at[s], sems.at[s])

    for s in range(slots):
        load(s).start()
    face[...] = jnp.zeros_like(face)
    for s in range(blocks):
        rows = pl.ds(s * width, width)
        load(s).wait()
        jv[rows, :] = dot(jac[s], modes[rows, :])
        turned[:, rows] = modes[rows, :].T
    base = nb_ref[1, 0]
    last = (blocks - 1) * width

    def step(s, carry):
        load(s).wait()
        r = nb_ref[0, s]
        c = nb_ref[1, s] - base
        live = r >= 0

        @pl.when(live & (c >= 0) & (c < blocks))
        def _():
            rows = pl.ds(pl.multiple_of(r * width, width), width)
            picked = pl.ds(pl.multiple_of(c * width, width), width)
            jv[rows, :] += dot(jac[s], modes[picked, :])

        @pl.when(live & (c < 0))
        def _():
            face[0] += dot(turned[:, :width], jac[s])

        @pl.when(live & (c >= blocks))
        def _():
            face[1] += dot(turned[:, last:], jac[s])

        return carry

    lax.fori_loop(blocks, slots, step, 0)
    for side in range(2):
        upper, lower = halves(face[side])
        t_ref[side, 0] = upper
        t_ref[side, 1] = lower
    for s in range(blocks):
        rows = pl.ds(s * width, width)
        upper, lower = halves(jv[rows, :])
        parts[rows, :n_modes] = upper
        parts[rows, n_modes:] = lower
    both = dot(turned[...], parts[...])
    p_ref[...] = both[:, :n_modes] + both[:, n_modes:]


def own_part(neighbours, jac_blocks, modes):
    slots, width, _ = jac_blocks.shape
    rows, n_modes = modes.shape
    blocks = rows // width
    flops = 2 * n_modes * width * width * slots + 4 * rows * n_modes * n_modes
    return pl.pallas_call(
        functools.partial(own_kernel, blocks),
        out_shape=(
            jax.ShapeDtypeStruct((n_modes, n_modes), jnp.float32),
            jax.ShapeDtypeStruct((2, 2, n_modes, width), jnp.bfloat16),
        ),
        in_specs=[
            pl.BlockSpec(memory_space=pltpu.SMEM),
            pl.BlockSpec(memory_space=pl.ANY),
            pl.BlockSpec(memory_space=pltpu.VMEM),
        ],
        out_specs=(pl.BlockSpec(memory_space=pltpu.VMEM), pl.BlockSpec(memory_space=pltpu.VMEM)),
        scratch_shapes=[
            pltpu.VMEM((slots, width, width), jnp.bfloat16),
            pltpu.VMEM((n_modes, rows), jnp.bfloat16),
            pltpu.VMEM((rows, n_modes), jnp.float32),
            pltpu.VMEM((rows, 2 * n_modes), jnp.bfloat16),
            pltpu.VMEM((2, n_modes, width), jnp.float32),
            pltpu.SemaphoreType.DMA((slots,)),
        ],
        compiler_params=pltpu.CompilerParams(vmem_limit_bytes=OWN_VMEM),
        cost_estimate=pl.CostEstimate(
            flops=flops, bytes_accessed=slots * width * width * 2 + rows * n_modes * 2, transcendentals=0
        ),
        name="own_part",
    )(neighbours, jac_blocks, modes)


def join_kernel(rows, p_ref, t_ref, inner_ref, outer_ref, keep_ref, give_ref):
    total = p_ref[...]
    core = lax.rem(lax.axis_index("cell"), 2)
    for side, halo in ((1 - core, inner_ref), (core, outer_ref)):
        for part in range(2):
            total += dot(t_ref[side, part], halo[...])
    first = core == 0
    for chip in range(total.shape[0] // (2 * rows)):
        even = total[2 * chip * rows : (2 * chip + 1) * rows]
        odd = total[(2 * chip + 1) * rows : (2 * chip + 2) * rows]
        place = slice(chip * rows, (chip + 1) * rows)
        keep_ref[place, :] = jnp.where(first, even, odd)
        give_ref[place, :] = jnp.where(first, odd, even)


def join(rows, p, t, inner, outer):
    half = jax.ShapeDtypeStruct((p.shape[0] // 2, p.shape[1]), jnp.float32)
    return pl.pallas_call(
        functools.partial(join_kernel, rows),
        out_shape=(half, half),
        in_specs=[pl.BlockSpec(memory_space=pltpu.VMEM)] * 4,
        out_specs=(pl.BlockSpec(memory_space=pltpu.VMEM),) * 2,
        compiler_params=pltpu.CompilerParams(vmem_limit_bytes=JOIN_VMEM),
        name="join",
    )(p, t, inner, outer)


def per_device(jac_blocks, modes, neighbours):
    width = jac_blocks.shape[1]
    rows, n_modes = modes.shape
    count = lax.axis_size("cell")
    core = lax.rem(lax.axis_index("cell"), 2)
    edge = rows - width
    across = [(i, min(max(i - 1 + 2 * (i % 2), 0), count - 1)) for i in range(count)]
    outer = lax.ppermute(lax.dynamic_slice_in_dim(modes, core * edge, width), "cell", across)
    inner = lax.ppermute(
        lax.dynamic_slice_in_dim(modes, (1 - core) * edge, width), "cell", [(i, i ^ 1) for i in range(count)]
    )
    p, t = own_part(neighbours.T, jac_blocks, modes)
    keep, give = join(n_modes // count, p, t, inner, outer)
    got = lax.ppermute(give, "cell", [(i, i ^ 1) for i in range(count)])
    pair = (keep + got).reshape(count // 2, n_modes // count, n_modes)
    same_core = [list(range(core, count, 2)) for core in range(2)]
    parts = lax.all_to_all(pair, "cell", 0, 0, axis_index_groups=same_core)
    return jnp.sum(parts, axis=0)


def solution(mesh):
    placed = (P(("grp", "cell"), None, None), P(("grp", "cell"), None), P(("grp", "cell"), None))
    return jax.shard_map(
        per_device, mesh=mesh, in_specs=placed, out_specs=P(("grp", "cell"), None), check_vma=False
    )
```

```python
import functools

import jax
import jax.numpy as jnp
from jax import lax
from jax.experimental import pallas as pl
from jax.experimental.pallas import tpu as pltpu
from jax.sharding import PartitionSpec as P

OWN_VMEM = 24 * 2**20
JOIN_VMEM = 8 * 2**20
STAGE_COST = 10**10


def dot(a, b):
    return jnp.dot(a, b, preferred_element_type=jnp.float32)


def halves(value):
    upper = value.astype(jnp.bfloat16)
    return upper, (value - upper.astype(jnp.float32)).astype(jnp.bfloat16)


def stage_kernel(modes, outer_ref, inner_ref):
    width = outer_ref.shape[0]
    head = modes[:width, :]
    tail = modes[modes.shape[0] - width :, :]
    first = lax.rem(lax.axis_index("cell"), 2) == 0
    outer_ref[...] = jnp.where(first, head, tail)
    inner_ref[...] = jnp.where(first, tail, head)


def stage(modes, width):
    edge = jax.ShapeDtypeStruct((width, modes.shape[1]), modes.dtype)
    return pl.pallas_call(
        stage_kernel,
        out_shape=(edge, edge),
        in_specs=[pl.BlockSpec(memory_space=pltpu.VMEM)],
        out_specs=(pl.BlockSpec(memory_space=pltpu.VMEM),) * 2,
        compiler_params=pltpu.CompilerParams(vmem_limit_bytes=JOIN_VMEM),
        cost_estimate=pl.CostEstimate(flops=STAGE_COST, bytes_accessed=4 * edge.size * 2, transcendentals=0),
        name="stage",
    )(modes)


def own_kernel(blocks, nb_ref, jac, modes, p_ref, t_ref, turned, jv, parts, face):
    slots, width, _ = jac.shape
    n_modes = modes.shape[1]

    face[...] = jnp.zeros_like(face)
    for s in range(blocks):
        rows = pl.ds(s * width, width)
        jv[rows, :] = dot(jac[s], modes[rows, :])
        turned[:, rows] = modes[rows, :].T
    base = nb_ref[1, 0]
    last = (blocks - 1) * width

    def step(s, carry):
        r = nb_ref[0, s]
        c = nb_ref[1, s] - base
        live = r >= 0

        @pl.when(live & (c >= 0) & (c < blocks))
        def _():
            rows = pl.ds(pl.multiple_of(r * width, width), width)
            picked = pl.ds(pl.multiple_of(c * width, width), width)
            jv[rows, :] += dot(jac[s], modes[picked, :])

        @pl.when(live & (c < 0))
        def _():
            face[0] += dot(turned[:, :width], jac[s])

        @pl.when(live & (c >= blocks))
        def _():
            face[1] += dot(turned[:, last:], jac[s])

        return carry

    lax.fori_loop(blocks, slots, step, 0)
    for side in range(2):
        upper, lower = halves(face[side])
        t_ref[side, 0] = upper
        t_ref[side, 1] = lower
    for s in range(blocks):
        rows = pl.ds(s * width, width)
        upper, lower = halves(jv[rows, :])
        parts[rows, :n_modes] = upper
        parts[rows, n_modes:] = lower
    both = dot(turned[...], parts[...])
    p_ref[...] = both[:, :n_modes] + both[:, n_modes:]


def own_part(neighbours, jac_blocks, modes):
    slots, width, _ = jac_blocks.shape
    rows, n_modes = modes.shape
    blocks = rows // width
    flops = 2 * n_modes * width * width * slots + 4 * rows * n_modes * n_modes
    return pl.pallas_call(
        functools.partial(own_kernel, blocks),
        out_shape=(
            jax.ShapeDtypeStruct((n_modes, n_modes), jnp.float32),
            jax.ShapeDtypeStruct((2, 2, n_modes, width), jnp.bfloat16),
        ),
        in_specs=[
            pl.BlockSpec(memory_space=pltpu.SMEM),
            pl.BlockSpec(memory_space=pltpu.VMEM),
            pl.BlockSpec(memory_space=pltpu.VMEM),
        ],
        out_specs=(pl.BlockSpec(memory_space=pltpu.VMEM), pl.BlockSpec(memory_space=pltpu.VMEM)),
        scratch_shapes=[
            pltpu.VMEM((n_modes, rows), jnp.bfloat16),
            pltpu.VMEM((rows, n_modes), jnp.float32),
            pltpu.VMEM((rows, 2 * n_modes), jnp.bfloat16),
            pltpu.VMEM((2, n_modes, width), jnp.float32),
        ],
        compiler_params=pltpu.CompilerParams(vmem_limit_bytes=OWN_VMEM),
        cost_estimate=pl.CostEstimate(
            flops=flops, bytes_accessed=slots * width * width * 2 + rows * n_modes * 2, transcendentals=0
        ),
        name="own_part",
    )(neighbours, jac_blocks, modes)


def join_kernel(rows, p_ref, t_ref, inner_ref, outer_ref, keep_ref, give_ref):
    total = p_ref[...]
    core = lax.rem(lax.axis_index("cell"), 2)
    for side, halo in ((1 - core, inner_ref), (core, outer_ref)):
        for part in range(2):
            total += dot(t_ref[side, part], halo[...])
    first = core == 0
    for chip in range(total.shape[0] // (2 * rows)):
        even = total[2 * chip * rows : (2 * chip + 1) * rows]
        odd = total[(2 * chip + 1) * rows : (2 * chip + 2) * rows]
        place = slice(chip * rows, (chip + 1) * rows)
        keep_ref[place, :] = jnp.where(first, even, odd)
        give_ref[place, :] = jnp.where(first, odd, even)


def join(rows, p, t, inner, outer):
    half = jax.ShapeDtypeStruct((p.shape[0] // 2, p.shape[1]), jnp.float32)
    return pl.pallas_call(
        functools.partial(join_kernel, rows),
        out_shape=(half, half),
        in_specs=[pl.BlockSpec(memory_space=pltpu.VMEM)] * 4,
        out_specs=(pl.BlockSpec(memory_space=pltpu.VMEM),) * 2,
        compiler_params=pltpu.CompilerParams(vmem_limit_bytes=JOIN_VMEM),
        name="join",
    )(p, t, inner, outer)


def per_device(jac_blocks, modes, neighbours):
    width = jac_blocks.shape[1]
    rows, n_modes = modes.shape
    count = lax.axis_size("cell")
    across = [(i, min(max(i - 1 + 2 * (i % 2), 0), count - 1)) for i in range(count)]
    outer, inner = stage(modes, width)
    outer = lax.ppermute(outer, "cell", across)
    inner = lax.ppermute(inner, "cell", [(i, i ^ 1) for i in range(count)])
    p, t = own_part(neighbours.T, jac_blocks, modes)
    keep, give = join(n_modes // count, p, t, inner, outer)
    got = lax.ppermute(give, "cell", [(i, i ^ 1) for i in range(count)])
    pair = (keep + got).reshape(count // 2, n_modes // count, n_modes)
    same_core = [list(range(core, count, 2)) for core in range(2)]
    parts = lax.all_to_all(pair, "cell", 0, 0, axis_index_groups=same_core)
    return jnp.sum(parts, axis=0)


def solution(mesh):
    placed = (P(("grp", "cell"), None, None), P(("grp", "cell"), None), P(("grp", "cell"), None))
    return jax.shard_map(
        per_device, mesh=mesh, in_specs=placed, out_specs=P(("grp", "cell"), None), check_vma=False
    )
```

```python
import functools

import jax
import jax.numpy as jnp
from jax import lax
from jax.experimental import pallas as pl
from jax.experimental.pallas import tpu as pltpu
from jax.sharding import PartitionSpec as P

OWN_VMEM = 24 * 2**20
JOIN_VMEM = 8 * 2**20
EDGES_COST = 10**10


def dot(a, b):
    return jnp.dot(a, b, preferred_element_type=jnp.float32)


def halves(value):
    upper = value.astype(jnp.bfloat16)
    return upper, (value - upper.astype(jnp.float32)).astype(jnp.bfloat16)


def edges_kernel(modes_hbm, outer_ref, inner_ref, sems):
    width = outer_ref.shape[0]
    last = modes_hbm.shape[0] - width
    core = lax.rem(lax.axis_index("cell"), 2)
    copies = []
    for k, (side, out_ref) in enumerate(((core, outer_ref), (1 - core, inner_ref))):
        rows = pl.ds(pl.multiple_of(side * last, 128), width)
        copies.append(pltpu.make_async_copy(modes_hbm.at[rows, :], out_ref, sems.at[k]))
    for copy in copies:
        copy.start()
    for copy in copies:
        copy.wait()


def edges(modes, width):
    edge = jax.ShapeDtypeStruct((width, modes.shape[1]), modes.dtype)
    return pl.pallas_call(
        edges_kernel,
        out_shape=(edge, edge),
        in_specs=[pl.BlockSpec(memory_space=pltpu.HBM)],
        out_specs=(pl.BlockSpec(memory_space=pltpu.VMEM),) * 2,
        scratch_shapes=[pltpu.SemaphoreType.DMA((2,))],
        compiler_params=pltpu.CompilerParams(vmem_limit_bytes=JOIN_VMEM),
        cost_estimate=pl.CostEstimate(flops=EDGES_COST, bytes_accessed=4 * edge.size * 2, transcendentals=0),
        name="edges",
    )(pltpu.with_memory_space_constraint(modes, pltpu.HBM))


def own_kernel(blocks, nb_ref, jac, modes, p_ref, t_ref, turned, jv, parts, face):
    slots, width, _ = jac.shape
    n_modes = modes.shape[1]

    face[...] = jnp.zeros_like(face)
    for s in range(blocks):
        rows = pl.ds(s * width, width)
        jv[rows, :] = dot(jac[s], modes[rows, :])
        turned[:, rows] = modes[rows, :].T
    base = nb_ref[1, 0]
    last = (blocks - 1) * width

    def step(s, carry):
        r = nb_ref[0, s]
        c = nb_ref[1, s] - base
        live = r >= 0

        @pl.when(live & (c >= 0) & (c < blocks))
        def _():
            rows = pl.ds(pl.multiple_of(r * width, width), width)
            picked = pl.ds(pl.multiple_of(c * width, width), width)
            jv[rows, :] += dot(jac[s], modes[picked, :])

        @pl.when(live & (c < 0))
        def _():
            face[0] += dot(turned[:, :width], jac[s])

        @pl.when(live & (c >= blocks))
        def _():
            face[1] += dot(turned[:, last:], jac[s])

        return carry

    lax.fori_loop(blocks, slots, step, 0)
    for side in range(2):
        upper, lower = halves(face[side])
        t_ref[side, 0] = upper
        t_ref[side, 1] = lower
    for s in range(blocks):
        rows = pl.ds(s * width, width)
        upper, lower = halves(jv[rows, :])
        parts[rows, :n_modes] = upper
        parts[rows, n_modes:] = lower
    both = dot(turned[...], parts[...])
    p_ref[...] = both[:, :n_modes] + both[:, n_modes:]


def own_part(neighbours, jac_blocks, modes):
    slots, width, _ = jac_blocks.shape
    rows, n_modes = modes.shape
    blocks = rows // width
    flops = 2 * n_modes * width * width * slots + 4 * rows * n_modes * n_modes
    return pl.pallas_call(
        functools.partial(own_kernel, blocks),
        out_shape=(
            jax.ShapeDtypeStruct((n_modes, n_modes), jnp.float32),
            jax.ShapeDtypeStruct((2, 2, n_modes, width), jnp.bfloat16),
        ),
        in_specs=[
            pl.BlockSpec(memory_space=pltpu.SMEM),
            pl.BlockSpec(memory_space=pltpu.VMEM),
            pl.BlockSpec(memory_space=pltpu.VMEM),
        ],
        out_specs=(pl.BlockSpec(memory_space=pltpu.VMEM), pl.BlockSpec(memory_space=pltpu.VMEM)),
        scratch_shapes=[
            pltpu.VMEM((n_modes, rows), jnp.bfloat16),
            pltpu.VMEM((rows, n_modes), jnp.float32),
            pltpu.VMEM((rows, 2 * n_modes), jnp.bfloat16),
            pltpu.VMEM((2, n_modes, width), jnp.float32),
        ],
        compiler_params=pltpu.CompilerParams(vmem_limit_bytes=OWN_VMEM),
        cost_estimate=pl.CostEstimate(
            flops=flops, bytes_accessed=slots * width * width * 2 + rows * n_modes * 2, transcendentals=0
        ),
        name="own_part",
    )(neighbours, jac_blocks, modes)


def join_kernel(rows, p_ref, t_ref, inner_ref, outer_ref, keep_ref, give_ref):
    total = p_ref[...]
    core = lax.rem(lax.axis_index("cell"), 2)
    for side, halo in ((1 - core, inner_ref), (core, outer_ref)):
        for part in range(2):
            total += dot(t_ref[side, part], halo[...])
    first = core == 0
    for chip in range(total.shape[0] // (2 * rows)):
        even = total[2 * chip * rows : (2 * chip + 1) * rows]
        odd = total[(2 * chip + 1) * rows : (2 * chip + 2) * rows]
        place = slice(chip * rows, (chip + 1) * rows)
        keep_ref[place, :] = jnp.where(first, even, odd)
        give_ref[place, :] = jnp.where(first, odd, even)


def join(rows, p, t, inner, outer):
    half = jax.ShapeDtypeStruct((p.shape[0] // 2, p.shape[1]), jnp.float32)
    return pl.pallas_call(
        functools.partial(join_kernel, rows),
        out_shape=(half, half),
        in_specs=[pl.BlockSpec(memory_space=pltpu.VMEM)] * 4,
        out_specs=(pl.BlockSpec(memory_space=pltpu.VMEM),) * 2,
        compiler_params=pltpu.CompilerParams(vmem_limit_bytes=JOIN_VMEM),
        name="join",
    )(p, t, inner, outer)


def per_device(jac_blocks, modes, neighbours):
    width = jac_blocks.shape[1]
    rows, n_modes = modes.shape
    count = lax.axis_size("cell")
    across = [(i, min(max(i - 1 + 2 * (i % 2), 0), count - 1)) for i in range(count)]
    outer, inner = edges(modes, width)
    outer = lax.ppermute(outer, "cell", across)
    inner = lax.ppermute(inner, "cell", [(i, i ^ 1) for i in range(count)])
    p, t = own_part(neighbours.T, jac_blocks, modes)
    keep, give = join(n_modes // count, p, t, inner, outer)
    got = lax.ppermute(give, "cell", [(i, i ^ 1) for i in range(count)])
    pair = (keep + got).reshape(count // 2, n_modes // count, n_modes)
    same_core = [list(range(core, count, 2)) for core in range(2)]
    parts = lax.all_to_all(pair, "cell", 0, 0, axis_index_groups=same_core)
    return jnp.sum(parts, axis=0)


def solution(mesh):
    placed = (P(("grp", "cell"), None, None), P(("grp", "cell"), None), P(("grp", "cell"), None))
    return jax.shard_map(
        per_device, mesh=mesh, in_specs=placed, out_specs=P(("grp", "cell"), None), check_vma=False
    )
```

```python
import functools

import jax
import jax.numpy as jnp
from jax import lax
from jax.experimental import pallas as pl
from jax.experimental.pallas import tpu as pltpu
from jax.sharding import PartitionSpec as P

OWN_VMEM = 24 * 2**20
SMALL_VMEM = 8 * 2**20
LOAD_COST = 5 * 10**9


def dot(a, b):
    return jnp.dot(a, b, preferred_element_type=jnp.float32)


def halves(value):
    upper = value.astype(jnp.bfloat16)
    return upper, (value - upper.astype(jnp.float32)).astype(jnp.bfloat16)


def edges_kernel(modes_hbm, outer_ref, inner_ref, sems):
    width = outer_ref.shape[0]
    last = modes_hbm.shape[0] - width
    core = lax.rem(lax.axis_index("cell"), 2)
    copies = []
    for k, (side, out_ref) in enumerate(((core, outer_ref), (1 - core, inner_ref))):
        rows = pl.ds(pl.multiple_of(side * last, 128), width)
        copies.append(pltpu.make_async_copy(modes_hbm.at[rows, :], out_ref, sems.at[k]))
    for copy in copies:
        copy.start()
    for copy in copies:
        copy.wait()


def edges(modes, width):
    edge = jax.ShapeDtypeStruct((width, modes.shape[1]), modes.dtype)
    return pl.pallas_call(
        edges_kernel,
        out_shape=(edge, edge),
        in_specs=[pl.BlockSpec(memory_space=pltpu.HBM)],
        out_specs=(pl.BlockSpec(memory_space=pltpu.VMEM),) * 2,
        scratch_shapes=[pltpu.SemaphoreType.DMA((2,))],
        compiler_params=pltpu.CompilerParams(vmem_limit_bytes=SMALL_VMEM),
        cost_estimate=pl.CostEstimate(flops=0, bytes_accessed=4 * edge.size * 2, transcendentals=0),
        name="edges",
    )(pltpu.with_memory_space_constraint(modes, pltpu.HBM))


def gate(outer, inner):
    edge = jax.ShapeDtypeStruct(outer.shape, outer.dtype)
    return pl.pallas_call(
        lambda *refs: None,
        out_shape=(edge, edge),
        in_specs=[pl.BlockSpec(memory_space=pltpu.VMEM)] * 2,
        out_specs=(pl.BlockSpec(memory_space=pltpu.VMEM),) * 2,
        input_output_aliases={0: 0, 1: 1},
        compiler_params=pltpu.CompilerParams(vmem_limit_bytes=SMALL_VMEM),
        cost_estimate=pl.CostEstimate(flops=LOAD_COST, bytes_accessed=0, transcendentals=0),
        name="gate",
    )(outer, inner)


def own_kernel(blocks, nb_ref, jac, modes, p_ref, t_ref, turned, jv, parts, face):
    slots, width, _ = jac.shape
    n_modes = modes.shape[1]

    face[...] = jnp.zeros_like(face)
    for s in range(blocks):
        rows = pl.ds(s * width, width)
        jv[rows, :] = dot(jac[s], modes[rows, :])
        turned[:, rows] = modes[rows, :].T
    base = nb_ref[1, 0]
    last = (blocks - 1) * width

    def step(s, carry):
        r = nb_ref[0, s]
        c = nb_ref[1, s] - base
        live = r >= 0

        @pl.when(live & (c >= 0) & (c < blocks))
        def _():
            rows = pl.ds(pl.multiple_of(r * width, width), width)
            picked = pl.ds(pl.multiple_of(c * width, width), width)
            jv[rows, :] += dot(jac[s], modes[picked, :])

        @pl.when(live & (c < 0))
        def _():
            face[0] += dot(turned[:, :width], jac[s])

        @pl.when(live & (c >= blocks))
        def _():
            face[1] += dot(turned[:, last:], jac[s])

        return carry

    lax.fori_loop(blocks, slots, step, 0)
    for side in range(2):
        upper, lower = halves(face[side])
        t_ref[side, 0] = upper
        t_ref[side, 1] = lower
    for s in range(blocks):
        rows = pl.ds(s * width, width)
        upper, lower = halves(jv[rows, :])
        parts[rows, :n_modes] = upper
        parts[rows, n_modes:] = lower
    both = dot(turned[...], parts[...])
    p_ref[...] = both[:, :n_modes] + both[:, n_modes:]


def own_part(neighbours, jac_blocks, modes):
    slots, width, _ = jac_blocks.shape
    rows, n_modes = modes.shape
    blocks = rows // width
    flops = 2 * n_modes * width * width * slots + 4 * rows * n_modes * n_modes
    return pl.pallas_call(
        functools.partial(own_kernel, blocks),
        out_shape=(
            jax.ShapeDtypeStruct((n_modes, n_modes), jnp.float32),
            jax.ShapeDtypeStruct((2, 2, n_modes, width), jnp.bfloat16),
        ),
        in_specs=[
            pl.BlockSpec(memory_space=pltpu.SMEM),
            pl.BlockSpec(memory_space=pltpu.VMEM),
            pl.BlockSpec(memory_space=pltpu.VMEM),
        ],
        out_specs=(pl.BlockSpec(memory_space=pltpu.VMEM), pl.BlockSpec(memory_space=pltpu.VMEM)),
        scratch_shapes=[
            pltpu.VMEM((n_modes, rows), jnp.bfloat16),
            pltpu.VMEM((rows, n_modes), jnp.float32),
            pltpu.VMEM((rows, 2 * n_modes), jnp.bfloat16),
            pltpu.VMEM((2, n_modes, width), jnp.float32),
        ],
        compiler_params=pltpu.CompilerParams(vmem_limit_bytes=OWN_VMEM),
        cost_estimate=pl.CostEstimate(
            flops=flops, bytes_accessed=slots * width * width * 2 + rows * n_modes * 2, transcendentals=0
        ),
        name="own_part",
    )(neighbours, pltpu.with_memory_space_constraint(jac_blocks, pltpu.VMEM), modes)


def join_kernel(rows, p_ref, t_ref, inner_ref, outer_ref, keep_ref, give_ref):
    total = p_ref[...]
    core = lax.rem(lax.axis_index("cell"), 2)
    for side, halo in ((1 - core, inner_ref), (core, outer_ref)):
        for part in range(2):
            total += dot(t_ref[side, part], halo[...])
    first = core == 0
    for chip in range(total.shape[0] // (2 * rows)):
        even = total[2 * chip * rows : (2 * chip + 1) * rows]
        odd = total[(2 * chip + 1) * rows : (2 * chip + 2) * rows]
        place = slice(chip * rows, (chip + 1) * rows)
        keep_ref[place, :] = jnp.where(first, even, odd)
        give_ref[place, :] = jnp.where(first, odd, even)


def join(rows, p, t, inner, outer):
    half = jax.ShapeDtypeStruct((p.shape[0] // 2, p.shape[1]), jnp.float32)
    return pl.pallas_call(
        functools.partial(join_kernel, rows),
        out_shape=(half, half),
        in_specs=[pl.BlockSpec(memory_space=pltpu.VMEM)] * 4,
        out_specs=(pl.BlockSpec(memory_space=pltpu.VMEM),) * 2,
        compiler_params=pltpu.CompilerParams(vmem_limit_bytes=SMALL_VMEM),
        name="join",
    )(p, t, inner, outer)


def per_device(jac_blocks, modes, neighbours):
    width = jac_blocks.shape[1]
    rows, n_modes = modes.shape
    count = lax.axis_size("cell")
    across = [(i, min(max(i - 1 + 2 * (i % 2), 0), count - 1)) for i in range(count)]
    outer, inner = gate(*edges(modes, width))
    outer = lax.ppermute(outer, "cell", across)
    inner = lax.ppermute(inner, "cell", [(i, i ^ 1) for i in range(count)])
    p, t = own_part(neighbours.T, jac_blocks, modes)
    keep, give = join(n_modes // count, p, t, inner, outer)
    got = lax.ppermute(give, "cell", [(i, i ^ 1) for i in range(count)])
    pair = (keep + got).reshape(count // 2, n_modes // count, n_modes)
    same_core = [list(range(core, count, 2)) for core in range(2)]
    parts = lax.all_to_all(pair, "cell", 0, 0, axis_index_groups=same_core)
    return jnp.sum(parts, axis=0)


def solution(mesh):
    placed = (P(("grp", "cell"), None, None), P(("grp", "cell"), None), P(("grp", "cell"), None))
    return jax.shard_map(
        per_device, mesh=mesh, in_specs=placed, out_specs=P(("grp", "cell"), None), check_vma=False
    )
```

```python
import functools

import jax
import jax.numpy as jnp
from jax import lax
from jax.experimental import pallas as pl
from jax.experimental.pallas import tpu as pltpu
from jax.sharding import PartitionSpec as P

OWN_VMEM = 24 * 2**20
JOIN_VMEM = 8 * 2**20
TILE_ROWS = 16
EDGES_COST = 10**10


def dot(a, b):
    return jnp.dot(a, b, preferred_element_type=jnp.float32)


def halves(value):
    upper = value.astype(jnp.bfloat16)
    return upper, (value - upper.astype(jnp.float32)).astype(jnp.bfloat16)


def edges_kernel(modes_hbm, outer_ref, inner_ref, sems):
    width = outer_ref.shape[0]
    last = modes_hbm.shape[0] - width
    core = lax.rem(lax.axis_index("cell"), 2)
    copies = []
    for k, (side, out_ref) in enumerate(((core, outer_ref), (1 - core, inner_ref))):
        rows = pl.ds(pl.multiple_of(side * last, 128), width)
        copies.append(pltpu.make_async_copy(modes_hbm.at[rows, :], out_ref, sems.at[k]))
    for copy in copies:
        copy.start()
    for copy in copies:
        copy.wait()


def edges(modes, width):
    edge = jax.ShapeDtypeStruct((width, modes.shape[1]), modes.dtype)
    return pl.pallas_call(
        edges_kernel,
        out_shape=(edge, edge),
        in_specs=[pl.BlockSpec(memory_space=pltpu.HBM)],
        out_specs=(pl.BlockSpec(memory_space=pltpu.VMEM),) * 2,
        scratch_shapes=[pltpu.SemaphoreType.DMA((2,))],
        compiler_params=pltpu.CompilerParams(vmem_limit_bytes=JOIN_VMEM),
        cost_estimate=pl.CostEstimate(flops=EDGES_COST, bytes_accessed=4 * edge.size * 2, transcendentals=0),
        name="edges",
    )(pltpu.with_memory_space_constraint(modes, pltpu.HBM))


def own_kernel(blocks, keep_rows, nb_ref, jac, modes, p_ref, t_ref, turned, jv, parts, face):
    slots, width, _ = jac.shape
    n_modes = modes.shape[1]

    face[...] = jnp.zeros_like(face)
    for s in range(blocks):
        rows = pl.ds(s * width, width)
        jv[rows, :] = dot(jac[s], modes[rows, :])
        block = modes[rows, :].T
        if keep_rows % TILE_ROWS:
            turned[:, rows] = block
        else:
            for k in range(n_modes // keep_rows):
                place = k % 2 * (n_modes // 2) + k // 2 * keep_rows
                turned[place : place + keep_rows, rows] = block[k * keep_rows : (k + 1) * keep_rows]
    base = nb_ref[1, 0]
    last = (blocks - 1) * width

    def step(s, carry):
        r = nb_ref[0, s]
        c = nb_ref[1, s] - base
        live = r >= 0

        @pl.when(live & (c >= 0) & (c < blocks))
        def _():
            rows = pl.ds(pl.multiple_of(r * width, width), width)
            picked = pl.ds(pl.multiple_of(c * width, width), width)
            jv[rows, :] += dot(jac[s], modes[picked, :])

        @pl.when(live & (c < 0))
        def _():
            face[0] += dot(turned[:, :width], jac[s])

        @pl.when(live & (c >= blocks))
        def _():
            face[1] += dot(turned[:, last:], jac[s])

        return carry

    lax.fori_loop(blocks, slots, step, 0)
    for side in range(2):
        upper, lower = halves(face[side])
        t_ref[side, 0] = upper
        t_ref[side, 1] = lower
    for s in range(blocks):
        rows = pl.ds(s * width, width)
        upper, lower = halves(jv[rows, :])
        parts[rows, :n_modes] = upper
        parts[rows, n_modes:] = lower
    both = dot(turned[...], parts[...])
    p_ref[...] = both[:, :n_modes] + both[:, n_modes:]


def own_part(keep_rows, neighbours, jac_blocks, modes):
    slots, width, _ = jac_blocks.shape
    rows, n_modes = modes.shape
    blocks = rows // width
    flops = 2 * n_modes * width * width * slots + 4 * rows * n_modes * n_modes
    return pl.pallas_call(
        functools.partial(own_kernel, blocks, keep_rows),
        out_shape=(
            jax.ShapeDtypeStruct((n_modes, n_modes), jnp.float32),
            jax.ShapeDtypeStruct((2, 2, n_modes, width), jnp.bfloat16),
        ),
        in_specs=[
            pl.BlockSpec(memory_space=pltpu.SMEM),
            pl.BlockSpec(memory_space=pltpu.VMEM),
            pl.BlockSpec(memory_space=pltpu.VMEM),
        ],
        out_specs=(pl.BlockSpec(memory_space=pltpu.VMEM), pl.BlockSpec(memory_space=pltpu.VMEM)),
        scratch_shapes=[
            pltpu.VMEM((n_modes, rows), jnp.bfloat16),
            pltpu.VMEM((rows, n_modes), jnp.float32),
            pltpu.VMEM((rows, 2 * n_modes), jnp.bfloat16),
            pltpu.VMEM((2, n_modes, width), jnp.float32),
        ],
        compiler_params=pltpu.CompilerParams(vmem_limit_bytes=OWN_VMEM),
        cost_estimate=pl.CostEstimate(
            flops=flops, bytes_accessed=slots * width * width * 2 + rows * n_modes * 2, transcendentals=0
        ),
        name="own_part",
    )(neighbours, jac_blocks, modes)


def regrouped(value, axis, keep_rows):
    shape = value.shape
    split = shape[:axis] + (shape[axis] // (2 * keep_rows), 2, keep_rows) + shape[axis + 1 :]
    return jnp.swapaxes(value.reshape(split), axis, axis + 1).reshape(shape)


def join_kernel(other, p_ref, t_ref, outer_ref, inner_ref, out_ref):
    core = lax.rem(lax.axis_index("cell"), 2)
    count = out_ref.shape[0]
    half = 1 - core if other else core
    rows = pl.ds(pl.multiple_of(half * count, TILE_ROWS), count)
    total = p_ref[rows, :]
    for side, halo in ((1 - core, inner_ref), (core, outer_ref)):
        for part in range(2):
            total += dot(t_ref[side, part, rows, :], halo[...])
    out_ref[...] = total


def join(other, p, t, outer, inner):
    rows = p.shape[0] // 2
    return pl.pallas_call(
        functools.partial(join_kernel, other),
        out_shape=jax.ShapeDtypeStruct((rows, p.shape[1]), jnp.float32),
        in_specs=[pl.BlockSpec(memory_space=pltpu.VMEM)] * 4,
        out_specs=pl.BlockSpec(memory_space=pltpu.VMEM),
        compiler_params=pltpu.CompilerParams(vmem_limit_bytes=JOIN_VMEM),
        cost_estimate=pl.CostEstimate(flops=8 * rows * outer.size, bytes_accessed=0, transcendentals=0),
        name="join_give" if other else "join_keep",
    )(p, t, outer, inner)


def per_device(jac_blocks, modes, neighbours):
    width = jac_blocks.shape[1]
    rows, n_modes = modes.shape
    count = lax.axis_size("cell")
    keep_rows = n_modes // count
    across = [(i, min(max(i - 1 + 2 * (i % 2), 0), count - 1)) for i in range(count)]
    swap = [(i, i ^ 1) for i in range(count)]
    outer, inner = edges(modes, width)
    outer = lax.ppermute(outer, "cell", across)
    inner = lax.ppermute(inner, "cell", swap)
    p, t = own_part(keep_rows, neighbours.T, jac_blocks, modes)
    if keep_rows % TILE_ROWS:
        p, t = regrouped(p, 0, keep_rows), regrouped(t, 2, keep_rows)
    got = lax.ppermute(join(True, p, t, outer, inner), "cell", swap)
    keep = join(False, p, t, outer, inner)
    pair = (keep + got).reshape(count // 2, keep_rows, n_modes)
    same_core = [list(range(core, count, 2)) for core in range(2)]
    parts = lax.all_to_all(pair, "cell", 0, 0, axis_index_groups=same_core)
    return jnp.sum(parts, axis=0)


def solution(mesh):
    placed = (P(("grp", "cell"), None, None), P(("grp", "cell"), None), P(("grp", "cell"), None))
    return jax.shard_map(
        per_device, mesh=mesh, in_specs=placed, out_specs=P(("grp", "cell"), None), check_vma=False
    )
```

```python
import functools

import jax
import jax.numpy as jnp
from jax import lax
from jax.experimental import pallas as pl
from jax.experimental.pallas import tpu as pltpu
from jax.sharding import PartitionSpec as P

OWN_VMEM = 24 * 2**20
SMALL_VMEM = 8 * 2**20
TILE_ROWS = 16
LOAD_COST = 5 * 10**9


def dot(a, b):
    return jnp.dot(a, b, preferred_element_type=jnp.float32)


def halves(value):
    upper = value.astype(jnp.bfloat16)
    return upper, (value - upper.astype(jnp.float32)).astype(jnp.bfloat16)


def outer_kernel(modes_hbm, out_ref, sem):
    width = out_ref.shape[0]
    start = lax.rem(lax.axis_index("cell"), 2) * (modes_hbm.shape[0] - width)
    copy = pltpu.make_async_copy(modes_hbm.at[pl.ds(pl.multiple_of(start, 128), width), :], out_ref, sem)
    copy.start()
    copy.wait()


def outer_edge(modes, width):
    return pl.pallas_call(
        outer_kernel,
        out_shape=jax.ShapeDtypeStruct((width, modes.shape[1]), modes.dtype),
        in_specs=[pl.BlockSpec(memory_space=pltpu.HBM)],
        out_specs=pl.BlockSpec(memory_space=pltpu.VMEM),
        scratch_shapes=[pltpu.SemaphoreType.DMA],
        compiler_params=pltpu.CompilerParams(vmem_limit_bytes=SMALL_VMEM),
        cost_estimate=pl.CostEstimate(flops=0, bytes_accessed=4 * width * modes.shape[1], transcendentals=0),
        name="outer_edge",
    )(pltpu.with_memory_space_constraint(modes, pltpu.HBM))


def gate(block):
    return pl.pallas_call(
        lambda block_ref, out_ref: None,
        out_shape=jax.ShapeDtypeStruct(block.shape, block.dtype),
        in_specs=[pl.BlockSpec(memory_space=pltpu.VMEM)],
        out_specs=pl.BlockSpec(memory_space=pltpu.VMEM),
        input_output_aliases={0: 0},
        compiler_params=pltpu.CompilerParams(vmem_limit_bytes=SMALL_VMEM),
        cost_estimate=pl.CostEstimate(flops=LOAD_COST, bytes_accessed=0, transcendentals=0),
        name="gate",
    )(block)


def inner_kernel(modes, out_ref):
    width = out_ref.shape[0]
    head = modes[:width, :]
    tail = modes[modes.shape[0] - width :, :]
    out_ref[...] = jnp.where(lax.rem(lax.axis_index("cell"), 2) == 0, tail, head)


def inner_edge(modes, width):
    return pl.pallas_call(
        inner_kernel,
        out_shape=jax.ShapeDtypeStruct((width, modes.shape[1]), modes.dtype),
        in_specs=[pl.BlockSpec(memory_space=pltpu.VMEM)],
        out_specs=pl.BlockSpec(memory_space=pltpu.VMEM),
        compiler_params=pltpu.CompilerParams(vmem_limit_bytes=SMALL_VMEM),
        name="inner_edge",
    )(modes)


def own_kernel(blocks, keep_rows, nb_ref, jac, modes, p_ref, t_ref, turned, jv, parts, face):
    slots, width, _ = jac.shape
    n_modes = modes.shape[1]

    face[...] = jnp.zeros_like(face)
    for s in range(blocks):
        rows = pl.ds(s * width, width)
        jv[rows, :] = dot(jac[s], modes[rows, :])
        block = modes[rows, :].T
        if keep_rows % TILE_ROWS:
            turned[:, rows] = block
        else:
            for k in range(n_modes // keep_rows):
                place = k % 2 * (n_modes // 2) + k // 2 * keep_rows
                turned[place : place + keep_rows, rows] = block[k * keep_rows : (k + 1) * keep_rows]
    base = nb_ref[1, 0]
    last = (blocks - 1) * width

    def step(s, carry):
        r = nb_ref[0, s]
        c = nb_ref[1, s] - base
        live = r >= 0

        @pl.when(live & (c >= 0) & (c < blocks))
        def _():
            rows = pl.ds(pl.multiple_of(r * width, width), width)
            picked = pl.ds(pl.multiple_of(c * width, width), width)
            jv[rows, :] += dot(jac[s], modes[picked, :])

        @pl.when(live & (c < 0))
        def _():
            face[0] += dot(turned[:, :width], jac[s])

        @pl.when(live & (c >= blocks))
        def _():
            face[1] += dot(turned[:, last:], jac[s])

        return carry

    lax.fori_loop(blocks, slots, step, 0)
    mid = n_modes // 2
    for side in range(2):
        upper, lower = halves(face[side])
        for half in range(2):
            t_ref[side, half, :mid] = upper[half * mid : (half + 1) * mid]
            t_ref[side, half, mid:] = lower[half * mid : (half + 1) * mid]
    for s in range(blocks):
        rows = pl.ds(s * width, width)
        upper, lower = halves(jv[rows, :])
        parts[rows, :n_modes] = upper
        parts[rows, n_modes:] = lower
    both = dot(turned[...], parts[...])
    p_ref[...] = both[:, :n_modes] + both[:, n_modes:]


def own_part(keep_rows, neighbours, jac_blocks, modes):
    slots, width, _ = jac_blocks.shape
    rows, n_modes = modes.shape
    blocks = rows // width
    flops = 2 * n_modes * width * width * slots + 4 * rows * n_modes * n_modes
    return pl.pallas_call(
        functools.partial(own_kernel, blocks, keep_rows),
        out_shape=(
            jax.ShapeDtypeStruct((n_modes, n_modes), jnp.float32),
            jax.ShapeDtypeStruct((2, 2, n_modes, width), jnp.bfloat16),
        ),
        in_specs=[
            pl.BlockSpec(memory_space=pltpu.SMEM),
            pl.BlockSpec(memory_space=pltpu.VMEM),
            pl.BlockSpec(memory_space=pltpu.VMEM),
        ],
        out_specs=(pl.BlockSpec(memory_space=pltpu.VMEM), pl.BlockSpec(memory_space=pltpu.VMEM)),
        scratch_shapes=[
            pltpu.VMEM((n_modes, rows), jnp.bfloat16),
            pltpu.VMEM((rows, n_modes), jnp.float32),
            pltpu.VMEM((rows, 2 * n_modes), jnp.bfloat16),
            pltpu.VMEM((2, n_modes, width), jnp.float32),
        ],
        compiler_params=pltpu.CompilerParams(vmem_limit_bytes=OWN_VMEM),
        cost_estimate=pl.CostEstimate(
            flops=flops, bytes_accessed=slots * width * width * 2 + rows * n_modes * 2, transcendentals=0
        ),
        name="own_part",
    )(neighbours, jac_blocks, modes)


def regrouped(value, axis, keep_rows):
    shape = value.shape
    split = shape[:axis] + (shape[axis] // (2 * keep_rows), 2, keep_rows) + shape[axis + 1 :]
    return jnp.swapaxes(value.reshape(split), axis, axis + 1).reshape(shape)


def join_kernel(other, p_ref, t_ref, outer_ref, inner_ref, out_ref):
    core = lax.rem(lax.axis_index("cell"), 2)
    count = out_ref.shape[0]
    half = 1 - core if other else core
    rows = pl.ds(pl.multiple_of(half * count, TILE_ROWS), count)
    both = dot(t_ref[1 - core, half], inner_ref[...]) + dot(t_ref[core, half], outer_ref[...])
    out_ref[...] = p_ref[rows, :] + both[:count] + both[count:]


def join(other, p, t, outer, inner):
    rows = p.shape[0] // 2
    return pl.pallas_call(
        functools.partial(join_kernel, other),
        out_shape=jax.ShapeDtypeStruct((rows, p.shape[1]), jnp.float32),
        in_specs=[pl.BlockSpec(memory_space=pltpu.VMEM)] * 4,
        out_specs=pl.BlockSpec(memory_space=pltpu.VMEM),
        compiler_params=pltpu.CompilerParams(vmem_limit_bytes=SMALL_VMEM),
        cost_estimate=pl.CostEstimate(flops=8 * rows * outer.size, bytes_accessed=0, transcendentals=0),
        name="join_give" if other else "join_keep",
    )(p, t, outer, inner)


def per_device(jac_blocks, modes, neighbours):
    width = jac_blocks.shape[1]
    rows, n_modes = modes.shape
    count = lax.axis_size("cell")
    keep_rows = n_modes // count
    across = [(i, min(max(i - 1 + 2 * (i % 2), 0), count - 1)) for i in range(count)]
    swap = [(i, i ^ 1) for i in range(count)]
    outer = lax.ppermute(gate(outer_edge(modes, width)), "cell", across)
    inner = lax.ppermute(inner_edge(modes, width), "cell", swap)
    p, t = own_part(keep_rows, neighbours.T, jac_blocks, modes)
    if keep_rows % TILE_ROWS:
        p = regrouped(p, 0, keep_rows)
        apart = jnp.swapaxes(t.reshape(2, 2, 2, n_modes // 2, width), 1, 2).reshape(2, 2, n_modes, width)
        apart = regrouped(apart, 2, keep_rows).reshape(2, 2, 2, n_modes // 2, width)
        t = jnp.swapaxes(apart, 1, 2).reshape(t.shape)
    got = lax.ppermute(join(True, p, t, outer, inner), "cell", swap)
    keep = join(False, p, t, outer, inner)
    pair = (keep + got).reshape(count // 2, keep_rows, n_modes)
    same_core = [list(range(core, count, 2)) for core in range(2)]
    parts = lax.all_to_all(pair, "cell", 0, 0, axis_index_groups=same_core)
    return jnp.sum(parts, axis=0)


def solution(mesh):
    placed = (P(("grp", "cell"), None, None), P(("grp", "cell"), None), P(("grp", "cell"), None))
    return jax.shard_map(
        per_device, mesh=mesh, in_specs=placed, out_specs=P(("grp", "cell"), None), check_vma=False
    )
```

```python
import functools

import jax
import jax.numpy as jnp
from jax import lax
from jax.experimental import pallas as pl
from jax.experimental.pallas import tpu as pltpu
from jax.sharding import PartitionSpec as P

OWN_VMEM = 24 * 2**20
SMALL_VMEM = 8 * 2**20
TILE_ROWS = 16
LOAD_COST = 35 * 10**8


def dot(a, b):
    return jnp.dot(a, b, preferred_element_type=jnp.float32)


def halves(value):
    upper = value.astype(jnp.bfloat16)
    return upper, (value - upper.astype(jnp.float32)).astype(jnp.bfloat16)


def outer_kernel(modes_hbm, out_ref, sem):
    width = out_ref.shape[0]
    start = lax.rem(lax.axis_index("cell"), 2) * (modes_hbm.shape[0] - width)
    copy = pltpu.make_async_copy(modes_hbm.at[pl.ds(pl.multiple_of(start, 128), width), :], out_ref, sem)
    copy.start()
    copy.wait()


def outer_edge(modes, width):
    return pl.pallas_call(
        outer_kernel,
        out_shape=jax.ShapeDtypeStruct((width, modes.shape[1]), modes.dtype),
        in_specs=[pl.BlockSpec(memory_space=pltpu.HBM)],
        out_specs=pl.BlockSpec(memory_space=pltpu.VMEM),
        scratch_shapes=[pltpu.SemaphoreType.DMA],
        compiler_params=pltpu.CompilerParams(vmem_limit_bytes=SMALL_VMEM),
        cost_estimate=pl.CostEstimate(flops=0, bytes_accessed=4 * width * modes.shape[1], transcendentals=0),
        name="outer_edge",
    )(pltpu.with_memory_space_constraint(modes, pltpu.HBM))


def gate_kernel(block_ref, out_ref):
    out_ref[...] = block_ref[...]


def gate(block):
    return pl.pallas_call(
        gate_kernel,
        out_shape=jax.ShapeDtypeStruct(block.shape, block.dtype),
        in_specs=[pl.BlockSpec(memory_space=pltpu.VMEM)],
        out_specs=pl.BlockSpec(memory_space=pltpu.VMEM),
        compiler_params=pltpu.CompilerParams(vmem_limit_bytes=SMALL_VMEM),
        cost_estimate=pl.CostEstimate(flops=LOAD_COST, bytes_accessed=0, transcendentals=0),
        name="gate",
    )(block)


def inner_kernel(modes, out_ref):
    width = out_ref.shape[0]
    head = modes[:width, :]
    tail = modes[modes.shape[0] - width :, :]
    out_ref[...] = jnp.where(lax.rem(lax.axis_index("cell"), 2) == 0, tail, head)


def inner_edge(modes, width):
    return pl.pallas_call(
        inner_kernel,
        out_shape=jax.ShapeDtypeStruct((width, modes.shape[1]), modes.dtype),
        in_specs=[pl.BlockSpec(memory_space=pltpu.VMEM)],
        out_specs=pl.BlockSpec(memory_space=pltpu.VMEM),
        compiler_params=pltpu.CompilerParams(vmem_limit_bytes=SMALL_VMEM),
        name="inner_edge",
    )(modes)


def turn_kernel(keep_rows, modes, out_ref):
    n_modes, count = out_ref.shape
    step = count // 4
    for start in range(0, count, step):
        columns = slice(start, start + step)
        block = modes[columns, :].T
        if keep_rows % TILE_ROWS:
            out_ref[:, columns] = block
        else:
            for k in range(n_modes // keep_rows):
                place = k % 2 * (n_modes // 2) + k // 2 * keep_rows
                out_ref[place : place + keep_rows, columns] = block[k * keep_rows : (k + 1) * keep_rows]


def turn(modes, keep_rows):
    count, n_modes = modes.shape
    return pl.pallas_call(
        functools.partial(turn_kernel, keep_rows),
        out_shape=jax.ShapeDtypeStruct((n_modes, count), modes.dtype),
        in_specs=[pl.BlockSpec(memory_space=pltpu.VMEM)],
        out_specs=pl.BlockSpec(memory_space=pltpu.VMEM),
        compiler_params=pltpu.CompilerParams(vmem_limit_bytes=SMALL_VMEM),
        cost_estimate=pl.CostEstimate(flops=0, bytes_accessed=4 * modes.size, transcendentals=0),
        name="turn",
    )(modes)


def own_kernel(blocks, nb_ref, jac, modes, turned, p_ref, t_ref, jv, parts, face, near, far):
    slots, width, _ = jac.shape
    n_modes = modes.shape[1]

    def block_at(k):
        return pl.ds(pl.multiple_of(k * width, width), width)

    base = nb_ref[1, 0]
    n_near = jnp.int32(0)
    n_far = jnp.int32(0)
    for s in range(blocks, slots):
        r = nb_ref[0, s]
        c = nb_ref[1, s] - base
        inside = (c >= 0) & (c < blocks)
        near[0, n_near] = s
        near[1, n_near] = r
        near[2, n_near] = c
        far[0, n_far] = s
        far[1, n_far] = jnp.where(c < 0, 0, 1)
        n_near += ((r >= 0) & inside).astype(jnp.int32)
        n_far += ((r >= 0) & jnp.logical_not(inside)).astype(jnp.int32)
    near[0, n_near] = 0
    near[1, n_near] = blocks
    near[2, n_near] = 0
    far[0, n_far] = 0
    far[1, n_far] = 2

    for s in range(blocks):
        rows = pl.ds(s * width, width)
        jv[rows, :] = dot(jac[s], modes[rows, :])
    face[...] = jnp.zeros_like(face)

    def near_pair(k, carry):
        for j in (2 * k, 2 * k + 1):
            jv[block_at(near[1, j]), :] += dot(jac[near[0, j]], modes[block_at(near[2, j]), :])
        return carry

    def far_pair(k, carry):
        for j in (2 * k, 2 * k + 1):
            side = far[1, j]
            edge = block_at(jnp.where(side == 1, blocks - 1, 0))
            face[side] += dot(turned[:, edge], jac[far[0, j]])
        return carry

    lax.fori_loop(0, (n_near + 1) // 2, near_pair, 0)
    lax.fori_loop(0, (n_far + 1) // 2, far_pair, 0)

    mid = n_modes // 2
    for side in range(2):
        upper, lower = halves(face[side])
        for half in range(2):
            t_ref[side, half, :mid] = upper[half * mid : (half + 1) * mid]
            t_ref[side, half, mid:] = lower[half * mid : (half + 1) * mid]
    both = jnp.zeros((n_modes, 2 * n_modes), jnp.float32)
    step = width * (2 if blocks % 2 == 0 else 1)
    for start in range(0, blocks * width, step):
        rows = pl.ds(start, step)
        upper, lower = halves(jv[rows, :])
        parts[rows, :n_modes] = upper
        parts[rows, n_modes:] = lower
        both += dot(turned[:, rows], parts[rows, :])
    p_ref[...] = both[:, :n_modes] + both[:, n_modes:]


def own_part(neighbours, jac_blocks, modes, turned):
    slots, width, _ = jac_blocks.shape
    rows, n_modes = modes.shape
    blocks = rows // width
    flops = 2 * n_modes * width * width * slots + 4 * rows * n_modes * n_modes
    return pl.pallas_call(
        functools.partial(own_kernel, blocks),
        out_shape=(
            jax.ShapeDtypeStruct((n_modes, n_modes), jnp.float32),
            jax.ShapeDtypeStruct((2, 2, n_modes, width), jnp.bfloat16),
        ),
        in_specs=[
            pl.BlockSpec(memory_space=pltpu.SMEM),
            pl.BlockSpec(memory_space=pltpu.VMEM),
            pl.BlockSpec(memory_space=pltpu.VMEM),
            pl.BlockSpec(memory_space=pltpu.VMEM),
        ],
        out_specs=(pl.BlockSpec(memory_space=pltpu.VMEM), pl.BlockSpec(memory_space=pltpu.VMEM)),
        scratch_shapes=[
            pltpu.VMEM((rows + width, n_modes), jnp.float32),
            pltpu.VMEM((rows, 2 * n_modes), jnp.bfloat16),
            pltpu.VMEM((3, n_modes, width), jnp.float32),
            pltpu.SMEM((3, slots + 1), jnp.int32),
            pltpu.SMEM((2, slots + 1), jnp.int32),
        ],
        compiler_params=pltpu.CompilerParams(vmem_limit_bytes=OWN_VMEM),
        cost_estimate=pl.CostEstimate(
            flops=flops, bytes_accessed=slots * width * width * 2 + rows * n_modes * 2, transcendentals=0
        ),
        name="own_part",
    )(neighbours, jac_blocks, modes, turned)


def regrouped(value, axis, keep_rows):
    shape = value.shape
    split = shape[:axis] + (shape[axis] // (2 * keep_rows), 2, keep_rows) + shape[axis + 1 :]
    return jnp.swapaxes(value.reshape(split), axis, axis + 1).reshape(shape)


def join_kernel(other, p_ref, t_ref, outer_ref, inner_ref, out_ref):
    core = lax.rem(lax.axis_index("cell"), 2)
    count = out_ref.shape[0]
    half = 1 - core if other else core
    rows = pl.ds(pl.multiple_of(half * count, TILE_ROWS), count)
    both = dot(t_ref[1 - core, half], inner_ref[...]) + dot(t_ref[core, half], outer_ref[...])
    out_ref[...] = p_ref[rows, :] + both[:count] + both[count:]


def join(other, p, t, outer, inner):
    rows = p.shape[0] // 2
    return pl.pallas_call(
        functools.partial(join_kernel, other),
        out_shape=jax.ShapeDtypeStruct((rows, p.shape[1]), jnp.float32),
        in_specs=[pl.BlockSpec(memory_space=pltpu.VMEM)] * 4,
        out_specs=pl.BlockSpec(memory_space=pltpu.VMEM),
        compiler_params=pltpu.CompilerParams(vmem_limit_bytes=SMALL_VMEM),
        cost_estimate=pl.CostEstimate(flops=8 * rows * outer.size, bytes_accessed=0, transcendentals=0),
        name="join_give" if other else "join_keep",
    )(p, t, outer, inner)


def per_device(jac_blocks, modes, neighbours):
    width = jac_blocks.shape[1]
    rows, n_modes = modes.shape
    count = lax.axis_size("cell")
    keep_rows = n_modes // count
    across = [(i, min(max(i - 1 + 2 * (i % 2), 0), count - 1)) for i in range(count)]
    swap = [(i, i ^ 1) for i in range(count)]
    outer = lax.ppermute(gate(outer_edge(modes, width)), "cell", across)
    inner = lax.ppermute(inner_edge(modes, width), "cell", swap)
    p, t = own_part(neighbours.T, jac_blocks, modes, turn(modes, keep_rows))
    if keep_rows % TILE_ROWS:
        p = regrouped(p, 0, keep_rows)
        apart = jnp.swapaxes(t.reshape(2, 2, 2, n_modes // 2, width), 1, 2).reshape(2, 2, n_modes, width)
        apart = regrouped(apart, 2, keep_rows).reshape(2, 2, 2, n_modes // 2, width)
        t = jnp.swapaxes(apart, 1, 2).reshape(t.shape)
    got = lax.ppermute(join(True, p, t, outer, inner), "cell", swap)
    keep = join(False, p, t, outer, inner)
    pair = (keep + got).reshape(count // 2, keep_rows, n_modes)
    same_core = [list(range(core, count, 2)) for core in range(2)]
    parts = lax.all_to_all(pair, "cell", 0, 0, axis_index_groups=same_core)
    return jnp.sum(parts, axis=0)


def solution(mesh):
    placed = (P(("grp", "cell"), None, None), P(("grp", "cell"), None), P(("grp", "cell"), None))
    return jax.shard_map(
        per_device, mesh=mesh, in_specs=placed, out_specs=P(("grp", "cell"), None), check_vma=False
    )
```

```python
import functools

import jax
import jax.numpy as jnp
from jax import lax
from jax.experimental import pallas as pl
from jax.experimental.pallas import tpu as pltpu
from jax.sharding import PartitionSpec as P

OWN_VMEM = 24 * 2**20
SMALL_VMEM = 8 * 2**20
TILE_ROWS = 16
EDGE_COPIES = 8
LOAD_COST = 35 * 10**8


def dot(a, b):
    return jnp.dot(a, b, preferred_element_type=jnp.float32)


def halves(value):
    upper = value.astype(jnp.bfloat16)
    return upper, (value - upper.astype(jnp.float32)).astype(jnp.bfloat16)


def outer_kernel(modes_hbm, out_ref, sem):
    width = out_ref.shape[0]
    start = lax.rem(lax.axis_index("cell"), 2) * (modes_hbm.shape[0] - width)
    step = width // EDGE_COPIES
    copies = []
    for k in range(EDGE_COPIES):
        rows = pl.ds(pl.multiple_of(start + k * step, TILE_ROWS), step)
        copies.append(pltpu.make_async_copy(modes_hbm.at[rows, :], out_ref.at[pl.ds(k * step, step), :], sem.at[k]))
    for copy in copies:
        copy.start()
    for copy in copies:
        copy.wait()


def outer_edge(modes, width):
    return pl.pallas_call(
        outer_kernel,
        out_shape=jax.ShapeDtypeStruct((width, modes.shape[1]), modes.dtype),
        in_specs=[pl.BlockSpec(memory_space=pltpu.HBM)],
        out_specs=pl.BlockSpec(memory_space=pltpu.VMEM),
        scratch_shapes=[pltpu.SemaphoreType.DMA((EDGE_COPIES,))],
        compiler_params=pltpu.CompilerParams(vmem_limit_bytes=SMALL_VMEM),
        cost_estimate=pl.CostEstimate(flops=0, bytes_accessed=4 * width * modes.shape[1], transcendentals=0),
        name="outer_edge",
    )(pltpu.with_memory_space_constraint(modes, pltpu.HBM))


def gate_kernel(block_ref, out_ref):
    out_ref[...] = block_ref[...]


def gate(block):
    return pl.pallas_call(
        gate_kernel,
        out_shape=jax.ShapeDtypeStruct(block.shape, block.dtype),
        in_specs=[pl.BlockSpec(memory_space=pltpu.VMEM)],
        out_specs=pl.BlockSpec(memory_space=pltpu.VMEM),
        compiler_params=pltpu.CompilerParams(vmem_limit_bytes=SMALL_VMEM),
        cost_estimate=pl.CostEstimate(flops=LOAD_COST, bytes_accessed=0, transcendentals=0),
        name="gate",
    )(block)


def inner_kernel(modes, out_ref):
    width = out_ref.shape[0]
    head = modes[:width, :]
    tail = modes[modes.shape[0] - width :, :]
    out_ref[...] = jnp.where(lax.rem(lax.axis_index("cell"), 2) == 0, tail, head)


def inner_edge(modes, width):
    return pl.pallas_call(
        inner_kernel,
        out_shape=jax.ShapeDtypeStruct((width, modes.shape[1]), modes.dtype),
        in_specs=[pl.BlockSpec(memory_space=pltpu.VMEM)],
        out_specs=pl.BlockSpec(memory_space=pltpu.VMEM),
        compiler_params=pltpu.CompilerParams(vmem_limit_bytes=SMALL_VMEM),
        name="inner_edge",
    )(modes)


def turn_kernel(keep_rows, modes, out_ref):
    n_modes, count = out_ref.shape
    step = count // 4
    for start in range(0, count, step):
        columns = slice(start, start + step)
        block = modes[columns, :].T
        if keep_rows % TILE_ROWS:
            out_ref[:, columns] = block
        else:
            for k in range(n_modes // keep_rows):
                place = (k ^ k // 2) % 2 * (n_modes // 2) + k // 2 * keep_rows
                out_ref[place : place + keep_rows, columns] = block[k * keep_rows : (k + 1) * keep_rows]


def turn(modes, keep_rows):
    count, n_modes = modes.shape
    return pl.pallas_call(
        functools.partial(turn_kernel, keep_rows),
        out_shape=jax.ShapeDtypeStruct((n_modes, count), modes.dtype),
        in_specs=[pl.BlockSpec(memory_space=pltpu.VMEM)],
        out_specs=pl.BlockSpec(memory_space=pltpu.VMEM),
        compiler_params=pltpu.CompilerParams(vmem_limit_bytes=SMALL_VMEM),
        cost_estimate=pl.CostEstimate(flops=0, bytes_accessed=4 * modes.size, transcendentals=0),
        name="turn",
    )(modes)


def own_kernel(blocks, nb_ref, jac, modes, turned, p_ref, t_ref, jv, parts, face, near, far):
    slots, width, _ = jac.shape
    n_modes = modes.shape[1]

    def block_at(k):
        return pl.ds(pl.multiple_of(k * width, width), width)

    base = nb_ref[1, 0]
    n_near = jnp.int32(0)
    n_far = jnp.int32(0)
    for s in range(blocks, slots):
        r = nb_ref[0, s]
        c = nb_ref[1, s] - base
        inside = (c >= 0) & (c < blocks)
        near[0, n_near] = s
        near[1, n_near] = r
        near[2, n_near] = c
        far[0, n_far] = s
        far[1, n_far] = jnp.where(c < 0, 0, 1)
        n_near += ((r >= 0) & inside).astype(jnp.int32)
        n_far += ((r >= 0) & jnp.logical_not(inside)).astype(jnp.int32)
    near[0, n_near] = 0
    near[1, n_near] = blocks
    near[2, n_near] = 0
    far[0, n_far] = 0
    far[1, n_far] = 2

    for s in range(blocks):
        rows = pl.ds(s * width, width)
        jv[rows, :] = dot(jac[s], modes[rows, :])
    face[...] = jnp.zeros_like(face)

    def near_pair(k, carry):
        for j in (2 * k, 2 * k + 1):
            jv[block_at(near[1, j]), :] += dot(jac[near[0, j]], modes[block_at(near[2, j]), :])
        return carry

    def far_pair(k, carry):
        for j in (2 * k, 2 * k + 1):
            side = far[1, j]
            edge = block_at(jnp.where(side == 1, blocks - 1, 0))
            face[side] += dot(turned[:, edge], jac[far[0, j]])
        return carry

    lax.fori_loop(0, (n_near + 1) // 2, near_pair, 0)
    lax.fori_loop(0, (n_far + 1) // 2, far_pair, 0)

    mid = n_modes // 2
    for side in range(2):
        upper, lower = halves(face[side])
        for half in range(2):
            t_ref[side, half, :mid] = upper[half * mid : (half + 1) * mid]
            t_ref[side, half, mid:] = lower[half * mid : (half + 1) * mid]
    both = jnp.zeros((n_modes, 2 * n_modes), jnp.float32)
    step = width * (2 if blocks % 2 == 0 else 1)
    for start in range(0, blocks * width, step):
        rows = pl.ds(start, step)
        upper, lower = halves(jv[rows, :])
        parts[rows, :n_modes] = upper
        parts[rows, n_modes:] = lower
        both += dot(turned[:, rows], parts[rows, :])
    p_ref[...] = both[:, :n_modes] + both[:, n_modes:]


def own_part(neighbours, jac_blocks, modes, turned):
    slots, width, _ = jac_blocks.shape
    rows, n_modes = modes.shape
    blocks = rows // width
    flops = 2 * n_modes * width * width * slots + 4 * rows * n_modes * n_modes
    return pl.pallas_call(
        functools.partial(own_kernel, blocks),
        out_shape=(
            jax.ShapeDtypeStruct((n_modes, n_modes), jnp.float32),
            jax.ShapeDtypeStruct((2, 2, n_modes, width), jnp.bfloat16),
        ),
        in_specs=[
            pl.BlockSpec(memory_space=pltpu.SMEM),
            pl.BlockSpec(memory_space=pltpu.VMEM),
            pl.BlockSpec(memory_space=pltpu.VMEM),
            pl.BlockSpec(memory_space=pltpu.VMEM),
        ],
        out_specs=(pl.BlockSpec(memory_space=pltpu.VMEM), pl.BlockSpec(memory_space=pltpu.VMEM)),
        scratch_shapes=[
            pltpu.VMEM((rows + width, n_modes), jnp.float32),
            pltpu.VMEM((rows, 2 * n_modes), jnp.bfloat16),
            pltpu.VMEM((3, n_modes, width), jnp.float32),
            pltpu.SMEM((3, slots + 1), jnp.int32),
            pltpu.SMEM((2, slots + 1), jnp.int32),
        ],
        compiler_params=pltpu.CompilerParams(vmem_limit_bytes=OWN_VMEM),
        cost_estimate=pl.CostEstimate(
            flops=flops, bytes_accessed=slots * width * width * 2 + rows * n_modes * 2, transcendentals=0
        ),
        name="own_part",
    )(neighbours, jac_blocks, modes, turned)


def teams(count):
    return [[2 * chip + (chip + half) % 2 for chip in range(count // 2)] for half in range(2)]


def own_team():
    me = lax.axis_index("cell")
    return lax.rem(me + me // 2, 2)


def regrouped(value, axis, keep_rows):
    first, second = teams(value.shape[axis] // keep_rows)
    starts = [k * keep_rows for k in first + second]
    return jnp.concatenate([lax.slice_in_dim(value, k, k + keep_rows, axis=axis) for k in starts], axis=axis)


def join_kernel(other, p_ref, t_ref, outer_ref, inner_ref, out_ref):
    core = lax.rem(lax.axis_index("cell"), 2)
    count = out_ref.shape[0]
    half = 1 - own_team() if other else own_team()
    rows = pl.ds(pl.multiple_of(half * count, TILE_ROWS), count)
    both = dot(t_ref[1 - core, half], inner_ref[...]) + dot(t_ref[core, half], outer_ref[...])
    out_ref[...] = p_ref[rows, :] + both[:count] + both[count:]


def join(other, p, t, outer, inner):
    rows = p.shape[0] // 2
    return pl.pallas_call(
        functools.partial(join_kernel, other),
        out_shape=jax.ShapeDtypeStruct((rows, p.shape[1]), jnp.float32),
        in_specs=[pl.BlockSpec(memory_space=pltpu.VMEM)] * 4,
        out_specs=pl.BlockSpec(memory_space=pltpu.VMEM),
        compiler_params=pltpu.CompilerParams(vmem_limit_bytes=SMALL_VMEM),
        cost_estimate=pl.CostEstimate(flops=8 * rows * outer.size, bytes_accessed=0, transcendentals=0),
        name="join_give" if other else "join_keep",
    )(p, t, outer, inner)


def per_device(jac_blocks, modes, neighbours):
    width = jac_blocks.shape[1]
    rows, n_modes = modes.shape
    count = lax.axis_size("cell")
    keep_rows = n_modes // count
    across = [(i, min(max(i - 1 + 2 * (i % 2), 0), count - 1)) for i in range(count)]
    swap = [(i, i ^ 1) for i in range(count)]
    outer = lax.ppermute(gate(outer_edge(modes, width)), "cell", across)
    inner = lax.ppermute(inner_edge(modes, width), "cell", swap)
    p, t = own_part(neighbours.T, jac_blocks, modes, turn(modes, keep_rows))
    if keep_rows % TILE_ROWS:
        p = regrouped(p, 0, keep_rows)
        apart = jnp.swapaxes(t.reshape(2, 2, 2, n_modes // 2, width), 1, 2).reshape(2, 2, n_modes, width)
        apart = regrouped(apart, 2, keep_rows).reshape(2, 2, 2, n_modes // 2, width)
        t = jnp.swapaxes(apart, 1, 2).reshape(t.shape)
    got = lax.ppermute(join(True, p, t, outer, inner), "cell", swap)
    keep = join(False, p, t, outer, inner)
    pair = (keep + got).reshape(count // 2, keep_rows, n_modes)
    parts = lax.all_to_all(pair, "cell", 0, 0, axis_index_groups=teams(count))
    return jnp.sum(parts, axis=0)


def solution(mesh):
    placed = (P(("grp", "cell"), None, None), P(("grp", "cell"), None), P(("grp", "cell"), None))
    return jax.shard_map(
        per_device, mesh=mesh, in_specs=placed, out_specs=P(("grp", "cell"), None), check_vma=False
    )
```

```python
import functools

import jax
import jax.numpy as jnp
from jax import lax
from jax.experimental import pallas as pl
from jax.experimental.pallas import tpu as pltpu
from jax.sharding import PartitionSpec as P

OWN_VMEM = 24 * 2**20
SMALL_VMEM = 8 * 2**20
TILE_ROWS = 16
LOAD_COST = 35 * 10**8


def dot(a, b):
    return jnp.dot(a, b, preferred_element_type=jnp.float32)


def halves(value):
    upper = value.astype(jnp.bfloat16)
    return upper, (value - upper.astype(jnp.float32)).astype(jnp.bfloat16)


def outer_kernel(modes_hbm, out_ref, sem):
    width = out_ref.shape[0]
    start = lax.rem(lax.axis_index("cell"), 2) * (modes_hbm.shape[0] - width)
    copy = pltpu.make_async_copy(modes_hbm.at[pl.ds(pl.multiple_of(start, 128), width), :], out_ref, sem)
    copy.start()
    copy.wait()


def outer_edge(modes, width):
    return pl.pallas_call(
        outer_kernel,
        out_shape=jax.ShapeDtypeStruct((width, modes.shape[1]), modes.dtype),
        in_specs=[pl.BlockSpec(memory_space=pltpu.HBM)],
        out_specs=pl.BlockSpec(memory_space=pltpu.VMEM),
        scratch_shapes=[pltpu.SemaphoreType.DMA],
        compiler_params=pltpu.CompilerParams(vmem_limit_bytes=SMALL_VMEM),
        cost_estimate=pl.CostEstimate(flops=0, bytes_accessed=4 * width * modes.shape[1], transcendentals=0),
        name="outer_edge",
    )(pltpu.with_memory_space_constraint(modes, pltpu.HBM))


def gate_kernel(block_ref, out_ref):
    out_ref[...] = block_ref[...]


def gate(block):
    return pl.pallas_call(
        gate_kernel,
        out_shape=jax.ShapeDtypeStruct(block.shape, block.dtype),
        in_specs=[pl.BlockSpec(memory_space=pltpu.VMEM)],
        out_specs=pl.BlockSpec(memory_space=pltpu.VMEM),
        compiler_params=pltpu.CompilerParams(vmem_limit_bytes=SMALL_VMEM),
        cost_estimate=pl.CostEstimate(flops=LOAD_COST, bytes_accessed=0, transcendentals=0),
        name="gate",
    )(block)


def inner_kernel(modes, out_ref):
    width = out_ref.shape[0]
    head = modes[:width, :]
    tail = modes[modes.shape[0] - width :, :]
    out_ref[...] = jnp.where(lax.rem(lax.axis_index("cell"), 2) == 0, tail, head)


def inner_edge(modes, width):
    return pl.pallas_call(
        inner_kernel,
        out_shape=jax.ShapeDtypeStruct((width, modes.shape[1]), modes.dtype),
        in_specs=[pl.BlockSpec(memory_space=pltpu.VMEM)],
        out_specs=pl.BlockSpec(memory_space=pltpu.VMEM),
        compiler_params=pltpu.CompilerParams(vmem_limit_bytes=SMALL_VMEM),
        name="inner_edge",
    )(modes)


def turn_kernel(keep_rows, modes, out_ref):
    n_modes, count = out_ref.shape
    step = count // 4
    for start in range(0, count, step):
        columns = slice(start, start + step)
        block = modes[columns, :].T
        if keep_rows % TILE_ROWS:
            out_ref[:, columns] = block
        else:
            for k in range(n_modes // keep_rows):
                place = (k ^ k // 2) % 2 * (n_modes // 2) + n_modes // 2 - (k // 2 + 1) * keep_rows
                out_ref[place : place + keep_rows, columns] = block[k * keep_rows : (k + 1) * keep_rows]


def turn(modes, keep_rows):
    count, n_modes = modes.shape
    return pl.pallas_call(
        functools.partial(turn_kernel, keep_rows),
        out_shape=jax.ShapeDtypeStruct((n_modes, count), modes.dtype),
        in_specs=[pl.BlockSpec(memory_space=pltpu.VMEM)],
        out_specs=pl.BlockSpec(memory_space=pltpu.VMEM),
        compiler_params=pltpu.CompilerParams(vmem_limit_bytes=SMALL_VMEM),
        cost_estimate=pl.CostEstimate(flops=0, bytes_accessed=4 * modes.size, transcendentals=0),
        name="turn",
    )(modes)


def own_kernel(blocks, nb_ref, jac, modes, turned, p_ref, t_ref, jv, parts, face, near, far):
    slots, width, _ = jac.shape
    n_modes = modes.shape[1]

    def block_at(k):
        return pl.ds(pl.multiple_of(k * width, width), width)

    base = nb_ref[1, 0]
    n_near = jnp.int32(0)
    n_far = jnp.int32(0)
    for s in range(blocks, slots):
        r = nb_ref[0, s]
        c = nb_ref[1, s] - base
        inside = (c >= 0) & (c < blocks)
        near[0, n_near] = s
        near[1, n_near] = r
        near[2, n_near] = c
        far[0, n_far] = s
        far[1, n_far] = jnp.where(c < 0, 0, 1)
        n_near += ((r >= 0) & inside).astype(jnp.int32)
        n_far += ((r >= 0) & jnp.logical_not(inside)).astype(jnp.int32)
    near[0, n_near] = 0
    near[1, n_near] = blocks
    near[2, n_near] = 0
    far[0, n_far] = 0
    far[1, n_far] = 2

    for s in range(blocks):
        rows = pl.ds(s * width, width)
        jv[rows, :] = dot(jac[s], modes[rows, :])
    face[...] = jnp.zeros_like(face)

    def near_pair(k, carry):
        for j in (2 * k, 2 * k + 1):
            jv[block_at(near[1, j]), :] += dot(jac[near[0, j]], modes[block_at(near[2, j]), :])
        return carry

    def far_pair(k, carry):
        for j in (2 * k, 2 * k + 1):
            side = far[1, j]
            edge = block_at(jnp.where(side == 1, blocks - 1, 0))
            face[side] += dot(turned[:, edge], jac[far[0, j]])
        return carry

    lax.fori_loop(0, (n_near + 1) // 2, near_pair, 0)
    lax.fori_loop(0, (n_far + 1) // 2, far_pair, 0)

    mid = n_modes // 2
    for side in range(2):
        upper, lower = halves(face[side])
        for half in range(2):
            t_ref[side, half, :mid] = upper[half * mid : (half + 1) * mid]
            t_ref[side, half, mid:] = lower[half * mid : (half + 1) * mid]
    both = jnp.zeros((n_modes, 2 * n_modes), jnp.float32)
    step = width * (2 if blocks % 2 == 0 else 1)
    for start in range(0, blocks * width, step):
        rows = pl.ds(start, step)
        upper, lower = halves(jv[rows, :])
        parts[rows, :n_modes] = upper
        parts[rows, n_modes:] = lower
        both += dot(turned[:, rows], parts[rows, :])
    p_ref[...] = both[:, :n_modes] + both[:, n_modes:]


def own_part(neighbours, jac_blocks, modes, turned):
    slots, width, _ = jac_blocks.shape
    rows, n_modes = modes.shape
    blocks = rows // width
    flops = 2 * n_modes * width * width * slots + 4 * rows * n_modes * n_modes
    return pl.pallas_call(
        functools.partial(own_kernel, blocks),
        out_shape=(
            jax.ShapeDtypeStruct((n_modes, n_modes), jnp.float32),
            jax.ShapeDtypeStruct((2, 2, n_modes, width), jnp.bfloat16),
        ),
        in_specs=[
            pl.BlockSpec(memory_space=pltpu.SMEM),
            pl.BlockSpec(memory_space=pltpu.VMEM),
            pl.BlockSpec(memory_space=pltpu.VMEM),
            pl.BlockSpec(memory_space=pltpu.VMEM),
        ],
        out_specs=(pl.BlockSpec(memory_space=pltpu.VMEM), pl.BlockSpec(memory_space=pltpu.VMEM)),
        scratch_shapes=[
            pltpu.VMEM((rows + width, n_modes), jnp.float32),
            pltpu.VMEM((rows, 2 * n_modes), jnp.bfloat16),
            pltpu.VMEM((3, n_modes, width), jnp.float32),
            pltpu.SMEM((3, slots + 1), jnp.int32),
            pltpu.SMEM((2, slots + 1), jnp.int32),
        ],
        compiler_params=pltpu.CompilerParams(vmem_limit_bytes=OWN_VMEM),
        cost_estimate=pl.CostEstimate(
            flops=flops, bytes_accessed=slots * width * width * 2 + rows * n_modes * 2, transcendentals=0
        ),
        name="own_part",
    )(neighbours, jac_blocks, modes, turned)


def teams(count):
    return [[2 * chip + (chip + half) % 2 for chip in reversed(range(count // 2))] for half in range(2)]


def own_team():
    me = lax.axis_index("cell")
    return lax.rem(me + me // 2, 2)


def regrouped(value, axis, keep_rows):
    first, second = teams(value.shape[axis] // keep_rows)
    starts = [k * keep_rows for k in first + second]
    return jnp.concatenate([lax.slice_in_dim(value, k, k + keep_rows, axis=axis) for k in starts], axis=axis)


def join_kernel(other, p_ref, t_ref, outer_ref, inner_ref, out_ref):
    core = lax.rem(lax.axis_index("cell"), 2)
    count = out_ref.shape[0]
    half = 1 - own_team() if other else own_team()
    rows = pl.ds(pl.multiple_of(half * count, TILE_ROWS), count)
    both = dot(t_ref[1 - core, half], inner_ref[...]) + dot(t_ref[core, half], outer_ref[...])
    out_ref[...] = p_ref[rows, :] + both[:count] + both[count:]


def join(other, p, t, outer, inner):
    rows = p.shape[0] // 2
    return pl.pallas_call(
        functools.partial(join_kernel, other),
        out_shape=jax.ShapeDtypeStruct((rows, p.shape[1]), jnp.float32),
        in_specs=[pl.BlockSpec(memory_space=pltpu.VMEM)] * 4,
        out_specs=pl.BlockSpec(memory_space=pltpu.VMEM),
        compiler_params=pltpu.CompilerParams(vmem_limit_bytes=SMALL_VMEM),
        cost_estimate=pl.CostEstimate(flops=8 * rows * outer.size, bytes_accessed=0, transcendentals=0),
        name="join_give" if other else "join_keep",
    )(p, t, outer, inner)


def per_device(jac_blocks, modes, neighbours):
    width = jac_blocks.shape[1]
    rows, n_modes = modes.shape
    count = lax.axis_size("cell")
    keep_rows = n_modes // count
    across = [(i, min(max(i - 1 + 2 * (i % 2), 0), count - 1)) for i in range(count)]
    swap = [(i, i ^ 1) for i in range(count)]
    outer = lax.ppermute(gate(outer_edge(modes, width)), "cell", across)
    inner = lax.ppermute(inner_edge(modes, width), "cell", swap)
    p, t = own_part(neighbours.T, jac_blocks, modes, turn(modes, keep_rows))
    if keep_rows % TILE_ROWS:
        p = regrouped(p, 0, keep_rows)
        apart = jnp.swapaxes(t.reshape(2, 2, 2, n_modes // 2, width), 1, 2).reshape(2, 2, n_modes, width)
        apart = regrouped(apart, 2, keep_rows).reshape(2, 2, 2, n_modes // 2, width)
        t = jnp.swapaxes(apart, 1, 2).reshape(t.shape)
    got = lax.ppermute(join(True, p, t, outer, inner), "cell", swap)
    keep = join(False, p, t, outer, inner)
    pair = (keep + got).reshape(count // 2, keep_rows, n_modes)
    parts = lax.all_to_all(pair, "cell", 0, 0, axis_index_groups=teams(count))
    return jnp.sum(parts, axis=0)


def solution(mesh):
    placed = (P(("grp", "cell"), None, None), P(("grp", "cell"), None), P(("grp", "cell"), None))
    return jax.shard_map(
        per_device, mesh=mesh, in_specs=placed, out_specs=P(("grp", "cell"), None), check_vma=False
    )
```

```python
import functools

import jax
import jax.numpy as jnp
from jax import lax
from jax.experimental import pallas as pl
from jax.experimental.pallas import tpu as pltpu
from jax.sharding import PartitionSpec as P

OWN_VMEM = 24 * 2**20
SMALL_VMEM = 8 * 2**20
TILE_ROWS = 16
LOAD_COST = 35 * 10**8


def dot(a, b):
    return jnp.dot(a, b, preferred_element_type=jnp.float32)


def halves(value):
    upper = value.astype(jnp.bfloat16)
    return upper, (value - upper.astype(jnp.float32)).astype(jnp.bfloat16)


def gate_kernel(block_ref, out_ref):
    out_ref[...] = block_ref[...]


def gate(block):
    return pl.pallas_call(
        gate_kernel,
        out_shape=jax.ShapeDtypeStruct(block.shape, block.dtype),
        in_specs=[pl.BlockSpec(memory_space=pltpu.VMEM)],
        out_specs=pl.BlockSpec(memory_space=pltpu.VMEM),
        compiler_params=pltpu.CompilerParams(vmem_limit_bytes=SMALL_VMEM),
        cost_estimate=pl.CostEstimate(flops=LOAD_COST, bytes_accessed=0, transcendentals=0),
        name="gate",
    )(block)


def inner_kernel(modes, out_ref):
    width = out_ref.shape[0]
    head = modes[:width, :]
    tail = modes[modes.shape[0] - width :, :]
    out_ref[...] = jnp.where(lax.rem(lax.axis_index("cell"), 2) == 0, tail, head)


def inner_edge(modes, width):
    return pl.pallas_call(
        inner_kernel,
        out_shape=jax.ShapeDtypeStruct((width, modes.shape[1]), modes.dtype),
        in_specs=[pl.BlockSpec(memory_space=pltpu.VMEM)],
        out_specs=pl.BlockSpec(memory_space=pltpu.VMEM),
        compiler_params=pltpu.CompilerParams(vmem_limit_bytes=SMALL_VMEM),
        name="inner_edge",
    )(modes)


def turn_kernel(keep_rows, modes, out_ref):
    n_modes, count = out_ref.shape
    step = count // 4
    for start in range(0, count, step):
        columns = slice(start, start + step)
        block = modes[columns, :].T
        if keep_rows % TILE_ROWS:
            out_ref[:, columns] = block
        else:
            for k in range(n_modes // keep_rows):
                place = (k ^ k // 2) % 2 * (n_modes // 2) + n_modes // 2 - (k // 2 + 1) * keep_rows
                out_ref[place : place + keep_rows, columns] = block[k * keep_rows : (k + 1) * keep_rows]


def turn(modes, keep_rows):
    count, n_modes = modes.shape
    return pl.pallas_call(
        functools.partial(turn_kernel, keep_rows),
        out_shape=jax.ShapeDtypeStruct((n_modes, count), modes.dtype),
        in_specs=[pl.BlockSpec(memory_space=pltpu.VMEM)],
        out_specs=pl.BlockSpec(memory_space=pltpu.VMEM),
        compiler_params=pltpu.CompilerParams(vmem_limit_bytes=SMALL_VMEM),
        cost_estimate=pl.CostEstimate(flops=0, bytes_accessed=4 * modes.size, transcendentals=0),
        name="turn",
    )(modes)


def own_kernel(blocks, nb_ref, jac, modes, turned, p_ref, t_ref, jv, parts, face, near, far):
    slots, width, _ = jac.shape
    n_modes = modes.shape[1]

    def block_at(k):
        return pl.ds(pl.multiple_of(k * width, width), width)

    base = nb_ref[1, 0]
    n_near = jnp.int32(0)
    n_far = jnp.int32(0)
    for s in range(blocks, slots):
        r = nb_ref[0, s]
        c = nb_ref[1, s] - base
        inside = (c >= 0) & (c < blocks)
        near[0, n_near] = s
        near[1, n_near] = r
        near[2, n_near] = c
        far[0, n_far] = s
        far[1, n_far] = jnp.where(c < 0, 0, 1)
        n_near += ((r >= 0) & inside).astype(jnp.int32)
        n_far += ((r >= 0) & jnp.logical_not(inside)).astype(jnp.int32)
    near[0, n_near] = 0
    near[1, n_near] = blocks
    near[2, n_near] = 0
    far[0, n_far] = 0
    far[1, n_far] = 2

    for s in range(blocks):
        rows = pl.ds(s * width, width)
        jv[rows, :] = dot(jac[s], modes[rows, :])
    face[...] = jnp.zeros_like(face)

    def near_pair(k, carry):
        for j in (2 * k, 2 * k + 1):
            jv[block_at(near[1, j]), :] += dot(jac[near[0, j]], modes[block_at(near[2, j]), :])
        return carry

    def far_pair(k, carry):
        for j in (2 * k, 2 * k + 1):
            side = far[1, j]
            edge = block_at(jnp.where(side == 1, blocks - 1, 0))
            face[side] += dot(turned[:, edge], jac[far[0, j]])
        return carry

    lax.fori_loop(0, (n_near + 1) // 2, near_pair, 0)
    lax.fori_loop(0, (n_far + 1) // 2, far_pair, 0)

    mid = n_modes // 2
    for side in range(2):
        upper, lower = halves(face[side])
        for half in range(2):
            t_ref[side, half, :mid] = upper[half * mid : (half + 1) * mid]
            t_ref[side, half, mid:] = lower[half * mid : (half + 1) * mid]
    both = jnp.zeros((n_modes, 2 * n_modes), jnp.float32)
    step = width * (2 if blocks % 2 == 0 else 1)
    for start in range(0, blocks * width, step):
        rows = pl.ds(start, step)
        upper, lower = halves(jv[rows, :])
        parts[rows, :n_modes] = upper
        parts[rows, n_modes:] = lower
        both += dot(turned[:, rows], parts[rows, :])
    p_ref[...] = both[:, :n_modes] + both[:, n_modes:]


def own_part(neighbours, jac_blocks, modes, turned):
    slots, width, _ = jac_blocks.shape
    rows, n_modes = modes.shape
    blocks = rows // width
    flops = 2 * n_modes * width * width * slots + 4 * rows * n_modes * n_modes
    return pl.pallas_call(
        functools.partial(own_kernel, blocks),
        out_shape=(
            jax.ShapeDtypeStruct((n_modes, n_modes), jnp.float32),
            jax.ShapeDtypeStruct((2, 2, n_modes, width), jnp.bfloat16),
        ),
        in_specs=[
            pl.BlockSpec(memory_space=pltpu.SMEM),
            pl.BlockSpec(memory_space=pltpu.VMEM),
            pl.BlockSpec(memory_space=pltpu.VMEM),
            pl.BlockSpec(memory_space=pltpu.VMEM),
        ],
        out_specs=(pl.BlockSpec(memory_space=pltpu.VMEM), pl.BlockSpec(memory_space=pltpu.VMEM)),
        scratch_shapes=[
            pltpu.VMEM((rows + width, n_modes), jnp.float32),
            pltpu.VMEM((rows, 2 * n_modes), jnp.bfloat16),
            pltpu.VMEM((3, n_modes, width), jnp.float32),
            pltpu.SMEM((3, slots + 1), jnp.int32),
            pltpu.SMEM((2, slots + 1), jnp.int32),
        ],
        compiler_params=pltpu.CompilerParams(vmem_limit_bytes=OWN_VMEM),
        cost_estimate=pl.CostEstimate(
            flops=flops, bytes_accessed=slots * width * width * 2 + rows * n_modes * 2, transcendentals=0
        ),
        name="own_part",
    )(neighbours, jac_blocks, modes, turned)


def teams(count):
    return [[2 * chip + (chip + half) % 2 for chip in reversed(range(count // 2))] for half in range(2)]


def own_team():
    me = lax.axis_index("cell")
    return lax.rem(me + me // 2, 2)


def regrouped(value, axis, keep_rows):
    first, second = teams(value.shape[axis] // keep_rows)
    starts = [k * keep_rows for k in first + second]
    return jnp.concatenate([lax.slice_in_dim(value, k, k + keep_rows, axis=axis) for k in starts], axis=axis)


def join_kernel(other, p_ref, t_ref, outer_ref, inner_ref, out_ref):
    core = lax.rem(lax.axis_index("cell"), 2)
    count = out_ref.shape[0]
    half = 1 - own_team() if other else own_team()
    rows = pl.ds(pl.multiple_of(half * count, TILE_ROWS), count)
    both = dot(t_ref[1 - core, half], inner_ref[...]) + dot(t_ref[core, half], outer_ref[...])
    out_ref[...] = p_ref[rows, :] + both[:count] + both[count:]


def join(other, p, t, outer, inner):
    rows = p.shape[0] // 2
    return pl.pallas_call(
        functools.partial(join_kernel, other),
        out_shape=jax.ShapeDtypeStruct((rows, p.shape[1]), jnp.float32),
        in_specs=[pl.BlockSpec(memory_space=pltpu.VMEM)] * 4,
        out_specs=pl.BlockSpec(memory_space=pltpu.VMEM),
        compiler_params=pltpu.CompilerParams(vmem_limit_bytes=SMALL_VMEM),
        cost_estimate=pl.CostEstimate(flops=8 * rows * outer.size, bytes_accessed=0, transcendentals=0),
        name="join_give" if other else "join_keep",
    )(p, t, outer, inner)


def sum_kernel(parts_ref, out_hbm, total, sem):
    total[...] = jnp.sum(parts_ref[...], axis=0)
    copy = pltpu.make_async_copy(total, out_hbm, sem)
    copy.start()
    copy.wait()


def sum_parts(parts):
    return pl.pallas_call(
        sum_kernel,
        out_shape=jax.ShapeDtypeStruct(parts.shape[1:], parts.dtype),
        in_specs=[pl.BlockSpec(memory_space=pltpu.VMEM)],
        out_specs=pl.BlockSpec(memory_space=pl.ANY),
        scratch_shapes=[pltpu.VMEM(parts.shape[1:], parts.dtype), pltpu.SemaphoreType.DMA],
        compiler_params=pltpu.CompilerParams(vmem_limit_bytes=SMALL_VMEM),
        name="sum_parts",
    )(parts)


def per_device(jac_blocks, modes, neighbours):
    width = jac_blocks.shape[1]
    rows, n_modes = modes.shape
    count = lax.axis_size("cell")
    keep_rows = n_modes // count
    across = [(i, min(max(i - 1 + 2 * (i % 2), 0), count - 1)) for i in range(count)]
    swap = [(i, i ^ 1) for i in range(count)]
    core = lax.rem(lax.axis_index("cell"), 2)
    outer_edge = lax.dynamic_slice_in_dim(modes, core * (rows - width), width)
    outer = lax.ppermute(gate(outer_edge), "cell", across)
    inner = lax.ppermute(inner_edge(modes, width), "cell", swap)
    p, t = own_part(neighbours.T, jac_blocks, modes, turn(modes, keep_rows))
    if keep_rows % TILE_ROWS:
        p = regrouped(p, 0, keep_rows)
        apart = jnp.swapaxes(t.reshape(2, 2, 2, n_modes // 2, width), 1, 2).reshape(2, 2, n_modes, width)
        apart = regrouped(apart, 2, keep_rows).reshape(2, 2, 2, n_modes // 2, width)
        t = jnp.swapaxes(apart, 1, 2).reshape(t.shape)
    got = lax.ppermute(join(True, p, t, outer, inner), "cell", swap)
    keep = join(False, p, t, outer, inner)
    pair = (keep + got).reshape(count // 2, keep_rows, n_modes)
    parts = lax.all_to_all(pair, "cell", 0, 0, axis_index_groups=teams(count))
    return sum_parts(parts)


def solution(mesh):
    placed = (P(("grp", "cell"), None, None), P(("grp", "cell"), None), P(("grp", "cell"), None))
    return jax.shard_map(
        per_device, mesh=mesh, in_specs=placed, out_specs=P(("grp", "cell"), None), check_vma=False
    )
```

```python
import functools

import jax
import jax.numpy as jnp
from jax import lax
from jax.experimental import pallas as pl
from jax.experimental.pallas import tpu as pltpu
from jax.sharding import PartitionSpec as P

OWN_VMEM = 24 * 2**20
SMALL_VMEM = 8 * 2**20
TILE_ROWS = 16
LOAD_COST = 35 * 10**8


def dot(a, b):
    return jnp.dot(a, b, preferred_element_type=jnp.float32)


def halves(value):
    upper = value.astype(jnp.bfloat16)
    return upper, (value - upper.astype(jnp.float32)).astype(jnp.bfloat16)


def gate_kernel(block_ref, out_ref):
    out_ref[...] = block_ref[...]


def gate(block):
    return pl.pallas_call(
        gate_kernel,
        out_shape=jax.ShapeDtypeStruct(block.shape, block.dtype),
        in_specs=[pl.BlockSpec(memory_space=pltpu.VMEM)],
        out_specs=pl.BlockSpec(memory_space=pltpu.VMEM),
        compiler_params=pltpu.CompilerParams(vmem_limit_bytes=SMALL_VMEM),
        cost_estimate=pl.CostEstimate(flops=LOAD_COST, bytes_accessed=0, transcendentals=0),
        name="gate",
    )(block)


def inner_kernel(modes, out_ref):
    width = out_ref.shape[0]
    head = modes[:width, :]
    tail = modes[modes.shape[0] - width :, :]
    out_ref[...] = jnp.where(lax.rem(lax.axis_index("cell"), 2) == 0, tail, head)


def inner_edge(modes, width):
    return pl.pallas_call(
        inner_kernel,
        out_shape=jax.ShapeDtypeStruct((width, modes.shape[1]), modes.dtype),
        in_specs=[pl.BlockSpec(memory_space=pltpu.VMEM)],
        out_specs=pl.BlockSpec(memory_space=pltpu.VMEM),
        compiler_params=pltpu.CompilerParams(vmem_limit_bytes=SMALL_VMEM),
        name="inner_edge",
    )(modes)


def turn_kernel(keep_rows, modes, out_ref):
    n_modes, count = out_ref.shape
    step = count // 4
    for start in range(0, count, step):
        columns = slice(start, start + step)
        block = modes[columns, :].T
        if keep_rows % TILE_ROWS:
            out_ref[:, columns] = block
        else:
            for k in range(n_modes // keep_rows):
                place = (k ^ k // 2) % 2 * (n_modes // 2) + n_modes // 2 - (k // 2 + 1) * keep_rows
                out_ref[place : place + keep_rows, columns] = block[k * keep_rows : (k + 1) * keep_rows]


def turn(modes, keep_rows):
    count, n_modes = modes.shape
    return pl.pallas_call(
        functools.partial(turn_kernel, keep_rows),
        out_shape=jax.ShapeDtypeStruct((n_modes, count), modes.dtype),
        in_specs=[pl.BlockSpec(memory_space=pltpu.VMEM)],
        out_specs=pl.BlockSpec(memory_space=pltpu.VMEM),
        compiler_params=pltpu.CompilerParams(vmem_limit_bytes=SMALL_VMEM),
        cost_estimate=pl.CostEstimate(flops=0, bytes_accessed=4 * modes.size, transcendentals=0),
        name="turn",
    )(modes)


def own_kernel(blocks, nb_ref, jac, modes, turned, p_ref, t_ref, left, parts, live):
    slots, width, _ = jac.shape
    n_modes = modes.shape[1]
    mid = n_modes // 2

    base = nb_ref[1, 0]
    count = jnp.int32(0)
    for s in range(blocks, slots):
        r = nb_ref[0, s]
        live[0, count] = s
        live[1, count] = r
        live[2, count] = nb_ref[1, s] - base + 1
        count += (r >= 0).astype(jnp.int32)
    live[0, count] = 0
    live[1, count] = 0
    live[2, count] = blocks + 2

    for s in range(blocks):
        left[s + 1] = dot(turned[:, s * width : (s + 1) * width], jac[s])
    left[0] = jnp.zeros((n_modes, width), jnp.float32)
    left[blocks + 1] = jnp.zeros((n_modes, width), jnp.float32)

    def pair(k, carry):
        for j in (2 * k, 2 * k + 1):
            columns = pl.ds(pl.multiple_of(live[1, j] * width, width), width)
            left[live[2, j]] += dot(turned[:, columns], jac[live[0, j]])
        return carry

    lax.fori_loop(0, (count + 1) // 2, pair, 0)

    both = jnp.zeros((2 * n_modes, n_modes), jnp.float32)
    step = 2 if blocks % 2 == 0 else 1
    for first in range(0, blocks, step):
        for c in range(first, first + step):
            upper, lower = halves(left[c + 1])
            parts[:n_modes, c * width : (c + 1) * width] = upper
            parts[n_modes:, c * width : (c + 1) * width] = lower
        inner = slice(first * width, (first + step) * width)
        both += dot(parts[:, inner], modes[inner, :])
    p_ref[...] = both[:n_modes] + both[n_modes:]
    for side, c in enumerate((0, blocks + 1)):
        upper, lower = halves(left[c])
        for half in range(2):
            t_ref[side, half, :mid] = upper[half * mid : (half + 1) * mid]
            t_ref[side, half, mid:] = lower[half * mid : (half + 1) * mid]


def own_part(neighbours, jac_blocks, modes, turned):
    slots, width, _ = jac_blocks.shape
    rows, n_modes = modes.shape
    blocks = rows // width
    flops = 2 * n_modes * width * width * slots + 4 * rows * n_modes * n_modes
    return pl.pallas_call(
        functools.partial(own_kernel, blocks),
        out_shape=(
            jax.ShapeDtypeStruct((n_modes, n_modes), jnp.float32),
            jax.ShapeDtypeStruct((2, 2, n_modes, width), jnp.bfloat16),
        ),
        in_specs=[
            pl.BlockSpec(memory_space=pltpu.SMEM),
            pl.BlockSpec(memory_space=pltpu.VMEM),
            pl.BlockSpec(memory_space=pltpu.VMEM),
            pl.BlockSpec(memory_space=pltpu.VMEM),
        ],
        out_specs=(pl.BlockSpec(memory_space=pltpu.VMEM), pl.BlockSpec(memory_space=pltpu.VMEM)),
        scratch_shapes=[
            pltpu.VMEM((blocks + 3, n_modes, width), jnp.float32),
            pltpu.VMEM((2 * n_modes, rows), jnp.bfloat16),
            pltpu.SMEM((3, slots + 1), jnp.int32),
        ],
        compiler_params=pltpu.CompilerParams(vmem_limit_bytes=OWN_VMEM),
        cost_estimate=pl.CostEstimate(
            flops=flops, bytes_accessed=slots * width * width * 2 + rows * n_modes * 2, transcendentals=0
        ),
        name="own_part",
    )(neighbours, jac_blocks, modes, turned)


def teams(count):
    return [[2 * chip + (chip + half) % 2 for chip in reversed(range(count // 2))] for half in range(2)]


def own_team():
    me = lax.axis_index("cell")
    return lax.rem(me + me // 2, 2)


def regrouped(value, axis, keep_rows):
    first, second = teams(value.shape[axis] // keep_rows)
    starts = [k * keep_rows for k in first + second]
    return jnp.concatenate([lax.slice_in_dim(value, k, k + keep_rows, axis=axis) for k in starts], axis=axis)


def join_kernel(other, p_ref, t_ref, outer_ref, inner_ref, out_ref):
    core = lax.rem(lax.axis_index("cell"), 2)
    count = out_ref.shape[0]
    half = 1 - own_team() if other else own_team()
    rows = pl.ds(pl.multiple_of(half * count, TILE_ROWS), count)
    both = dot(t_ref[1 - core, half], inner_ref[...]) + dot(t_ref[core, half], outer_ref[...])
    out_ref[...] = p_ref[rows, :] + both[:count] + both[count:]


def join(other, p, t, outer, inner):
    rows = p.shape[0] // 2
    return pl.pallas_call(
        functools.partial(join_kernel, other),
        out_shape=jax.ShapeDtypeStruct((rows, p.shape[1]), jnp.float32),
        in_specs=[pl.BlockSpec(memory_space=pltpu.VMEM)] * 4,
        out_specs=pl.BlockSpec(memory_space=pltpu.VMEM),
        compiler_params=pltpu.CompilerParams(vmem_limit_bytes=SMALL_VMEM),
        cost_estimate=pl.CostEstimate(flops=8 * rows * outer.size, bytes_accessed=0, transcendentals=0),
        name="join_give" if other else "join_keep",
    )(p, t, outer, inner)


def sum_kernel(parts_ref, out_hbm, total, sem):
    total[...] = jnp.sum(parts_ref[...], axis=0)
    copy = pltpu.make_async_copy(total, out_hbm, sem)
    copy.start()
    copy.wait()


def sum_parts(parts):
    return pl.pallas_call(
        sum_kernel,
        out_shape=jax.ShapeDtypeStruct(parts.shape[1:], parts.dtype),
        in_specs=[pl.BlockSpec(memory_space=pltpu.VMEM)],
        out_specs=pl.BlockSpec(memory_space=pl.ANY),
        scratch_shapes=[pltpu.VMEM(parts.shape[1:], parts.dtype), pltpu.SemaphoreType.DMA],
        compiler_params=pltpu.CompilerParams(vmem_limit_bytes=SMALL_VMEM),
        name="sum_parts",
    )(parts)


def per_device(jac_blocks, modes, neighbours):
    width = jac_blocks.shape[1]
    rows, n_modes = modes.shape
    count = lax.axis_size("cell")
    keep_rows = n_modes // count
    across = [(i, min(max(i - 1 + 2 * (i % 2), 0), count - 1)) for i in range(count)]
    swap = [(i, i ^ 1) for i in range(count)]
    core = lax.rem(lax.axis_index("cell"), 2)
    outer_edge = lax.dynamic_slice_in_dim(modes, core * (rows - width), width)
    outer = lax.ppermute(gate(outer_edge), "cell", across)
    inner = lax.ppermute(inner_edge(modes, width), "cell", swap)
    p, t = own_part(neighbours.T, jac_blocks, modes, turn(modes, keep_rows))
    if keep_rows % TILE_ROWS:
        p = regrouped(p, 0, keep_rows)
        apart = jnp.swapaxes(t.reshape(2, 2, 2, n_modes // 2, width), 1, 2).reshape(2, 2, n_modes, width)
        apart = regrouped(apart, 2, keep_rows).reshape(2, 2, 2, n_modes // 2, width)
        t = jnp.swapaxes(apart, 1, 2).reshape(t.shape)
    got = lax.ppermute(join(True, p, t, outer, inner), "cell", swap)
    keep = join(False, p, t, outer, inner)
    pair = (keep + got).reshape(count // 2, keep_rows, n_modes)
    parts = lax.all_to_all(pair, "cell", 0, 0, axis_index_groups=teams(count))
    return sum_parts(parts)


def solution(mesh):
    placed = (P(("grp", "cell"), None, None), P(("grp", "cell"), None), P(("grp", "cell"), None))
    return jax.shard_map(
        per_device, mesh=mesh, in_specs=placed, out_specs=P(("grp", "cell"), None), check_vma=False
    )
```

```python
import functools

import jax
import jax.numpy as jnp
from jax import lax
from jax.experimental import pallas as pl
from jax.experimental.pallas import tpu as pltpu
from jax.sharding import PartitionSpec as P

OWN_VMEM = 24 * 2**20
SMALL_VMEM = 8 * 2**20
TILE_ROWS = 16
LOAD_COST = 35 * 10**8


def dot(a, b):
    return jnp.dot(a, b, preferred_element_type=jnp.float32)


def halves(value):
    upper = value.astype(jnp.bfloat16)
    return upper, (value - upper.astype(jnp.float32)).astype(jnp.bfloat16)


def gate_kernel(block_ref, out_ref):
    out_ref[...] = block_ref[...]


def gate(block):
    return pl.pallas_call(
        gate_kernel,
        out_shape=jax.ShapeDtypeStruct(block.shape, block.dtype),
        in_specs=[pl.BlockSpec(memory_space=pltpu.VMEM)],
        out_specs=pl.BlockSpec(memory_space=pltpu.VMEM),
        compiler_params=pltpu.CompilerParams(vmem_limit_bytes=SMALL_VMEM),
        cost_estimate=pl.CostEstimate(flops=LOAD_COST, bytes_accessed=0, transcendentals=0),
        name="gate",
    )(block)


def inner_kernel(modes, out_ref):
    width = out_ref.shape[0]
    head = modes[:width, :]
    tail = modes[modes.shape[0] - width :, :]
    out_ref[...] = jnp.where(lax.rem(lax.axis_index("cell"), 2) == 0, tail, head)


def inner_edge(modes, width):
    return pl.pallas_call(
        inner_kernel,
        out_shape=jax.ShapeDtypeStruct((width, modes.shape[1]), modes.dtype),
        in_specs=[pl.BlockSpec(memory_space=pltpu.VMEM)],
        out_specs=pl.BlockSpec(memory_space=pltpu.VMEM),
        compiler_params=pltpu.CompilerParams(vmem_limit_bytes=SMALL_VMEM),
        name="inner_edge",
    )(modes)


def turn_kernel(keep_rows, modes, out_ref):
    n_modes, count = out_ref.shape
    step = count // 4
    for start in range(0, count, step):
        columns = slice(start, start + step)
        block = modes[columns, :].T
        if keep_rows % TILE_ROWS:
            out_ref[:, columns] = block
        else:
            for place, k in enumerate(sum(teams(n_modes // keep_rows), [])):
                rows = slice(place * keep_rows, (place + 1) * keep_rows)
                out_ref[rows, columns] = block[k * keep_rows : (k + 1) * keep_rows]


def turn(modes, keep_rows):
    count, n_modes = modes.shape
    return pl.pallas_call(
        functools.partial(turn_kernel, keep_rows),
        out_shape=jax.ShapeDtypeStruct((n_modes, count), modes.dtype),
        in_specs=[pl.BlockSpec(memory_space=pltpu.VMEM)],
        out_specs=pl.BlockSpec(memory_space=pltpu.VMEM),
        compiler_params=pltpu.CompilerParams(vmem_limit_bytes=SMALL_VMEM),
        cost_estimate=pl.CostEstimate(flops=0, bytes_accessed=4 * modes.size, transcendentals=0),
        name="turn",
    )(modes)


def own_kernel(blocks, nb_ref, jac, modes, turned, p_ref, t_ref, left, parts, live):
    slots, width, _ = jac.shape
    n_modes = modes.shape[1]
    mid = n_modes // 2

    base = nb_ref[1, 0]
    count = jnp.int32(0)
    for s in range(blocks, slots):
        r = nb_ref[0, s]
        live[0, count] = s
        live[1, count] = r
        live[2, count] = nb_ref[1, s] - base + 1
        count += (r >= 0).astype(jnp.int32)
    live[0, count] = 0
    live[1, count] = 0
    live[2, count] = blocks + 2

    for s in range(blocks):
        left[s + 1] = dot(turned[:, s * width : (s + 1) * width], jac[s])
    left[0] = jnp.zeros((n_modes, width), jnp.float32)
    left[blocks + 1] = jnp.zeros((n_modes, width), jnp.float32)

    def pair(k, carry):
        for j in (2 * k, 2 * k + 1):
            columns = pl.ds(pl.multiple_of(live[1, j] * width, width), width)
            left[live[2, j]] += dot(turned[:, columns], jac[live[0, j]])
        return carry

    lax.fori_loop(0, (count + 1) // 2, pair, 0)

    both = jnp.zeros((2 * n_modes, n_modes), jnp.float32)
    step = 2 if blocks % 2 == 0 else 1
    for first in range(0, blocks, step):
        for c in range(first, first + step):
            upper, lower = halves(left[c + 1])
            parts[:n_modes, c * width : (c + 1) * width] = upper
            parts[n_modes:, c * width : (c + 1) * width] = lower
        inner = slice(first * width, (first + step) * width)
        both += dot(parts[:, inner], modes[inner, :])
    p_ref[...] = both[:n_modes] + both[n_modes:]
    for side, c in enumerate((0, blocks + 1)):
        upper, lower = halves(left[c])
        for half in range(2):
            t_ref[side, half, :mid] = upper[half * mid : (half + 1) * mid]
            t_ref[side, half, mid:] = lower[half * mid : (half + 1) * mid]


def own_part(neighbours, jac_blocks, modes, turned):
    slots, width, _ = jac_blocks.shape
    rows, n_modes = modes.shape
    blocks = rows // width
    flops = 2 * n_modes * width * width * slots + 4 * rows * n_modes * n_modes
    return pl.pallas_call(
        functools.partial(own_kernel, blocks),
        out_shape=(
            jax.ShapeDtypeStruct((n_modes, n_modes), jnp.float32),
            jax.ShapeDtypeStruct((2, 2, n_modes, width), jnp.bfloat16),
        ),
        in_specs=[
            pl.BlockSpec(memory_space=pltpu.SMEM),
            pl.BlockSpec(memory_space=pltpu.VMEM),
            pl.BlockSpec(memory_space=pltpu.VMEM),
            pl.BlockSpec(memory_space=pltpu.VMEM),
        ],
        out_specs=(pl.BlockSpec(memory_space=pltpu.VMEM), pl.BlockSpec(memory_space=pltpu.VMEM)),
        scratch_shapes=[
            pltpu.VMEM((blocks + 3, n_modes, width), jnp.float32),
            pltpu.VMEM((2 * n_modes, rows), jnp.bfloat16),
            pltpu.SMEM((3, slots + 1), jnp.int32),
        ],
        compiler_params=pltpu.CompilerParams(vmem_limit_bytes=OWN_VMEM),
        cost_estimate=pl.CostEstimate(
            flops=flops, bytes_accessed=slots * width * width * 2 + rows * n_modes * 2, transcendentals=0
        ),
        name="own_part",
    )(neighbours, jac_blocks, modes, turned)


def chip_order(chips):
    ring = [0, 2, 3, 1] + list(range(4, chips)) if chips >= 4 else list(range(chips))
    return ring[::-1]


def teams(count):
    return [[2 * chip + (chip + half) % 2 for chip in chip_order(count // 2)] for half in range(2)]


def own_team():
    me = lax.axis_index("cell")
    return lax.rem(me + me // 2, 2)


def regrouped(value, axis, keep_rows):
    first, second = teams(value.shape[axis] // keep_rows)
    starts = [k * keep_rows for k in first + second]
    return jnp.concatenate([lax.slice_in_dim(value, k, k + keep_rows, axis=axis) for k in starts], axis=axis)


def join_kernel(other, p_ref, t_ref, outer_ref, inner_ref, out_ref):
    core = lax.rem(lax.axis_index("cell"), 2)
    count = out_ref.shape[0]
    half = 1 - own_team() if other else own_team()
    rows = pl.ds(pl.multiple_of(half * count, TILE_ROWS), count)
    both = dot(t_ref[1 - core, half], inner_ref[...]) + dot(t_ref[core, half], outer_ref[...])
    out_ref[...] = p_ref[rows, :] + both[:count] + both[count:]


def join(other, p, t, outer, inner):
    rows = p.shape[0] // 2
    return pl.pallas_call(
        functools.partial(join_kernel, other),
        out_shape=jax.ShapeDtypeStruct((rows, p.shape[1]), jnp.float32),
        in_specs=[pl.BlockSpec(memory_space=pltpu.VMEM)] * 4,
        out_specs=pl.BlockSpec(memory_space=pltpu.VMEM),
        compiler_params=pltpu.CompilerParams(vmem_limit_bytes=SMALL_VMEM),
        cost_estimate=pl.CostEstimate(flops=8 * rows * outer.size, bytes_accessed=0, transcendentals=0),
        name="join_give" if other else "join_keep",
    )(p, t, outer, inner)


def sum_kernel(parts_ref, out_hbm, total, sem):
    total[...] = jnp.sum(parts_ref[...], axis=0)
    copy = pltpu.make_async_copy(total, out_hbm, sem)
    copy.start()
    copy.wait()


def sum_parts(parts):
    return pl.pallas_call(
        sum_kernel,
        out_shape=jax.ShapeDtypeStruct(parts.shape[1:], parts.dtype),
        in_specs=[pl.BlockSpec(memory_space=pltpu.VMEM)],
        out_specs=pl.BlockSpec(memory_space=pl.ANY),
        scratch_shapes=[pltpu.VMEM(parts.shape[1:], parts.dtype), pltpu.SemaphoreType.DMA],
        compiler_params=pltpu.CompilerParams(vmem_limit_bytes=SMALL_VMEM),
        name="sum_parts",
    )(parts)


def per_device(jac_blocks, modes, neighbours):
    width = jac_blocks.shape[1]
    rows, n_modes = modes.shape
    count = lax.axis_size("cell")
    keep_rows = n_modes // count
    across = [(i, min(max(i - 1 + 2 * (i % 2), 0), count - 1)) for i in range(count)]
    swap = [(i, i ^ 1) for i in range(count)]
    core = lax.rem(lax.axis_index("cell"), 2)
    outer_edge = lax.dynamic_slice_in_dim(modes, core * (rows - width), width)
    outer = lax.ppermute(gate(outer_edge), "cell", across)
    inner = lax.ppermute(inner_edge(modes, width), "cell", swap)
    p, t = own_part(neighbours.T, jac_blocks, modes, turn(modes, keep_rows))
    if keep_rows % TILE_ROWS:
        p = regrouped(p, 0, keep_rows)
        apart = jnp.swapaxes(t.reshape(2, 2, 2, n_modes // 2, width), 1, 2).reshape(2, 2, n_modes, width)
        apart = regrouped(apart, 2, keep_rows).reshape(2, 2, 2, n_modes // 2, width)
        t = jnp.swapaxes(apart, 1, 2).reshape(t.shape)
    got = lax.ppermute(join(True, p, t, outer, inner), "cell", swap)
    keep = join(False, p, t, outer, inner)
    pair = (keep + got).reshape(count // 2, keep_rows, n_modes)
    parts = lax.all_to_all(pair, "cell", 0, 0, axis_index_groups=teams(count))
    return sum_parts(parts)


def solution(mesh):
    placed = (P(("grp", "cell"), None, None), P(("grp", "cell"), None), P(("grp", "cell"), None))
    return jax.shard_map(
        per_device, mesh=mesh, in_specs=placed, out_specs=P(("grp", "cell"), None), check_vma=False
    )
```

```python
import functools

import jax
import jax.numpy as jnp
from jax import lax
from jax.experimental import pallas as pl
from jax.experimental.pallas import tpu as pltpu
from jax.sharding import PartitionSpec as P

OWN_VMEM = 24 * 2**20
SMALL_VMEM = 8 * 2**20
TILE_ROWS = 16
LOAD_COST = 35 * 10**8


def dot(a, b):
    return jnp.dot(a, b, preferred_element_type=jnp.float32)


def halves(value):
    upper = value.astype(jnp.bfloat16)
    return upper, (value - upper.astype(jnp.float32)).astype(jnp.bfloat16)


def gate_kernel(block_ref, out_ref):
    out_ref[...] = block_ref[...]


def gate(block):
    return pl.pallas_call(
        gate_kernel,
        out_shape=jax.ShapeDtypeStruct(block.shape, block.dtype),
        in_specs=[pl.BlockSpec(memory_space=pltpu.VMEM)],
        out_specs=pl.BlockSpec(memory_space=pltpu.VMEM),
        compiler_params=pltpu.CompilerParams(vmem_limit_bytes=SMALL_VMEM),
        cost_estimate=pl.CostEstimate(flops=LOAD_COST, bytes_accessed=0, transcendentals=0),
        name="gate",
    )(block)


def inner_kernel(modes, out_ref):
    width = out_ref.shape[0]
    head = modes[:width, :]
    tail = modes[modes.shape[0] - width :, :]
    out_ref[...] = jnp.where(lax.rem(lax.axis_index("cell"), 2) == 0, tail, head)


def inner_edge(modes, width):
    return pl.pallas_call(
        inner_kernel,
        out_shape=jax.ShapeDtypeStruct((width, modes.shape[1]), modes.dtype),
        in_specs=[pl.BlockSpec(memory_space=pltpu.VMEM)],
        out_specs=pl.BlockSpec(memory_space=pltpu.VMEM),
        compiler_params=pltpu.CompilerParams(vmem_limit_bytes=SMALL_VMEM),
        name="inner_edge",
    )(modes)


def turn_kernel(keep_rows, modes, out_ref):
    n_modes, count = out_ref.shape
    step = count // 4
    for start in range(0, count, step):
        columns = slice(start, start + step)
        block = modes[columns, :].T
        if keep_rows % TILE_ROWS:
            out_ref[:, columns] = block
        else:
            for place, k in enumerate(sum(teams(n_modes // keep_rows), [])):
                rows = slice(place * keep_rows, (place + 1) * keep_rows)
                out_ref[rows, columns] = block[k * keep_rows : (k + 1) * keep_rows]


def turn(modes, keep_rows):
    count, n_modes = modes.shape
    return pl.pallas_call(
        functools.partial(turn_kernel, keep_rows),
        out_shape=jax.ShapeDtypeStruct((n_modes, count), modes.dtype),
        in_specs=[pl.BlockSpec(memory_space=pltpu.VMEM)],
        out_specs=pl.BlockSpec(memory_space=pltpu.VMEM),
        compiler_params=pltpu.CompilerParams(vmem_limit_bytes=SMALL_VMEM),
        cost_estimate=pl.CostEstimate(flops=0, bytes_accessed=4 * modes.size, transcendentals=0),
        name="turn",
    )(modes)


def own_kernel(blocks, nb_ref, jac, modes, turned, p_ref, t_ref, left, parts, live):
    slots, width, _ = jac.shape
    n_modes = modes.shape[1]
    mid = n_modes // 2

    base = nb_ref[1, 0]
    count = jnp.int32(0)
    for s in range(blocks, slots):
        r = nb_ref[0, s]
        live[0, count] = s
        live[1, count] = r
        live[2, count] = nb_ref[1, s] - base + 1
        count += (r >= 0).astype(jnp.int32)
    live[0, count] = 0
    live[1, count] = 0
    live[2, count] = blocks + 2

    for s in range(blocks):
        left[s + 1] = dot(turned[:, s * width : (s + 1) * width], jac[s])
    left[0] = jnp.zeros((n_modes, width), jnp.float32)
    left[blocks + 1] = jnp.zeros((n_modes, width), jnp.float32)

    def pair(k, carry):
        for j in (2 * k, 2 * k + 1):
            columns = pl.ds(pl.multiple_of(live[1, j] * width, width), width)
            left[live[2, j]] += dot(turned[:, columns], jac[live[0, j]])
        return carry

    lax.fori_loop(0, (count + 1) // 2, pair, 0)

    both = jnp.zeros((2 * n_modes, n_modes), jnp.float32)
    step = 2 if blocks % 2 == 0 else 1
    for first in range(0, blocks, step):
        for c in range(first, first + step):
            upper, lower = halves(left[c + 1])
            parts[:n_modes, c * width : (c + 1) * width] = upper
            parts[n_modes:, c * width : (c + 1) * width] = lower
        inner = slice(first * width, (first + step) * width)
        both += dot(parts[:, inner], modes[inner, :])
    p_ref[...] = both[:n_modes] + both[n_modes:]
    for side, c in enumerate((0, blocks + 1)):
        upper, lower = halves(left[c])
        for half in range(2):
            t_ref[side, half, :mid] = upper[half * mid : (half + 1) * mid]
            t_ref[side, half, mid:] = lower[half * mid : (half + 1) * mid]


def own_part(neighbours, jac_blocks, modes, turned):
    slots, width, _ = jac_blocks.shape
    rows, n_modes = modes.shape
    blocks = rows // width
    flops = 2 * n_modes * width * width * slots + 4 * rows * n_modes * n_modes
    return pl.pallas_call(
        functools.partial(own_kernel, blocks),
        out_shape=(
            jax.ShapeDtypeStruct((n_modes, n_modes), jnp.float32),
            jax.ShapeDtypeStruct((2, 2, n_modes, width), jnp.bfloat16),
        ),
        in_specs=[
            pl.BlockSpec(memory_space=pltpu.SMEM),
            pl.BlockSpec(memory_space=pltpu.VMEM),
            pl.BlockSpec(memory_space=pltpu.VMEM),
            pl.BlockSpec(memory_space=pltpu.VMEM),
        ],
        out_specs=(pl.BlockSpec(memory_space=pltpu.VMEM), pl.BlockSpec(memory_space=pltpu.VMEM)),
        scratch_shapes=[
            pltpu.VMEM((blocks + 3, n_modes, width), jnp.float32),
            pltpu.VMEM((2 * n_modes, rows), jnp.bfloat16),
            pltpu.SMEM((3, slots + 1), jnp.int32),
        ],
        compiler_params=pltpu.CompilerParams(vmem_limit_bytes=OWN_VMEM),
        cost_estimate=pl.CostEstimate(
            flops=flops, bytes_accessed=slots * width * width * 2 + rows * n_modes * 2, transcendentals=0
        ),
        name="own_part",
    )(neighbours, jac_blocks, modes, turned)


def chip_order(chips):
    far = 5 * chips // 8
    return ([0, far] + [chip for chip in range(1, chips) if chip != far] if far else [0])[::-1]


def teams(count):
    return [[2 * chip + (chip + half) % 2 for chip in chip_order(count // 2)] for half in range(2)]


def own_team():
    me = lax.axis_index("cell")
    return lax.rem(me + me // 2, 2)


def regrouped(value, axis, keep_rows):
    first, second = teams(value.shape[axis] // keep_rows)
    starts = [k * keep_rows for k in first + second]
    return jnp.concatenate([lax.slice_in_dim(value, k, k + keep_rows, axis=axis) for k in starts], axis=axis)


def join_kernel(other, p_ref, t_ref, outer_ref, inner_ref, out_ref):
    core = lax.rem(lax.axis_index("cell"), 2)
    count = out_ref.shape[0]
    half = 1 - own_team() if other else own_team()
    rows = pl.ds(pl.multiple_of(half * count, TILE_ROWS), count)
    both = dot(t_ref[1 - core, half], inner_ref[...]) + dot(t_ref[core, half], outer_ref[...])
    out_ref[...] = p_ref[rows, :] + both[:count] + both[count:]


def join(other, p, t, outer, inner):
    rows = p.shape[0] // 2
    return pl.pallas_call(
        functools.partial(join_kernel, other),
        out_shape=jax.ShapeDtypeStruct((rows, p.shape[1]), jnp.float32),
        in_specs=[pl.BlockSpec(memory_space=pltpu.VMEM)] * 4,
        out_specs=pl.BlockSpec(memory_space=pltpu.VMEM),
        compiler_params=pltpu.CompilerParams(vmem_limit_bytes=SMALL_VMEM),
        cost_estimate=pl.CostEstimate(flops=8 * rows * outer.size, bytes_accessed=0, transcendentals=0),
        name="join_give" if other else "join_keep",
    )(p, t, outer, inner)


def sum_kernel(parts_ref, out_hbm, total, sem):
    total[...] = jnp.sum(parts_ref[...], axis=0)
    copy = pltpu.make_async_copy(total, out_hbm, sem)
    copy.start()
    copy.wait()


def sum_parts(parts):
    return pl.pallas_call(
        sum_kernel,
        out_shape=jax.ShapeDtypeStruct(parts.shape[1:], parts.dtype),
        in_specs=[pl.BlockSpec(memory_space=pltpu.VMEM)],
        out_specs=pl.BlockSpec(memory_space=pl.ANY),
        scratch_shapes=[pltpu.VMEM(parts.shape[1:], parts.dtype), pltpu.SemaphoreType.DMA],
        compiler_params=pltpu.CompilerParams(vmem_limit_bytes=SMALL_VMEM),
        name="sum_parts",
    )(parts)


def per_device(jac_blocks, modes, neighbours):
    width = jac_blocks.shape[1]
    rows, n_modes = modes.shape
    count = lax.axis_size("cell")
    keep_rows = n_modes // count
    across = [(i, min(max(i - 1 + 2 * (i % 2), 0), count - 1)) for i in range(count)]
    swap = [(i, i ^ 1) for i in range(count)]
    core = lax.rem(lax.axis_index("cell"), 2)
    outer_edge = lax.dynamic_slice_in_dim(modes, core * (rows - width), width)
    outer = lax.ppermute(gate(outer_edge), "cell", across)
    inner = lax.ppermute(inner_edge(modes, width), "cell", swap)
    p, t = own_part(neighbours.T, jac_blocks, modes, turn(modes, keep_rows))
    if keep_rows % TILE_ROWS:
        p = regrouped(p, 0, keep_rows)
        apart = jnp.swapaxes(t.reshape(2, 2, 2, n_modes // 2, width), 1, 2).reshape(2, 2, n_modes, width)
        apart = regrouped(apart, 2, keep_rows).reshape(2, 2, 2, n_modes // 2, width)
        t = jnp.swapaxes(apart, 1, 2).reshape(t.shape)
    got = lax.ppermute(join(True, p, t, outer, inner), "cell", swap)
    keep = join(False, p, t, outer, inner)
    pair = (keep + got).reshape(count // 2, keep_rows, n_modes)
    parts = lax.all_to_all(pair, "cell", 0, 0, axis_index_groups=teams(count))
    return sum_parts(parts)


def solution(mesh):
    placed = (P(("grp", "cell"), None, None), P(("grp", "cell"), None), P(("grp", "cell"), None))
    return jax.shard_map(
        per_device, mesh=mesh, in_specs=placed, out_specs=P(("grp", "cell"), None), check_vma=False
    )
```

```python
import functools

import jax
import jax.numpy as jnp
from jax import lax
from jax.experimental import pallas as pl
from jax.experimental.pallas import tpu as pltpu
from jax.sharding import PartitionSpec as P

OWN_VMEM = 24 * 2**20
SMALL_VMEM = 8 * 2**20
TILE_ROWS = 16
LOAD_COST = 35 * 10**8


def dot(a, b):
    return jnp.dot(a, b, preferred_element_type=jnp.float32)


def halves(value):
    upper = value.astype(jnp.bfloat16)
    return upper, (value - upper.astype(jnp.float32)).astype(jnp.bfloat16)


def gate_kernel(block_ref, out_ref):
    out_ref[...] = block_ref[...]


def gate(block):
    return pl.pallas_call(
        gate_kernel,
        out_shape=jax.ShapeDtypeStruct(block.shape, block.dtype),
        in_specs=[pl.BlockSpec(memory_space=pltpu.VMEM)],
        out_specs=pl.BlockSpec(memory_space=pltpu.VMEM),
        compiler_params=pltpu.CompilerParams(vmem_limit_bytes=SMALL_VMEM),
        cost_estimate=pl.CostEstimate(flops=LOAD_COST, bytes_accessed=0, transcendentals=0),
        name="gate",
    )(block)


def inner_kernel(modes, out_ref):
    width = out_ref.shape[0]
    head = modes[:width, :]
    tail = modes[modes.shape[0] - width :, :]
    out_ref[...] = jnp.where(lax.rem(lax.axis_index("cell"), 2) == 0, tail, head)


def inner_edge(modes, width):
    return pl.pallas_call(
        inner_kernel,
        out_shape=jax.ShapeDtypeStruct((width, modes.shape[1]), modes.dtype),
        in_specs=[pl.BlockSpec(memory_space=pltpu.VMEM)],
        out_specs=pl.BlockSpec(memory_space=pltpu.VMEM),
        compiler_params=pltpu.CompilerParams(vmem_limit_bytes=SMALL_VMEM),
        name="inner_edge",
    )(modes)


def turn_kernel(keep_rows, modes, out_ref):
    n_modes, count = out_ref.shape
    step = count // 4
    for start in range(0, count, step):
        columns = slice(start, start + step)
        block = modes[columns, :].T
        if keep_rows % TILE_ROWS:
            out_ref[:, columns] = block
        else:
            for place, k in enumerate(sum(teams(n_modes // keep_rows), [])):
                rows = slice(place * keep_rows, (place + 1) * keep_rows)
                out_ref[rows, columns] = block[k * keep_rows : (k + 1) * keep_rows]


def turn(modes, keep_rows):
    count, n_modes = modes.shape
    return pl.pallas_call(
        functools.partial(turn_kernel, keep_rows),
        out_shape=jax.ShapeDtypeStruct((n_modes, count), modes.dtype),
        in_specs=[pl.BlockSpec(memory_space=pltpu.VMEM)],
        out_specs=pl.BlockSpec(memory_space=pltpu.VMEM),
        compiler_params=pltpu.CompilerParams(vmem_limit_bytes=SMALL_VMEM),
        cost_estimate=pl.CostEstimate(flops=0, bytes_accessed=4 * modes.size, transcendentals=0),
        name="turn",
    )(modes)


def own_kernel(blocks, nb_ref, jac, modes, turned, p_ref, t_ref, left, parts, live):
    slots, width, _ = jac.shape
    n_modes = modes.shape[1]
    mid = n_modes // 2

    base = nb_ref[1, 0]
    count = jnp.int32(0)
    for s in range(blocks, slots):
        r = nb_ref[0, s]
        live[0, count] = s
        live[1, count] = r
        live[2, count] = nb_ref[1, s] - base + 1
        count += (r >= 0).astype(jnp.int32)
    live[0, count] = 0
    live[1, count] = 0
    live[2, count] = blocks + 2

    for s in range(blocks):
        left[s + 1] = dot(turned[:, s * width : (s + 1) * width], jac[s])
    left[0] = jnp.zeros((n_modes, width), jnp.float32)
    left[blocks + 1] = jnp.zeros((n_modes, width), jnp.float32)

    def pair(k, carry):
        for j in (2 * k, 2 * k + 1):
            columns = pl.ds(pl.multiple_of(live[1, j] * width, width), width)
            left[live[2, j]] += dot(turned[:, columns], jac[live[0, j]])
        return carry

    lax.fori_loop(0, (count + 1) // 2, pair, 0)

    both = jnp.zeros((2 * n_modes, n_modes), jnp.float32)
    step = 2 if blocks % 2 == 0 else 1
    for first in range(0, blocks, step):
        for c in range(first, first + step):
            upper, lower = halves(left[c + 1])
            parts[:n_modes, c * width : (c + 1) * width] = upper
            parts[n_modes:, c * width : (c + 1) * width] = lower
        inner = slice(first * width, (first + step) * width)
        both += dot(parts[:, inner], modes[inner, :])
    p_ref[...] = both[:n_modes] + both[n_modes:]
    for side, c in enumerate((0, blocks + 1)):
        upper, lower = halves(left[c])
        for half in range(2):
            t_ref[side, half, :mid] = upper[half * mid : (half + 1) * mid]
            t_ref[side, half, mid:] = lower[half * mid : (half + 1) * mid]


def own_part(neighbours, jac_blocks, modes, turned):
    slots, width, _ = jac_blocks.shape
    rows, n_modes = modes.shape
    blocks = rows // width
    flops = 2 * n_modes * width * width * slots + 4 * rows * n_modes * n_modes
    return pl.pallas_call(
        functools.partial(own_kernel, blocks),
        out_shape=(
            jax.ShapeDtypeStruct((n_modes, n_modes), jnp.float32),
            jax.ShapeDtypeStruct((2, 2, n_modes, width), jnp.bfloat16),
        ),
        in_specs=[
            pl.BlockSpec(memory_space=pltpu.SMEM),
            pl.BlockSpec(memory_space=pltpu.VMEM),
            pl.BlockSpec(memory_space=pltpu.VMEM),
            pl.BlockSpec(memory_space=pltpu.VMEM),
        ],
        out_specs=(pl.BlockSpec(memory_space=pltpu.VMEM), pl.BlockSpec(memory_space=pltpu.VMEM)),
        scratch_shapes=[
            pltpu.VMEM((blocks + 3, n_modes, width), jnp.float32),
            pltpu.VMEM((2 * n_modes, rows), jnp.bfloat16),
            pltpu.SMEM((3, slots + 1), jnp.int32),
        ],
        compiler_params=pltpu.CompilerParams(vmem_limit_bytes=OWN_VMEM),
        cost_estimate=pl.CostEstimate(
            flops=flops, bytes_accessed=slots * width * width * 2 + rows * n_modes * 2, transcendentals=0
        ),
        name="own_part",
    )(neighbours, jac_blocks, modes, turned)


def teams(count):
    chips = list(range(count // 2))
    mid = count // 4
    rings = [chips, [mid] + chips[:mid] + chips[mid + 1 :]]
    return [[2 * chip + (chip + half) % 2 for chip in reversed(rings[half])] for half in range(2)]


def own_team():
    me = lax.axis_index("cell")
    return lax.rem(me + me // 2, 2)


def regrouped(value, axis, keep_rows):
    first, second = teams(value.shape[axis] // keep_rows)
    starts = [k * keep_rows for k in first + second]
    return jnp.concatenate([lax.slice_in_dim(value, k, k + keep_rows, axis=axis) for k in starts], axis=axis)


def join_kernel(other, p_ref, t_ref, outer_ref, inner_ref, out_ref):
    core = lax.rem(lax.axis_index("cell"), 2)
    count = out_ref.shape[0]
    half = 1 - own_team() if other else own_team()
    rows = pl.ds(pl.multiple_of(half * count, TILE_ROWS), count)
    both = dot(t_ref[1 - core, half], inner_ref[...]) + dot(t_ref[core, half], outer_ref[...])
    out_ref[...] = p_ref[rows, :] + both[:count] + both[count:]


def join(other, p, t, outer, inner):
    rows = p.shape[0] // 2
    return pl.pallas_call(
        functools.partial(join_kernel, other),
        out_shape=jax.ShapeDtypeStruct((rows, p.shape[1]), jnp.float32),
        in_specs=[pl.BlockSpec(memory_space=pltpu.VMEM)] * 4,
        out_specs=pl.BlockSpec(memory_space=pltpu.VMEM),
        compiler_params=pltpu.CompilerParams(vmem_limit_bytes=SMALL_VMEM),
        cost_estimate=pl.CostEstimate(flops=8 * rows * outer.size, bytes_accessed=0, transcendentals=0),
        name="join_give" if other else "join_keep",
    )(p, t, outer, inner)


def sum_kernel(parts_ref, out_hbm, total, sem):
    total[...] = jnp.sum(parts_ref[...], axis=0)
    copy = pltpu.make_async_copy(total, out_hbm, sem)
    copy.start()
    copy.wait()


def sum_parts(parts):
    return pl.pallas_call(
        sum_kernel,
        out_shape=jax.ShapeDtypeStruct(parts.shape[1:], parts.dtype),
        in_specs=[pl.BlockSpec(memory_space=pltpu.VMEM)],
        out_specs=pl.BlockSpec(memory_space=pl.ANY),
        scratch_shapes=[pltpu.VMEM(parts.shape[1:], parts.dtype), pltpu.SemaphoreType.DMA],
        compiler_params=pltpu.CompilerParams(vmem_limit_bytes=SMALL_VMEM),
        name="sum_parts",
    )(parts)


def per_device(jac_blocks, modes, neighbours):
    width = jac_blocks.shape[1]
    rows, n_modes = modes.shape
    count = lax.axis_size("cell")
    keep_rows = n_modes // count
    across = [(i, min(max(i - 1 + 2 * (i % 2), 0), count - 1)) for i in range(count)]
    swap = [(i, i ^ 1) for i in range(count)]
    core = lax.rem(lax.axis_index("cell"), 2)
    outer_edge = lax.dynamic_slice_in_dim(modes, core * (rows - width), width)
    outer = lax.ppermute(gate(outer_edge), "cell", across)
    inner = lax.ppermute(inner_edge(modes, width), "cell", swap)
    p, t = own_part(neighbours.T, jac_blocks, modes, turn(modes, keep_rows))
    if keep_rows % TILE_ROWS:
        p = regrouped(p, 0, keep_rows)
        apart = jnp.swapaxes(t.reshape(2, 2, 2, n_modes // 2, width), 1, 2).reshape(2, 2, n_modes, width)
        apart = regrouped(apart, 2, keep_rows).reshape(2, 2, 2, n_modes // 2, width)
        t = jnp.swapaxes(apart, 1, 2).reshape(t.shape)
    got = lax.ppermute(join(True, p, t, outer, inner), "cell", swap)
    keep = join(False, p, t, outer, inner)
    pair = (keep + got).reshape(count // 2, keep_rows, n_modes)
    parts = lax.all_to_all(pair, "cell", 0, 0, axis_index_groups=teams(count))
    return sum_parts(parts)


def solution(mesh):
    placed = (P(("grp", "cell"), None, None), P(("grp", "cell"), None), P(("grp", "cell"), None))
    return jax.shard_map(
        per_device, mesh=mesh, in_specs=placed, out_specs=P(("grp", "cell"), None), check_vma=False
    )
```

```python
import functools

import jax
import jax.numpy as jnp
from jax import lax
from jax.experimental import pallas as pl
from jax.experimental.pallas import tpu as pltpu
from jax.sharding import PartitionSpec as P

OWN_VMEM = 24 * 2**20
SMALL_VMEM = 8 * 2**20
TILE_ROWS = 16
LOAD_COST = 35 * 10**8


def dot(a, b):
    return jnp.dot(a, b, preferred_element_type=jnp.float32)


def halves(value):
    upper = value.astype(jnp.bfloat16)
    return upper, (value - upper.astype(jnp.float32)).astype(jnp.bfloat16)


def gate_kernel(block_ref, out_ref):
    out_ref[...] = block_ref[...]


def gate(block):
    return pl.pallas_call(
        gate_kernel,
        out_shape=jax.ShapeDtypeStruct(block.shape, block.dtype),
        in_specs=[pl.BlockSpec(memory_space=pltpu.VMEM)],
        out_specs=pl.BlockSpec(memory_space=pltpu.VMEM),
        compiler_params=pltpu.CompilerParams(vmem_limit_bytes=SMALL_VMEM),
        cost_estimate=pl.CostEstimate(flops=LOAD_COST, bytes_accessed=0, transcendentals=0),
        name="gate",
    )(block)


def inner_kernel(modes, out_ref):
    width = out_ref.shape[0]
    head = modes[:width, :]
    tail = modes[modes.shape[0] - width :, :]
    out_ref[...] = jnp.where(lax.rem(lax.axis_index("cell"), 2) == 0, tail, head)


def inner_edge(modes, width):
    return pl.pallas_call(
        inner_kernel,
        out_shape=jax.ShapeDtypeStruct((width, modes.shape[1]), modes.dtype),
        in_specs=[pl.BlockSpec(memory_space=pltpu.VMEM)],
        out_specs=pl.BlockSpec(memory_space=pltpu.VMEM),
        compiler_params=pltpu.CompilerParams(vmem_limit_bytes=SMALL_VMEM),
        name="inner_edge",
    )(modes)


def turn_kernel(keep_rows, modes, out_ref):
    n_modes, count = out_ref.shape
    step = count // 4
    for start in range(0, count, step):
        columns = slice(start, start + step)
        block = modes[columns, :].T
        if keep_rows % TILE_ROWS:
            out_ref[:, columns] = block
        else:
            for place, k in enumerate(sum(teams(n_modes // keep_rows), [])):
                rows = slice(place * keep_rows, (place + 1) * keep_rows)
                out_ref[rows, columns] = block[k * keep_rows : (k + 1) * keep_rows]


def turn(modes, keep_rows):
    count, n_modes = modes.shape
    return pl.pallas_call(
        functools.partial(turn_kernel, keep_rows),
        out_shape=jax.ShapeDtypeStruct((n_modes, count), modes.dtype),
        in_specs=[pl.BlockSpec(memory_space=pltpu.VMEM)],
        out_specs=pl.BlockSpec(memory_space=pltpu.VMEM),
        compiler_params=pltpu.CompilerParams(vmem_limit_bytes=SMALL_VMEM),
        cost_estimate=pl.CostEstimate(flops=0, bytes_accessed=4 * modes.size, transcendentals=0),
        name="turn",
    )(modes)


def own_kernel(blocks, nb_ref, jac, modes, turned, p_ref, t_ref, left, parts, live):
    slots, width, _ = jac.shape
    n_modes = modes.shape[1]
    mid = n_modes // 2

    base = nb_ref[1, 0]
    count = jnp.int32(0)
    for s in range(blocks, slots):
        r = nb_ref[0, s]
        live[0, count] = s
        live[1, count] = r
        live[2, count] = nb_ref[1, s] - base + 1
        count += (r >= 0).astype(jnp.int32)
    live[0, count] = 0
    live[1, count] = 0
    live[2, count] = blocks + 2

    for s in range(blocks):
        left[s + 1] = dot(turned[:, s * width : (s + 1) * width], jac[s])
    left[0] = jnp.zeros((n_modes, width), jnp.float32)
    left[blocks + 1] = jnp.zeros((n_modes, width), jnp.float32)

    def pair(k, carry):
        for j in (2 * k, 2 * k + 1):
            columns = pl.ds(pl.multiple_of(live[1, j] * width, width), width)
            left[live[2, j]] += dot(turned[:, columns], jac[live[0, j]])
        return carry

    lax.fori_loop(0, (count + 1) // 2, pair, 0)

    both = jnp.zeros((2 * n_modes, n_modes), jnp.float32)
    step = 2 if blocks % 2 == 0 else 1
    for first in range(0, blocks, step):
        for c in range(first, first + step):
            upper, lower = halves(left[c + 1])
            parts[:n_modes, c * width : (c + 1) * width] = upper
            parts[n_modes:, c * width : (c + 1) * width] = lower
        inner = slice(first * width, (first + step) * width)
        both += dot(parts[:, inner], modes[inner, :])
    p_ref[...] = both[:n_modes] + both[n_modes:]
    for side, c in enumerate((0, blocks + 1)):
        upper, lower = halves(left[c])
        for half in range(2):
            t_ref[side, half, :mid] = upper[half * mid : (half + 1) * mid]
            t_ref[side, half, mid:] = lower[half * mid : (half + 1) * mid]


def own_part(neighbours, jac_blocks, modes, turned):
    slots, width, _ = jac_blocks.shape
    rows, n_modes = modes.shape
    blocks = rows // width
    flops = 2 * n_modes * width * width * slots + 4 * rows * n_modes * n_modes
    return pl.pallas_call(
        functools.partial(own_kernel, blocks),
        out_shape=(
            jax.ShapeDtypeStruct((n_modes, n_modes), jnp.float32),
            jax.ShapeDtypeStruct((2, 2, n_modes, width), jnp.bfloat16),
        ),
        in_specs=[
            pl.BlockSpec(memory_space=pltpu.SMEM),
            pl.BlockSpec(memory_space=pltpu.VMEM),
            pl.BlockSpec(memory_space=pltpu.VMEM),
            pl.BlockSpec(memory_space=pltpu.VMEM),
        ],
        out_specs=(pl.BlockSpec(memory_space=pltpu.VMEM), pl.BlockSpec(memory_space=pltpu.VMEM)),
        scratch_shapes=[
            pltpu.VMEM((blocks + 3, n_modes, width), jnp.float32),
            pltpu.VMEM((2 * n_modes, rows), jnp.bfloat16),
            pltpu.SMEM((3, slots + 1), jnp.int32),
        ],
        compiler_params=pltpu.CompilerParams(vmem_limit_bytes=OWN_VMEM),
        cost_estimate=pl.CostEstimate(
            flops=flops, bytes_accessed=slots * width * width * 2 + rows * n_modes * 2, transcendentals=0
        ),
        name="own_part",
    )(neighbours, jac_blocks, modes, turned)


def teams(count):
    chips = range(count // 2)
    middle = [chip for chip in (count // 4, count // 4 + 1) if 0 < chip < count // 2]
    rest = [chip for chip in chips if chip not in middle]
    rings = [middle[::-1] + rest, middle + rest]
    return [[2 * chip + (chip + half) % 2 for chip in reversed(rings[half])] for half in range(2)]


def own_team():
    me = lax.axis_index("cell")
    return lax.rem(me + me // 2, 2)


def regrouped(value, axis, keep_rows):
    first, second = teams(value.shape[axis] // keep_rows)
    starts = [k * keep_rows for k in first + second]
    return jnp.concatenate([lax.slice_in_dim(value, k, k + keep_rows, axis=axis) for k in starts], axis=axis)


def join_kernel(other, p_ref, t_ref, outer_ref, inner_ref, out_ref):
    core = lax.rem(lax.axis_index("cell"), 2)
    count = out_ref.shape[0]
    half = 1 - own_team() if other else own_team()
    rows = pl.ds(pl.multiple_of(half * count, TILE_ROWS), count)
    both = dot(t_ref[1 - core, half], inner_ref[...]) + dot(t_ref[core, half], outer_ref[...])
    out_ref[...] = p_ref[rows, :] + both[:count] + both[count:]


def join(other, p, t, outer, inner):
    rows = p.shape[0] // 2
    return pl.pallas_call(
        functools.partial(join_kernel, other),
        out_shape=jax.ShapeDtypeStruct((rows, p.shape[1]), jnp.float32),
        in_specs=[pl.BlockSpec(memory_space=pltpu.VMEM)] * 4,
        out_specs=pl.BlockSpec(memory_space=pltpu.VMEM),
        compiler_params=pltpu.CompilerParams(vmem_limit_bytes=SMALL_VMEM),
        cost_estimate=pl.CostEstimate(flops=8 * rows * outer.size, bytes_accessed=0, transcendentals=0),
        name="join_give" if other else "join_keep",
    )(p, t, outer, inner)


def sum_kernel(parts_ref, out_hbm, total, sem):
    total[...] = jnp.sum(parts_ref[...], axis=0)
    copy = pltpu.make_async_copy(total, out_hbm, sem)
    copy.start()
    copy.wait()


def sum_parts(parts):
    return pl.pallas_call(
        sum_kernel,
        out_shape=jax.ShapeDtypeStruct(parts.shape[1:], parts.dtype),
        in_specs=[pl.BlockSpec(memory_space=pltpu.VMEM)],
        out_specs=pl.BlockSpec(memory_space=pl.ANY),
        scratch_shapes=[pltpu.VMEM(parts.shape[1:], parts.dtype), pltpu.SemaphoreType.DMA],
        compiler_params=pltpu.CompilerParams(vmem_limit_bytes=SMALL_VMEM),
        name="sum_parts",
    )(parts)


def per_device(jac_blocks, modes, neighbours):
    width = jac_blocks.shape[1]
    rows, n_modes = modes.shape
    count = lax.axis_size("cell")
    keep_rows = n_modes // count
    across = [(i, min(max(i - 1 + 2 * (i % 2), 0), count - 1)) for i in range(count)]
    swap = [(i, i ^ 1) for i in range(count)]
    core = lax.rem(lax.axis_index("cell"), 2)
    outer_edge = lax.dynamic_slice_in_dim(modes, core * (rows - width), width)
    outer = lax.ppermute(gate(outer_edge), "cell", across)
    inner = lax.ppermute(inner_edge(modes, width), "cell", swap)
    p, t = own_part(neighbours.T, jac_blocks, modes, turn(modes, keep_rows))
    if keep_rows % TILE_ROWS:
        p = regrouped(p, 0, keep_rows)
        apart = jnp.swapaxes(t.reshape(2, 2, 2, n_modes // 2, width), 1, 2).reshape(2, 2, n_modes, width)
        apart = regrouped(apart, 2, keep_rows).reshape(2, 2, 2, n_modes // 2, width)
        t = jnp.swapaxes(apart, 1, 2).reshape(t.shape)
    got = lax.ppermute(join(True, p, t, outer, inner), "cell", swap)
    keep = join(False, p, t, outer, inner)
    pair = (keep + got).reshape(count // 2, keep_rows, n_modes)
    parts = lax.all_to_all(pair, "cell", 0, 0, axis_index_groups=teams(count))
    return sum_parts(parts)


def solution(mesh):
    placed = (P(("grp", "cell"), None, None), P(("grp", "cell"), None), P(("grp", "cell"), None))
    return jax.shard_map(
        per_device, mesh=mesh, in_specs=placed, out_specs=P(("grp", "cell"), None), check_vma=False
    )
```

```python
import functools

import jax
import jax.numpy as jnp
from jax import lax
from jax.experimental import pallas as pl
from jax.experimental.pallas import tpu as pltpu
from jax.sharding import PartitionSpec as P

OWN_VMEM = 24 * 2**20
SMALL_VMEM = 8 * 2**20
TILE_ROWS = 16
LOAD_COST = 35 * 10**8


def dot(a, b):
    return jnp.dot(a, b, preferred_element_type=jnp.float32)


def halves(value):
    upper = value.astype(jnp.bfloat16)
    return upper, (value - upper.astype(jnp.float32)).astype(jnp.bfloat16)


def gate_kernel(block_ref, out_ref):
    out_ref[...] = block_ref[...]


def gate(block):
    return pl.pallas_call(
        gate_kernel,
        out_shape=jax.ShapeDtypeStruct(block.shape, block.dtype),
        in_specs=[pl.BlockSpec(memory_space=pltpu.VMEM)],
        out_specs=pl.BlockSpec(memory_space=pltpu.VMEM),
        compiler_params=pltpu.CompilerParams(vmem_limit_bytes=SMALL_VMEM),
        cost_estimate=pl.CostEstimate(flops=LOAD_COST, bytes_accessed=0, transcendentals=0),
        name="gate",
    )(block)


def inner_kernel(modes, out_ref):
    width = out_ref.shape[0]
    head = modes[:width, :]
    tail = modes[modes.shape[0] - width :, :]
    out_ref[...] = jnp.where(lax.rem(lax.axis_index("cell"), 2) == 0, tail, head)


def inner_edge(modes, width):
    return pl.pallas_call(
        inner_kernel,
        out_shape=jax.ShapeDtypeStruct((width, modes.shape[1]), modes.dtype),
        in_specs=[pl.BlockSpec(memory_space=pltpu.VMEM)],
        out_specs=pl.BlockSpec(memory_space=pltpu.VMEM),
        compiler_params=pltpu.CompilerParams(vmem_limit_bytes=SMALL_VMEM),
        name="inner_edge",
    )(modes)


def turn_kernel(keep_rows, modes, out_ref):
    n_modes, count = out_ref.shape
    step = count // 4
    for start in range(0, count, step):
        columns = slice(start, start + step)
        block = modes[columns, :].T
        if keep_rows % TILE_ROWS:
            out_ref[:, columns] = block
        else:
            for place, k in enumerate(sum(teams(n_modes // keep_rows), [])):
                rows = slice(place * keep_rows, (place + 1) * keep_rows)
                out_ref[rows, columns] = block[k * keep_rows : (k + 1) * keep_rows]


def turn(modes, keep_rows):
    count, n_modes = modes.shape
    return pl.pallas_call(
        functools.partial(turn_kernel, keep_rows),
        out_shape=jax.ShapeDtypeStruct((n_modes, count), modes.dtype),
        in_specs=[pl.BlockSpec(memory_space=pltpu.VMEM)],
        out_specs=pl.BlockSpec(memory_space=pltpu.VMEM),
        compiler_params=pltpu.CompilerParams(vmem_limit_bytes=SMALL_VMEM),
        cost_estimate=pl.CostEstimate(flops=0, bytes_accessed=4 * modes.size, transcendentals=0),
        name="turn",
    )(modes)


def own_kernel(blocks, nb_ref, jac, modes, turned, p_ref, t_ref, left, parts, live):
    slots, width, _ = jac.shape
    n_modes = modes.shape[1]
    mid = n_modes // 2

    base = nb_ref[1, 0]
    count = jnp.int32(0)
    for s in range(blocks, slots):
        r = nb_ref[0, s]
        live[0, count] = s
        live[1, count] = r
        live[2, count] = nb_ref[1, s] - base + 1
        count += (r >= 0).astype(jnp.int32)
    live[0, count] = 0
    live[1, count] = 0
    live[2, count] = blocks + 2

    for s in range(blocks):
        left[s + 1] = dot(turned[:, s * width : (s + 1) * width], jac[s])
    left[0] = jnp.zeros((n_modes, width), jnp.float32)
    left[blocks + 1] = jnp.zeros((n_modes, width), jnp.float32)

    def pair(k, carry):
        for j in (2 * k, 2 * k + 1):
            columns = pl.ds(pl.multiple_of(live[1, j] * width, width), width)
            left[live[2, j]] += dot(turned[:, columns], jac[live[0, j]])
        return carry

    lax.fori_loop(0, (count + 1) // 2, pair, 0)

    both = jnp.zeros((2 * n_modes, n_modes), jnp.float32)
    step = 2 if blocks % 2 == 0 else 1
    for first in range(0, blocks, step):
        for c in range(first, first + step):
            upper, lower = halves(left[c + 1])
            parts[:n_modes, c * width : (c + 1) * width] = upper
            parts[n_modes:, c * width : (c + 1) * width] = lower
        inner = slice(first * width, (first + step) * width)
        both += dot(parts[:, inner], modes[inner, :])
    p_ref[...] = both[:n_modes] + both[n_modes:]
    for side, c in enumerate((0, blocks + 1)):
        upper, lower = halves(left[c])
        for half in range(2):
            t_ref[side, half, :mid] = upper[half * mid : (half + 1) * mid]
            t_ref[side, half, mid:] = lower[half * mid : (half + 1) * mid]


def own_part(neighbours, jac_blocks, modes, turned):
    slots, width, _ = jac_blocks.shape
    rows, n_modes = modes.shape
    blocks = rows // width
    flops = 2 * n_modes * width * width * slots + 4 * rows * n_modes * n_modes
    return pl.pallas_call(
        functools.partial(own_kernel, blocks),
        out_shape=(
            jax.ShapeDtypeStruct((n_modes, n_modes), jnp.float32),
            jax.ShapeDtypeStruct((2, 2, n_modes, width), jnp.bfloat16),
        ),
        in_specs=[
            pl.BlockSpec(memory_space=pltpu.SMEM),
            pl.BlockSpec(memory_space=pltpu.VMEM),
            pl.BlockSpec(memory_space=pltpu.VMEM),
            pl.BlockSpec(memory_space=pltpu.VMEM),
        ],
        out_specs=(pl.BlockSpec(memory_space=pltpu.VMEM), pl.BlockSpec(memory_space=pltpu.VMEM)),
        scratch_shapes=[
            pltpu.VMEM((blocks + 3, n_modes, width), jnp.float32),
            pltpu.VMEM((2 * n_modes, rows), jnp.bfloat16),
            pltpu.SMEM((3, slots + 1), jnp.int32),
        ],
        compiler_params=pltpu.CompilerParams(vmem_limit_bytes=OWN_VMEM),
        cost_estimate=pl.CostEstimate(
            flops=flops, bytes_accessed=slots * width * width * 2 + rows * n_modes * 2, transcendentals=0
        ),
        name="own_part",
    )(neighbours, jac_blocks, modes, turned)


def teams(count):
    chips = range(count // 2)
    middle = [chip for chip in (count // 4, count // 4 + 1) if 0 < chip < count // 2]
    rest = [chip for chip in chips if chip not in middle]
    rings = [middle + rest, middle + rest[:-2] + rest[: -3 : -1]]
    return [[2 * chip + (chip + half) % 2 for chip in reversed(rings[half])] for half in range(2)]


def own_team():
    me = lax.axis_index("cell")
    return lax.rem(me + me // 2, 2)


def regrouped(value, axis, keep_rows):
    first, second = teams(value.shape[axis] // keep_rows)
    starts = [k * keep_rows for k in first + second]
    return jnp.concatenate([lax.slice_in_dim(value, k, k + keep_rows, axis=axis) for k in starts], axis=axis)


def join_kernel(other, p_ref, t_ref, outer_ref, inner_ref, out_ref):
    core = lax.rem(lax.axis_index("cell"), 2)
    count = out_ref.shape[0]
    half = 1 - own_team() if other else own_team()
    rows = pl.ds(pl.multiple_of(half * count, TILE_ROWS), count)
    both = dot(t_ref[1 - core, half], inner_ref[...]) + dot(t_ref[core, half], outer_ref[...])
    out_ref[...] = p_ref[rows, :] + both[:count] + both[count:]


def join(other, p, t, outer, inner):
    rows = p.shape[0] // 2
    return pl.pallas_call(
        functools.partial(join_kernel, other),
        out_shape=jax.ShapeDtypeStruct((rows, p.shape[1]), jnp.float32),
        in_specs=[pl.BlockSpec(memory_space=pltpu.VMEM)] * 4,
        out_specs=pl.BlockSpec(memory_space=pltpu.VMEM),
        compiler_params=pltpu.CompilerParams(vmem_limit_bytes=SMALL_VMEM),
        cost_estimate=pl.CostEstimate(flops=8 * rows * outer.size, bytes_accessed=0, transcendentals=0),
        name="join_give" if other else "join_keep",
    )(p, t, outer, inner)


def sum_kernel(parts_ref, out_hbm, total, sem):
    total[...] = jnp.sum(parts_ref[...], axis=0)
    copy = pltpu.make_async_copy(total, out_hbm, sem)
    copy.start()
    copy.wait()


def sum_parts(parts):
    return pl.pallas_call(
        sum_kernel,
        out_shape=jax.ShapeDtypeStruct(parts.shape[1:], parts.dtype),
        in_specs=[pl.BlockSpec(memory_space=pltpu.VMEM)],
        out_specs=pl.BlockSpec(memory_space=pl.ANY),
        scratch_shapes=[pltpu.VMEM(parts.shape[1:], parts.dtype), pltpu.SemaphoreType.DMA],
        compiler_params=pltpu.CompilerParams(vmem_limit_bytes=SMALL_VMEM),
        name="sum_parts",
    )(parts)


def per_device(jac_blocks, modes, neighbours):
    width = jac_blocks.shape[1]
    rows, n_modes = modes.shape
    count = lax.axis_size("cell")
    keep_rows = n_modes // count
    across = [(i, min(max(i - 1 + 2 * (i % 2), 0), count - 1)) for i in range(count)]
    swap = [(i, i ^ 1) for i in range(count)]
    core = lax.rem(lax.axis_index("cell"), 2)
    outer_edge = lax.dynamic_slice_in_dim(modes, core * (rows - width), width)
    outer = lax.ppermute(gate(outer_edge), "cell", across)
    inner = lax.ppermute(inner_edge(modes, width), "cell", swap)
    p, t = own_part(neighbours.T, jac_blocks, modes, turn(modes, keep_rows))
    if keep_rows % TILE_ROWS:
        p = regrouped(p, 0, keep_rows)
        apart = jnp.swapaxes(t.reshape(2, 2, 2, n_modes // 2, width), 1, 2).reshape(2, 2, n_modes, width)
        apart = regrouped(apart, 2, keep_rows).reshape(2, 2, 2, n_modes // 2, width)
        t = jnp.swapaxes(apart, 1, 2).reshape(t.shape)
    got = lax.ppermute(join(True, p, t, outer, inner), "cell", swap)
    keep = join(False, p, t, outer, inner)
    pair = (keep + got).reshape(count // 2, keep_rows, n_modes)
    parts = lax.all_to_all(pair, "cell", 0, 0, axis_index_groups=teams(count))
    return sum_parts(parts)


def solution(mesh):
    placed = (P(("grp", "cell"), None, None), P(("grp", "cell"), None), P(("grp", "cell"), None))
    return jax.shard_map(
        per_device, mesh=mesh, in_specs=placed, out_specs=P(("grp", "cell"), None), check_vma=False
    )
```

```python
import functools

import jax
import jax.numpy as jnp
from jax import lax
from jax.experimental import pallas as pl
from jax.experimental.pallas import tpu as pltpu
from jax.sharding import PartitionSpec as P

OWN_VMEM = 24 * 2**20
SMALL_VMEM = 8 * 2**20
TILE_ROWS = 16
LOAD_COST = 35 * 10**8


def dot(a, b):
    return jnp.dot(a, b, preferred_element_type=jnp.float32)


def halves(value):
    upper = value.astype(jnp.bfloat16)
    return upper, (value - upper.astype(jnp.float32)).astype(jnp.bfloat16)


def gate_kernel(block_ref, out_ref):
    out_ref[...] = block_ref[...]


def gate(block):
    return pl.pallas_call(
        gate_kernel,
        out_shape=jax.ShapeDtypeStruct(block.shape, block.dtype),
        in_specs=[pl.BlockSpec(memory_space=pltpu.VMEM)],
        out_specs=pl.BlockSpec(memory_space=pltpu.VMEM),
        compiler_params=pltpu.CompilerParams(vmem_limit_bytes=SMALL_VMEM),
        cost_estimate=pl.CostEstimate(flops=LOAD_COST, bytes_accessed=0, transcendentals=0),
        name="gate",
    )(block)


def inner_kernel(modes, out_ref):
    width = out_ref.shape[0]
    head = modes[:width, :]
    tail = modes[modes.shape[0] - width :, :]
    out_ref[...] = jnp.where(lax.rem(lax.axis_index("cell"), 2) == 0, tail, head)


def inner_edge(modes, width):
    return pl.pallas_call(
        inner_kernel,
        out_shape=jax.ShapeDtypeStruct((width, modes.shape[1]), modes.dtype),
        in_specs=[pl.BlockSpec(memory_space=pltpu.VMEM)],
        out_specs=pl.BlockSpec(memory_space=pltpu.VMEM),
        compiler_params=pltpu.CompilerParams(vmem_limit_bytes=SMALL_VMEM),
        name="inner_edge",
    )(modes)


def turn_kernel(keep_rows, modes, out_ref):
    n_modes, count = out_ref.shape
    step = count // 4
    for start in range(0, count, step):
        columns = slice(start, start + step)
        block = modes[columns, :].T
        if keep_rows % TILE_ROWS:
            out_ref[:, columns] = block
        else:
            for place, k in enumerate(sum(teams(n_modes // keep_rows), [])):
                rows = slice(place * keep_rows, (place + 1) * keep_rows)
                out_ref[rows, columns] = block[k * keep_rows : (k + 1) * keep_rows]


def turn(modes, keep_rows):
    count, n_modes = modes.shape
    return pl.pallas_call(
        functools.partial(turn_kernel, keep_rows),
        out_shape=jax.ShapeDtypeStruct((n_modes, count), modes.dtype),
        in_specs=[pl.BlockSpec(memory_space=pltpu.VMEM)],
        out_specs=pl.BlockSpec(memory_space=pltpu.VMEM),
        compiler_params=pltpu.CompilerParams(vmem_limit_bytes=SMALL_VMEM),
        cost_estimate=pl.CostEstimate(flops=0, bytes_accessed=4 * modes.size, transcendentals=0),
        name="turn",
    )(modes)


def own_kernel(blocks, nb_ref, jac, modes, turned, p_ref, t_ref, left, parts, live):
    slots, width, _ = jac.shape
    n_modes = modes.shape[1]
    mid = n_modes // 2

    base = nb_ref[1, 0]
    count = jnp.int32(0)
    for s in range(blocks, slots):
        r = nb_ref[0, s]
        live[0, count] = s
        live[1, count] = r
        live[2, count] = nb_ref[1, s] - base + 1
        count += (r >= 0).astype(jnp.int32)
    live[0, count] = 0
    live[1, count] = 0
    live[2, count] = blocks + 2

    for s in range(blocks):
        left[s + 1] = dot(turned[:, s * width : (s + 1) * width], jac[s])
    left[0] = jnp.zeros((n_modes, width), jnp.float32)
    left[blocks + 1] = jnp.zeros((n_modes, width), jnp.float32)

    def pair(k, carry):
        for j in (2 * k, 2 * k + 1):
            columns = pl.ds(pl.multiple_of(live[1, j] * width, width), width)
            left[live[2, j]] += dot(turned[:, columns], jac[live[0, j]])
        return carry

    lax.fori_loop(0, (count + 1) // 2, pair, 0)

    both = jnp.zeros((2 * n_modes, n_modes), jnp.float32)
    step = 2 if blocks % 2 == 0 else 1
    for first in range(0, blocks, step):
        for c in range(first, first + step):
            upper, lower = halves(left[c + 1])
            parts[:n_modes, c * width : (c + 1) * width] = upper
            parts[n_modes:, c * width : (c + 1) * width] = lower
        inner = slice(first * width, (first + step) * width)
        both += dot(parts[:, inner], modes[inner, :])
    p_ref[...] = both[:n_modes] + both[n_modes:]
    for side, c in enumerate((0, blocks + 1)):
        upper, lower = halves(left[c])
        for half in range(2):
            t_ref[side, half, :mid] = upper[half * mid : (half + 1) * mid]
            t_ref[side, half, mid:] = lower[half * mid : (half + 1) * mid]


def own_part(neighbours, jac_blocks, modes, turned):
    slots, width, _ = jac_blocks.shape
    rows, n_modes = modes.shape
    blocks = rows // width
    flops = 2 * n_modes * width * width * slots + 4 * rows * n_modes * n_modes
    return pl.pallas_call(
        functools.partial(own_kernel, blocks),
        out_shape=(
            jax.ShapeDtypeStruct((n_modes, n_modes), jnp.float32),
            jax.ShapeDtypeStruct((2, 2, n_modes, width), jnp.bfloat16),
        ),
        in_specs=[
            pl.BlockSpec(memory_space=pltpu.SMEM),
            pl.BlockSpec(memory_space=pltpu.VMEM),
            pl.BlockSpec(memory_space=pltpu.VMEM),
            pl.BlockSpec(memory_space=pltpu.VMEM),
        ],
        out_specs=(pl.BlockSpec(memory_space=pltpu.VMEM), pl.BlockSpec(memory_space=pltpu.VMEM)),
        scratch_shapes=[
            pltpu.VMEM((blocks + 3, n_modes, width), jnp.float32),
            pltpu.VMEM((2 * n_modes, rows), jnp.bfloat16),
            pltpu.SMEM((3, slots + 1), jnp.int32),
        ],
        compiler_params=pltpu.CompilerParams(vmem_limit_bytes=OWN_VMEM),
        cost_estimate=pl.CostEstimate(
            flops=flops, bytes_accessed=slots * width * width * 2 + rows * n_modes * 2, transcendentals=0
        ),
        name="own_part",
    )(neighbours, jac_blocks, modes, turned)


def teams(count):
    chips = range(count // 2)
    middle = [chip for chip in (count // 4, count // 4 + 1) if 0 < chip < count // 2]
    rest = [chip for chip in chips if chip not in middle]
    rings = [middle + rest, middle + rest[:-2] + rest[: -3 : -1]]
    return [[2 * chip + (chip + half) % 2 for chip in reversed(rings[half])] for half in range(2)]


def own_team():
    me = lax.axis_index("cell")
    return lax.rem(me + me // 2, 2)


def regrouped(value, axis, keep_rows):
    first, second = teams(value.shape[axis] // keep_rows)
    starts = [k * keep_rows for k in first + second]
    return jnp.concatenate([lax.slice_in_dim(value, k, k + keep_rows, axis=axis) for k in starts], axis=axis)


def join_kernel(other, p_ref, t_ref, outer_ref, inner_ref, *out_refs):
    core = lax.rem(lax.axis_index("cell"), 2)
    count = p_ref.shape[0] // 2
    half = 1 - own_team() if other else own_team()
    rows = pl.ds(pl.multiple_of(half * count, TILE_ROWS), count)
    both = dot(t_ref[1 - core, half], inner_ref[...]) + dot(t_ref[core, half], outer_ref[...])
    total = p_ref[rows, :] + both[:count] + both[count:]
    step = count // len(out_refs)
    for k, out_ref in enumerate(out_refs):
        out_ref[...] = total[k * step : (k + 1) * step]


def join(other, pieces, p, t, outer, inner):
    rows = p.shape[0] // 2
    return pl.pallas_call(
        functools.partial(join_kernel, other),
        out_shape=(jax.ShapeDtypeStruct((rows // pieces, p.shape[1]), jnp.float32),) * pieces,
        in_specs=[pl.BlockSpec(memory_space=pltpu.VMEM)] * 4,
        out_specs=(pl.BlockSpec(memory_space=pltpu.VMEM),) * pieces,
        compiler_params=pltpu.CompilerParams(vmem_limit_bytes=SMALL_VMEM),
        cost_estimate=pl.CostEstimate(flops=8 * rows * outer.size, bytes_accessed=0, transcendentals=0),
        name="join_give" if other else "join_keep",
    )(p, t, outer, inner)


def sum_kernel(parts_ref, out_hbm, total, sem):
    total[...] = jnp.sum(parts_ref[...], axis=0)
    copy = pltpu.make_async_copy(total, out_hbm, sem)
    copy.start()
    copy.wait()


def sum_parts(parts):
    return pl.pallas_call(
        sum_kernel,
        out_shape=jax.ShapeDtypeStruct(parts.shape[1:], parts.dtype),
        in_specs=[pl.BlockSpec(memory_space=pltpu.VMEM)],
        out_specs=pl.BlockSpec(memory_space=pl.ANY),
        scratch_shapes=[pltpu.VMEM(parts.shape[1:], parts.dtype), pltpu.SemaphoreType.DMA],
        compiler_params=pltpu.CompilerParams(vmem_limit_bytes=SMALL_VMEM),
        name="sum_parts",
    )(parts)


def per_device(jac_blocks, modes, neighbours):
    width = jac_blocks.shape[1]
    rows, n_modes = modes.shape
    count = lax.axis_size("cell")
    keep_rows = n_modes // count
    across = [(i, min(max(i - 1 + 2 * (i % 2), 0), count - 1)) for i in range(count)]
    swap = [(i, i ^ 1) for i in range(count)]
    core = lax.rem(lax.axis_index("cell"), 2)
    outer_edge = lax.dynamic_slice_in_dim(modes, core * (rows - width), width)
    outer = lax.ppermute(gate(outer_edge), "cell", across)
    inner = lax.ppermute(inner_edge(modes, width), "cell", swap)
    p, t = own_part(neighbours.T, jac_blocks, modes, turn(modes, keep_rows))
    if keep_rows % TILE_ROWS:
        p = regrouped(p, 0, keep_rows)
        apart = jnp.swapaxes(t.reshape(2, 2, 2, n_modes // 2, width), 1, 2).reshape(2, 2, n_modes, width)
        apart = regrouped(apart, 2, keep_rows).reshape(2, 2, 2, n_modes // 2, width)
        t = jnp.swapaxes(apart, 1, 2).reshape(t.shape)
    got = [lax.ppermute(piece, "cell", swap) for piece in join(True, 2, p, t, outer, inner)]
    keep = join(False, 1, p, t, outer, inner)[0]
    pair = (keep + jnp.concatenate(got)).reshape(count // 2, keep_rows, n_modes)
    parts = lax.all_to_all(pair, "cell", 0, 0, axis_index_groups=teams(count))
    return sum_parts(parts)


def solution(mesh):
    placed = (P(("grp", "cell"), None, None), P(("grp", "cell"), None), P(("grp", "cell"), None))
    return jax.shard_map(
        per_device, mesh=mesh, in_specs=placed, out_specs=P(("grp", "cell"), None), check_vma=False
    )
```

```python
import functools

import jax
import jax.numpy as jnp
from jax import lax
from jax.experimental import pallas as pl
from jax.experimental.pallas import tpu as pltpu
from jax.sharding import PartitionSpec as P

OWN_VMEM = 24 * 2**20
SMALL_VMEM = 8 * 2**20
TILE_ROWS = 16
LOAD_COST = 35 * 10**8


def dot(a, b):
    return jnp.dot(a, b, preferred_element_type=jnp.float32)


def halves(value):
    upper = value.astype(jnp.bfloat16)
    return upper, (value - upper.astype(jnp.float32)).astype(jnp.bfloat16)


def gate_kernel(block_ref, out_ref):
    out_ref[...] = block_ref[...]


def gate(block):
    return pl.pallas_call(
        gate_kernel,
        out_shape=jax.ShapeDtypeStruct(block.shape, block.dtype),
        in_specs=[pl.BlockSpec(memory_space=pltpu.VMEM)],
        out_specs=pl.BlockSpec(memory_space=pltpu.VMEM),
        compiler_params=pltpu.CompilerParams(vmem_limit_bytes=SMALL_VMEM),
        cost_estimate=pl.CostEstimate(flops=LOAD_COST, bytes_accessed=0, transcendentals=0),
        name="gate",
    )(block)


def inner_kernel(modes, out_ref):
    width = out_ref.shape[0]
    head = modes[:width, :]
    tail = modes[modes.shape[0] - width :, :]
    out_ref[...] = jnp.where(lax.rem(lax.axis_index("cell"), 2) == 0, tail, head)


def inner_edge(modes, width):
    return pl.pallas_call(
        inner_kernel,
        out_shape=jax.ShapeDtypeStruct((width, modes.shape[1]), modes.dtype),
        in_specs=[pl.BlockSpec(memory_space=pltpu.VMEM)],
        out_specs=pl.BlockSpec(memory_space=pltpu.VMEM),
        compiler_params=pltpu.CompilerParams(vmem_limit_bytes=SMALL_VMEM),
        name="inner_edge",
    )(modes)


def turn_kernel(keep_rows, modes, out_ref):
    n_modes, count = out_ref.shape
    step = count // 4
    for start in range(0, count, step):
        columns = slice(start, start + step)
        block = modes[columns, :].T
        if keep_rows % TILE_ROWS:
            out_ref[:, columns] = block
        else:
            for place, k in enumerate(sum(teams(n_modes // keep_rows), [])):
                rows = slice(place * keep_rows, (place + 1) * keep_rows)
                out_ref[rows, columns] = block[k * keep_rows : (k + 1) * keep_rows]


def turn(modes, keep_rows):
    count, n_modes = modes.shape
    return pl.pallas_call(
        functools.partial(turn_kernel, keep_rows),
        out_shape=jax.ShapeDtypeStruct((n_modes, count), modes.dtype),
        in_specs=[pl.BlockSpec(memory_space=pltpu.VMEM)],
        out_specs=pl.BlockSpec(memory_space=pltpu.VMEM),
        compiler_params=pltpu.CompilerParams(vmem_limit_bytes=SMALL_VMEM),
        cost_estimate=pl.CostEstimate(flops=0, bytes_accessed=4 * modes.size, transcendentals=0),
        name="turn",
    )(modes)


def own_kernel(blocks, nb_ref, jac, modes, turned, p_ref, t_ref, left, parts, live):
    slots, width, _ = jac.shape
    n_modes = modes.shape[1]
    mid = n_modes // 2

    base = nb_ref[1, 0]
    count = jnp.int32(0)
    for s in range(blocks, slots):
        r = nb_ref[0, s]
        live[0, count] = s
        live[1, count] = r
        live[2, count] = nb_ref[1, s] - base + 1
        count += (r >= 0).astype(jnp.int32)
    live[0, count] = 0
    live[1, count] = 0
    live[2, count] = blocks + 2

    for s in range(blocks):
        left[s + 1] = dot(turned[:, s * width : (s + 1) * width], jac[s])
    left[0] = jnp.zeros((n_modes, width), jnp.float32)
    left[blocks + 1] = jnp.zeros((n_modes, width), jnp.float32)

    def pair(k, carry):
        for j in (2 * k, 2 * k + 1):
            columns = pl.ds(pl.multiple_of(live[1, j] * width, width), width)
            left[live[2, j]] += dot(turned[:, columns], jac[live[0, j]])
        return carry

    lax.fori_loop(0, (count + 1) // 2, pair, 0)

    both = jnp.zeros((2 * n_modes, n_modes), jnp.float32)
    step = 2 if blocks % 2 == 0 else 1
    for first in range(0, blocks, step):
        for c in range(first, first + step):
            upper, lower = halves(left[c + 1])
            parts[:n_modes, c * width : (c + 1) * width] = upper
            parts[n_modes:, c * width : (c + 1) * width] = lower
        inner = slice(first * width, (first + step) * width)
        both += dot(parts[:, inner], modes[inner, :])
    p_ref[...] = both[:n_modes] + both[n_modes:]
    for side, c in enumerate((0, blocks + 1)):
        upper, lower = halves(left[c])
        for half in range(2):
            t_ref[side, half, :mid] = upper[half * mid : (half + 1) * mid]
            t_ref[side, half, mid:] = lower[half * mid : (half + 1) * mid]


def own_part(neighbours, jac_blocks, modes, turned):
    slots, width, _ = jac_blocks.shape
    rows, n_modes = modes.shape
    blocks = rows // width
    flops = 2 * n_modes * width * width * slots + 4 * rows * n_modes * n_modes
    return pl.pallas_call(
        functools.partial(own_kernel, blocks),
        out_shape=(
            jax.ShapeDtypeStruct((n_modes, n_modes), jnp.float32),
            jax.ShapeDtypeStruct((2, 2, n_modes, width), jnp.bfloat16),
        ),
        in_specs=[
            pl.BlockSpec(memory_space=pltpu.SMEM),
            pl.BlockSpec(memory_space=pltpu.VMEM),
            pl.BlockSpec(memory_space=pltpu.VMEM),
            pl.BlockSpec(memory_space=pltpu.VMEM),
        ],
        out_specs=(pl.BlockSpec(memory_space=pltpu.VMEM), pl.BlockSpec(memory_space=pltpu.VMEM)),
        scratch_shapes=[
            pltpu.VMEM((blocks + 3, n_modes, width), jnp.float32),
            pltpu.VMEM((2 * n_modes, rows), jnp.bfloat16),
            pltpu.SMEM((3, slots + 1), jnp.int32),
        ],
        compiler_params=pltpu.CompilerParams(vmem_limit_bytes=OWN_VMEM),
        cost_estimate=pl.CostEstimate(
            flops=flops, bytes_accessed=slots * width * width * 2 + rows * n_modes * 2, transcendentals=0
        ),
        name="own_part",
    )(neighbours, jac_blocks, modes, turned)


def teams(count):
    chips = range(count // 2)
    middle = [chip for chip in (count // 4, count // 4 + 1) if 0 < chip < count // 2]
    rest = [chip for chip in chips if chip not in middle]
    near = count // 8
    rings = [[chip for chip in rest if chip != near] + [near] + middle, middle + rest[:-2] + rest[: -3 : -1]]
    return [[2 * chip + (chip + half) % 2 for chip in reversed(rings[half])] for half in range(2)]


def own_team():
    me = lax.axis_index("cell")
    return lax.rem(me + me // 2, 2)


def regrouped(value, axis, keep_rows):
    first, second = teams(value.shape[axis] // keep_rows)
    starts = [k * keep_rows for k in first + second]
    return jnp.concatenate([lax.slice_in_dim(value, k, k + keep_rows, axis=axis) for k in starts], axis=axis)


def join_kernel(other, p_ref, t_ref, outer_ref, inner_ref, out_ref):
    core = lax.rem(lax.axis_index("cell"), 2)
    count = out_ref.shape[0]
    half = 1 - own_team() if other else own_team()
    rows = pl.ds(pl.multiple_of(half * count, TILE_ROWS), count)
    both = dot(t_ref[1 - core, half], inner_ref[...]) + dot(t_ref[core, half], outer_ref[...])
    out_ref[...] = p_ref[rows, :] + both[:count] + both[count:]


def join(other, p, t, outer, inner):
    rows = p.shape[0] // 2
    return pl.pallas_call(
        functools.partial(join_kernel, other),
        out_shape=jax.ShapeDtypeStruct((rows, p.shape[1]), jnp.float32),
        in_specs=[pl.BlockSpec(memory_space=pltpu.VMEM)] * 4,
        out_specs=pl.BlockSpec(memory_space=pltpu.VMEM),
        compiler_params=pltpu.CompilerParams(vmem_limit_bytes=SMALL_VMEM),
        cost_estimate=pl.CostEstimate(flops=8 * rows * outer.size, bytes_accessed=0, transcendentals=0),
        name="join_give" if other else "join_keep",
    )(p, t, outer, inner)


def sum_kernel(parts_ref, out_hbm, total, sem):
    total[...] = jnp.sum(parts_ref[...], axis=0)
    copy = pltpu.make_async_copy(total, out_hbm, sem)
    copy.start()
    copy.wait()


def sum_parts(parts):
    return pl.pallas_call(
        sum_kernel,
        out_shape=jax.ShapeDtypeStruct(parts.shape[1:], parts.dtype),
        in_specs=[pl.BlockSpec(memory_space=pltpu.VMEM)],
        out_specs=pl.BlockSpec(memory_space=pl.ANY),
        scratch_shapes=[pltpu.VMEM(parts.shape[1:], parts.dtype), pltpu.SemaphoreType.DMA],
        compiler_params=pltpu.CompilerParams(vmem_limit_bytes=SMALL_VMEM),
        name="sum_parts",
    )(parts)


def per_device(jac_blocks, modes, neighbours):
    width = jac_blocks.shape[1]
    rows, n_modes = modes.shape
    count = lax.axis_size("cell")
    keep_rows = n_modes // count
    across = [(i, min(max(i - 1 + 2 * (i % 2), 0), count - 1)) for i in range(count)]
    swap = [(i, i ^ 1) for i in range(count)]
    core = lax.rem(lax.axis_index("cell"), 2)
    outer_edge = lax.dynamic_slice_in_dim(modes, core * (rows - width), width)
    outer = lax.ppermute(gate(outer_edge), "cell", across)
    inner = lax.ppermute(inner_edge(modes, width), "cell", swap)
    p, t = own_part(neighbours.T, jac_blocks, modes, turn(modes, keep_rows))
    if keep_rows % TILE_ROWS:
        p = regrouped(p, 0, keep_rows)
        apart = jnp.swapaxes(t.reshape(2, 2, 2, n_modes // 2, width), 1, 2).reshape(2, 2, n_modes, width)
        apart = regrouped(apart, 2, keep_rows).reshape(2, 2, 2, n_modes // 2, width)
        t = jnp.swapaxes(apart, 1, 2).reshape(t.shape)
    got = lax.ppermute(join(True, p, t, outer, inner), "cell", swap)
    keep = join(False, p, t, outer, inner)
    pair = (keep + got).reshape(count // 2, keep_rows, n_modes)
    parts = lax.all_to_all(pair, "cell", 0, 0, axis_index_groups=teams(count))
    return sum_parts(parts)


def solution(mesh):
    placed = (P(("grp", "cell"), None, None), P(("grp", "cell"), None), P(("grp", "cell"), None))
    return jax.shard_map(
        per_device, mesh=mesh, in_specs=placed, out_specs=P(("grp", "cell"), None), check_vma=False
    )
```

```python
import functools

import jax
import jax.numpy as jnp
from jax import lax
from jax.experimental import pallas as pl
from jax.experimental.pallas import tpu as pltpu
from jax.sharding import PartitionSpec as P

OWN_VMEM = 24 * 2**20
SMALL_VMEM = 8 * 2**20
TILE_ROWS = 16
LOAD_COST = 35 * 10**8


def dot(a, b):
    return jnp.dot(a, b, preferred_element_type=jnp.float32)


def halves(value):
    upper = value.astype(jnp.bfloat16)
    return upper, (value - upper.astype(jnp.float32)).astype(jnp.bfloat16)


def gate_kernel(block_ref, out_ref):
    out_ref[...] = block_ref[...]


def gate(block):
    return pl.pallas_call(
        gate_kernel,
        out_shape=jax.ShapeDtypeStruct(block.shape, block.dtype),
        in_specs=[pl.BlockSpec(memory_space=pltpu.VMEM)],
        out_specs=pl.BlockSpec(memory_space=pltpu.VMEM),
        compiler_params=pltpu.CompilerParams(vmem_limit_bytes=SMALL_VMEM),
        cost_estimate=pl.CostEstimate(flops=LOAD_COST, bytes_accessed=0, transcendentals=0),
        name="gate",
    )(block)


def inner_kernel(modes, out_ref):
    width = out_ref.shape[0]
    head = modes[:width, :]
    tail = modes[modes.shape[0] - width :, :]
    out_ref[...] = jnp.where(lax.rem(lax.axis_index("cell"), 2) == 0, tail, head)


def inner_edge(modes, width):
    return pl.pallas_call(
        inner_kernel,
        out_shape=jax.ShapeDtypeStruct((width, modes.shape[1]), modes.dtype),
        in_specs=[pl.BlockSpec(memory_space=pltpu.VMEM)],
        out_specs=pl.BlockSpec(memory_space=pltpu.VMEM),
        compiler_params=pltpu.CompilerParams(vmem_limit_bytes=SMALL_VMEM),
        name="inner_edge",
    )(modes)


def turn_kernel(keep_rows, modes, out_ref):
    n_modes, count = out_ref.shape
    step = count // 4
    for start in range(0, count, step):
        columns = slice(start, start + step)
        block = modes[columns, :].T
        if keep_rows % TILE_ROWS:
            out_ref[:, columns] = block
        else:
            for place, k in enumerate(sum(teams(n_modes // keep_rows), [])):
                rows = slice(place * keep_rows, (place + 1) * keep_rows)
                out_ref[rows, columns] = block[k * keep_rows : (k + 1) * keep_rows]


def turn(modes, keep_rows):
    count, n_modes = modes.shape
    return pl.pallas_call(
        functools.partial(turn_kernel, keep_rows),
        out_shape=jax.ShapeDtypeStruct((n_modes, count), modes.dtype),
        in_specs=[pl.BlockSpec(memory_space=pltpu.VMEM)],
        out_specs=pl.BlockSpec(memory_space=pltpu.VMEM),
        compiler_params=pltpu.CompilerParams(vmem_limit_bytes=SMALL_VMEM),
        cost_estimate=pl.CostEstimate(flops=0, bytes_accessed=4 * modes.size, transcendentals=0),
        name="turn",
    )(modes)


def own_kernel(blocks, nb_ref, jac, modes, turned, p_ref, t_ref, left, parts, live):
    slots, width, _ = jac.shape
    n_modes = modes.shape[1]
    mid = n_modes // 2

    base = nb_ref[1, 0]
    count = jnp.int32(0)
    for s in range(blocks, slots):
        r = nb_ref[0, s]
        live[0, count] = s
        live[1, count] = r
        live[2, count] = nb_ref[1, s] - base + 1
        count += (r >= 0).astype(jnp.int32)
    live[0, count] = 0
    live[1, count] = 0
    live[2, count] = blocks + 2

    for s in range(blocks):
        left[s + 1] = dot(turned[:, s * width : (s + 1) * width], jac[s])
    left[0] = jnp.zeros((n_modes, width), jnp.float32)
    left[blocks + 1] = jnp.zeros((n_modes, width), jnp.float32)

    def pair(k, carry):
        for j in (2 * k, 2 * k + 1):
            columns = pl.ds(pl.multiple_of(live[1, j] * width, width), width)
            left[live[2, j]] += dot(turned[:, columns], jac[live[0, j]])
        return carry

    lax.fori_loop(0, (count + 1) // 2, pair, 0)

    both = jnp.zeros((2 * n_modes, n_modes), jnp.float32)
    step = 2 if blocks % 2 == 0 else 1
    for first in range(0, blocks, step):
        for c in range(first, first + step):
            upper, lower = halves(left[c + 1])
            parts[:n_modes, c * width : (c + 1) * width] = upper
            parts[n_modes:, c * width : (c + 1) * width] = lower
        inner = slice(first * width, (first + step) * width)
        both += dot(parts[:, inner], modes[inner, :])
    p_ref[...] = both[:n_modes] + both[n_modes:]
    for side, c in enumerate((0, blocks + 1)):
        upper, lower = halves(left[c])
        for half in range(2):
            t_ref[side, half, :mid] = upper[half * mid : (half + 1) * mid]
            t_ref[side, half, mid:] = lower[half * mid : (half + 1) * mid]


def own_part(neighbours, jac_blocks, modes, turned):
    slots, width, _ = jac_blocks.shape
    rows, n_modes = modes.shape
    blocks = rows // width
    flops = 2 * n_modes * width * width * slots + 4 * rows * n_modes * n_modes
    return pl.pallas_call(
        functools.partial(own_kernel, blocks),
        out_shape=(
            jax.ShapeDtypeStruct((n_modes, n_modes), jnp.float32),
            jax.ShapeDtypeStruct((2, 2, n_modes, width), jnp.bfloat16),
        ),
        in_specs=[
            pl.BlockSpec(memory_space=pltpu.SMEM),
            pl.BlockSpec(memory_space=pltpu.VMEM),
            pl.BlockSpec(memory_space=pltpu.VMEM),
            pl.BlockSpec(memory_space=pltpu.VMEM),
        ],
        out_specs=(pl.BlockSpec(memory_space=pltpu.VMEM), pl.BlockSpec(memory_space=pltpu.VMEM)),
        scratch_shapes=[
            pltpu.VMEM((blocks + 3, n_modes, width), jnp.float32),
            pltpu.VMEM((2 * n_modes, rows), jnp.bfloat16),
            pltpu.SMEM((3, slots + 1), jnp.int32),
        ],
        compiler_params=pltpu.CompilerParams(vmem_limit_bytes=OWN_VMEM),
        cost_estimate=pl.CostEstimate(
            flops=flops, bytes_accessed=slots * width * width * 2 + rows * n_modes * 2, transcendentals=0
        ),
        name="own_part",
    )(neighbours, jac_blocks, modes, turned)


def teams(count):
    chips = range(count // 2)
    middle = [chip for chip in (count // 4, count // 4 + 1) if 0 < chip < count // 2]
    rings = []
    for near in ((count // 8 - 1, count // 8), (count // 8,)):
        near = [chip for chip in near if chip > 0]
        rings.append([chip for chip in chips if chip not in near + middle] + near + middle)
    return [[2 * chip + (chip + half) % 2 for chip in reversed(rings[half])] for half in range(2)]


def own_team():
    me = lax.axis_index("cell")
    return lax.rem(me + me // 2, 2)


def regrouped(value, axis, keep_rows):
    first, second = teams(value.shape[axis] // keep_rows)
    starts = [k * keep_rows for k in first + second]
    return jnp.concatenate([lax.slice_in_dim(value, k, k + keep_rows, axis=axis) for k in starts], axis=axis)


def join_kernel(other, p_ref, t_ref, outer_ref, inner_ref, out_ref):
    core = lax.rem(lax.axis_index("cell"), 2)
    count = out_ref.shape[0]
    half = 1 - own_team() if other else own_team()
    rows = pl.ds(pl.multiple_of(half * count, TILE_ROWS), count)
    both = dot(t_ref[1 - core, half], inner_ref[...]) + dot(t_ref[core, half], outer_ref[...])
    out_ref[...] = p_ref[rows, :] + both[:count] + both[count:]


def join(other, p, t, outer, inner):
    rows = p.shape[0] // 2
    return pl.pallas_call(
        functools.partial(join_kernel, other),
        out_shape=jax.ShapeDtypeStruct((rows, p.shape[1]), jnp.float32),
        in_specs=[pl.BlockSpec(memory_space=pltpu.VMEM)] * 4,
        out_specs=pl.BlockSpec(memory_space=pltpu.VMEM),
        compiler_params=pltpu.CompilerParams(vmem_limit_bytes=SMALL_VMEM),
        cost_estimate=pl.CostEstimate(flops=8 * rows * outer.size, bytes_accessed=0, transcendentals=0),
        name="join_give" if other else "join_keep",
    )(p, t, outer, inner)


def sum_kernel(parts_ref, out_hbm, total, sem):
    total[...] = jnp.sum(parts_ref[...], axis=0)
    copy = pltpu.make_async_copy(total, out_hbm, sem)
    copy.start()
    copy.wait()


def sum_parts(parts):
    return pl.pallas_call(
        sum_kernel,
        out_shape=jax.ShapeDtypeStruct(parts.shape[1:], parts.dtype),
        in_specs=[pl.BlockSpec(memory_space=pltpu.VMEM)],
        out_specs=pl.BlockSpec(memory_space=pl.ANY),
        scratch_shapes=[pltpu.VMEM(parts.shape[1:], parts.dtype), pltpu.SemaphoreType.DMA],
        compiler_params=pltpu.CompilerParams(vmem_limit_bytes=SMALL_VMEM),
        name="sum_parts",
    )(parts)


def per_device(jac_blocks, modes, neighbours):
    width = jac_blocks.shape[1]
    rows, n_modes = modes.shape
    count = lax.axis_size("cell")
    keep_rows = n_modes // count
    across = [(i, min(max(i - 1 + 2 * (i % 2), 0), count - 1)) for i in range(count)]
    swap = [(i, i ^ 1) for i in range(count)]
    core = lax.rem(lax.axis_index("cell"), 2)
    outer_edge = lax.dynamic_slice_in_dim(modes, core * (rows - width), width)
    outer = lax.ppermute(gate(outer_edge), "cell", across)
    inner = lax.ppermute(inner_edge(modes, width), "cell", swap)
    p, t = own_part(neighbours.T, jac_blocks, modes, turn(modes, keep_rows))
    if keep_rows % TILE_ROWS:
        p = regrouped(p, 0, keep_rows)
        apart = jnp.swapaxes(t.reshape(2, 2, 2, n_modes // 2, width), 1, 2).reshape(2, 2, n_modes, width)
        apart = regrouped(apart, 2, keep_rows).reshape(2, 2, 2, n_modes // 2, width)
        t = jnp.swapaxes(apart, 1, 2).reshape(t.shape)
    got = lax.ppermute(join(True, p, t, outer, inner), "cell", swap)
    keep = join(False, p, t, outer, inner)
    pair = (keep + got).reshape(count // 2, keep_rows, n_modes)
    parts = lax.all_to_all(pair, "cell", 0, 0, axis_index_groups=teams(count))
    return sum_parts(parts)


def solution(mesh):
    placed = (P(("grp", "cell"), None, None), P(("grp", "cell"), None), P(("grp", "cell"), None))
    return jax.shard_map(
        per_device, mesh=mesh, in_specs=placed, out_specs=P(("grp", "cell"), None), check_vma=False
    )
```

```python
import functools

import jax
import jax.numpy as jnp
from jax import lax
from jax.experimental import pallas as pl
from jax.experimental.pallas import tpu as pltpu
from jax.sharding import PartitionSpec as P

OWN_VMEM = 24 * 2**20
SMALL_VMEM = 8 * 2**20
TILE_ROWS = 16
LOAD_COST = 35 * 10**8


def dot(a, b):
    return jnp.dot(a, b, preferred_element_type=jnp.float32)


def halves(value):
    upper = value.astype(jnp.bfloat16)
    return upper, (value - upper.astype(jnp.float32)).astype(jnp.bfloat16)


def gate_kernel(block_ref, out_ref):
    out_ref[...] = block_ref[...]


def gate(block):
    return pl.pallas_call(
        gate_kernel,
        out_shape=jax.ShapeDtypeStruct(block.shape, block.dtype),
        in_specs=[pl.BlockSpec(memory_space=pltpu.VMEM)],
        out_specs=pl.BlockSpec(memory_space=pltpu.VMEM),
        compiler_params=pltpu.CompilerParams(vmem_limit_bytes=SMALL_VMEM),
        cost_estimate=pl.CostEstimate(flops=LOAD_COST, bytes_accessed=0, transcendentals=0),
        name="gate",
    )(block)


def inner_kernel(modes, out_ref):
    width = out_ref.shape[0]
    head = modes[:width, :]
    tail = modes[modes.shape[0] - width :, :]
    out_ref[...] = jnp.where(lax.rem(lax.axis_index("cell"), 2) == 0, tail, head)


def inner_edge(modes, width):
    return pl.pallas_call(
        inner_kernel,
        out_shape=jax.ShapeDtypeStruct((width, modes.shape[1]), modes.dtype),
        in_specs=[pl.BlockSpec(memory_space=pltpu.VMEM)],
        out_specs=pl.BlockSpec(memory_space=pltpu.VMEM),
        compiler_params=pltpu.CompilerParams(vmem_limit_bytes=SMALL_VMEM),
        name="inner_edge",
    )(modes)


def turn_kernel(keep_rows, modes, out_ref):
    n_modes, count = out_ref.shape
    step = count // 4
    for start in range(0, count, step):
        columns = slice(start, start + step)
        block = modes[columns, :].T
        if keep_rows % TILE_ROWS:
            out_ref[:, columns] = block
        else:
            for place, k in enumerate(sum(teams(n_modes // keep_rows), [])):
                rows = slice(place * keep_rows, (place + 1) * keep_rows)
                out_ref[rows, columns] = block[k * keep_rows : (k + 1) * keep_rows]


def turn(modes, keep_rows):
    count, n_modes = modes.shape
    return pl.pallas_call(
        functools.partial(turn_kernel, keep_rows),
        out_shape=jax.ShapeDtypeStruct((n_modes, count), modes.dtype),
        in_specs=[pl.BlockSpec(memory_space=pltpu.VMEM)],
        out_specs=pl.BlockSpec(memory_space=pltpu.VMEM),
        compiler_params=pltpu.CompilerParams(vmem_limit_bytes=SMALL_VMEM),
        cost_estimate=pl.CostEstimate(flops=0, bytes_accessed=4 * modes.size, transcendentals=0),
        name="turn",
    )(modes)


def own_kernel(blocks, nb_ref, jac, modes, turned, p_ref, t_ref, left, parts, live):
    slots, width, _ = jac.shape
    n_modes = modes.shape[1]
    mid = n_modes // 2

    base = nb_ref[1, 0]
    count = jnp.int32(0)
    for s in range(blocks, slots):
        r = nb_ref[0, s]
        live[0, count] = s
        live[1, count] = r
        live[2, count] = nb_ref[1, s] - base + 1
        count += (r >= 0).astype(jnp.int32)
    live[0, count] = 0
    live[1, count] = 0
    live[2, count] = blocks + 2

    for s in range(blocks):
        left[s + 1] = dot(turned[:, s * width : (s + 1) * width], jac[s])
    left[0] = jnp.zeros((n_modes, width), jnp.float32)
    left[blocks + 1] = jnp.zeros((n_modes, width), jnp.float32)

    def pair(k, carry):
        for j in (2 * k, 2 * k + 1):
            columns = pl.ds(pl.multiple_of(live[1, j] * width, width), width)
            left[live[2, j]] += dot(turned[:, columns], jac[live[0, j]])
        return carry

    lax.fori_loop(0, (count + 1) // 2, pair, 0)

    both = jnp.zeros((2 * n_modes, n_modes), jnp.float32)
    step = 2 if blocks % 2 == 0 else 1
    for first in range(0, blocks, step):
        for c in range(first, first + step):
            upper, lower = halves(left[c + 1])
            parts[:n_modes, c * width : (c + 1) * width] = upper
            parts[n_modes:, c * width : (c + 1) * width] = lower
        inner = slice(first * width, (first + step) * width)
        both += dot(parts[:, inner], modes[inner, :])
    p_ref[...] = both[:n_modes] + both[n_modes:]
    for side, c in enumerate((0, blocks + 1)):
        upper, lower = halves(left[c])
        for half in range(2):
            t_ref[side, half, :mid] = upper[half * mid : (half + 1) * mid]
            t_ref[side, half, mid:] = lower[half * mid : (half + 1) * mid]


def own_part(neighbours, jac_blocks, modes, turned):
    slots, width, _ = jac_blocks.shape
    rows, n_modes = modes.shape
    blocks = rows // width
    flops = 2 * n_modes * width * width * slots + 4 * rows * n_modes * n_modes
    return pl.pallas_call(
        functools.partial(own_kernel, blocks),
        out_shape=(
            jax.ShapeDtypeStruct((n_modes, n_modes), jnp.float32),
            jax.ShapeDtypeStruct((2, 2, n_modes, width), jnp.bfloat16),
        ),
        in_specs=[
            pl.BlockSpec(memory_space=pltpu.SMEM),
            pl.BlockSpec(memory_space=pltpu.VMEM),
            pl.BlockSpec(memory_space=pltpu.VMEM),
            pl.BlockSpec(memory_space=pltpu.VMEM),
        ],
        out_specs=(pl.BlockSpec(memory_space=pltpu.VMEM), pl.BlockSpec(memory_space=pltpu.VMEM)),
        scratch_shapes=[
            pltpu.VMEM((blocks + 3, n_modes, width), jnp.float32),
            pltpu.VMEM((2 * n_modes, rows), jnp.bfloat16),
            pltpu.SMEM((3, slots + 1), jnp.int32),
        ],
        compiler_params=pltpu.CompilerParams(vmem_limit_bytes=OWN_VMEM),
        cost_estimate=pl.CostEstimate(
            flops=flops, bytes_accessed=slots * width * width * 2 + rows * n_modes * 2, transcendentals=0
        ),
        name="own_part",
    )(neighbours, jac_blocks, modes, turned)


def teams(count):
    chips = range(count // 2)
    middle = [chip for chip in (count // 4, count // 4 + 1) if 0 < chip < count // 2]
    rest = [chip for chip in chips if chip not in middle]
    near = count // 8
    rings = [[chip for chip in rest if chip != near] + [near] + middle, middle + rest[:-2] + rest[: -3 : -1]]
    return [[2 * chip + half for chip in reversed(rings[half])] for half in range(2)]


def own_team():
    return lax.rem(lax.axis_index("cell"), 2)


def regrouped(value, axis, keep_rows):
    first, second = teams(value.shape[axis] // keep_rows)
    starts = [k * keep_rows for k in first + second]
    return jnp.concatenate([lax.slice_in_dim(value, k, k + keep_rows, axis=axis) for k in starts], axis=axis)


def join_kernel(other, p_ref, t_ref, outer_ref, inner_ref, out_ref):
    core = lax.rem(lax.axis_index("cell"), 2)
    count = out_ref.shape[0]
    half = 1 - own_team() if other else own_team()
    rows = pl.ds(pl.multiple_of(half * count, TILE_ROWS), count)
    both = dot(t_ref[1 - core, half], inner_ref[...]) + dot(t_ref[core, half], outer_ref[...])
    out_ref[...] = p_ref[rows, :] + both[:count] + both[count:]


def join(other, p, t, outer, inner):
    rows = p.shape[0] // 2
    return pl.pallas_call(
        functools.partial(join_kernel, other),
        out_shape=jax.ShapeDtypeStruct((rows, p.shape[1]), jnp.float32),
        in_specs=[pl.BlockSpec(memory_space=pltpu.VMEM)] * 4,
        out_specs=pl.BlockSpec(memory_space=pltpu.VMEM),
        compiler_params=pltpu.CompilerParams(vmem_limit_bytes=SMALL_VMEM),
        cost_estimate=pl.CostEstimate(flops=8 * rows * outer.size, bytes_accessed=0, transcendentals=0),
        name="join_give" if other else "join_keep",
    )(p, t, outer, inner)


def sum_kernel(parts_ref, out_hbm, total, sem):
    total[...] = jnp.sum(parts_ref[...], axis=0)
    copy = pltpu.make_async_copy(total, out_hbm, sem)
    copy.start()
    copy.wait()


def sum_parts(parts):
    return pl.pallas_call(
        sum_kernel,
        out_shape=jax.ShapeDtypeStruct(parts.shape[1:], parts.dtype),
        in_specs=[pl.BlockSpec(memory_space=pltpu.VMEM)],
        out_specs=pl.BlockSpec(memory_space=pl.ANY),
        scratch_shapes=[pltpu.VMEM(parts.shape[1:], parts.dtype), pltpu.SemaphoreType.DMA],
        compiler_params=pltpu.CompilerParams(vmem_limit_bytes=SMALL_VMEM),
        name="sum_parts",
    )(parts)


def per_device(jac_blocks, modes, neighbours):
    width = jac_blocks.shape[1]
    rows, n_modes = modes.shape
    count = lax.axis_size("cell")
    keep_rows = n_modes // count
    across = [(i, min(max(i - 1 + 2 * (i % 2), 0), count - 1)) for i in range(count)]
    swap = [(i, i ^ 1) for i in range(count)]
    core = lax.rem(lax.axis_index("cell"), 2)
    outer_edge = lax.dynamic_slice_in_dim(modes, core * (rows - width), width)
    outer = lax.ppermute(gate(outer_edge), "cell", across)
    inner = lax.ppermute(inner_edge(modes, width), "cell", swap)
    p, t = own_part(neighbours.T, jac_blocks, modes, turn(modes, keep_rows))
    if keep_rows % TILE_ROWS:
        p = regrouped(p, 0, keep_rows)
        apart = jnp.swapaxes(t.reshape(2, 2, 2, n_modes // 2, width), 1, 2).reshape(2, 2, n_modes, width)
        apart = regrouped(apart, 2, keep_rows).reshape(2, 2, 2, n_modes // 2, width)
        t = jnp.swapaxes(apart, 1, 2).reshape(t.shape)
    got = lax.ppermute(join(True, p, t, outer, inner), "cell", swap)
    keep = join(False, p, t, outer, inner)
    pair = (keep + got).reshape(count // 2, keep_rows, n_modes)
    parts = lax.all_to_all(pair, "cell", 0, 0, axis_index_groups=teams(count))
    return sum_parts(parts)


def solution(mesh):
    placed = (P(("grp", "cell"), None, None), P(("grp", "cell"), None), P(("grp", "cell"), None))
    return jax.shard_map(
        per_device, mesh=mesh, in_specs=placed, out_specs=P(("grp", "cell"), None), check_vma=False
    )
```

```python
import functools

import jax
import jax.numpy as jnp
from jax import lax
from jax.experimental import pallas as pl
from jax.experimental.pallas import tpu as pltpu
from jax.sharding import PartitionSpec as P

OWN_VMEM = 24 * 2**20
SMALL_VMEM = 8 * 2**20
TILE_ROWS = 16
LOAD_COST = 35 * 10**8


def dot(a, b):
    return jnp.dot(a, b, preferred_element_type=jnp.float32)


def halves(value):
    upper = value.astype(jnp.bfloat16)
    return upper, (value - upper.astype(jnp.float32)).astype(jnp.bfloat16)


def gate(block):
    return pl.pallas_call(
        lambda block_ref, out_ref: None,
        out_shape=jax.ShapeDtypeStruct(block.shape, block.dtype),
        in_specs=[pl.BlockSpec(memory_space=pl.ANY)],
        out_specs=pl.BlockSpec(memory_space=pl.ANY),
        input_output_aliases={0: 0},
        compiler_params=pltpu.CompilerParams(vmem_limit_bytes=SMALL_VMEM),
        cost_estimate=pl.CostEstimate(flops=LOAD_COST, bytes_accessed=0, transcendentals=0),
        name="gate",
    )(block)


def inner_kernel(modes, out_ref):
    width = out_ref.shape[0]
    head = modes[:width, :]
    tail = modes[modes.shape[0] - width :, :]
    out_ref[...] = jnp.where(lax.rem(lax.axis_index("cell"), 2) == 0, tail, head)


def inner_edge(modes, width):
    return pl.pallas_call(
        inner_kernel,
        out_shape=jax.ShapeDtypeStruct((width, modes.shape[1]), modes.dtype),
        in_specs=[pl.BlockSpec(memory_space=pltpu.VMEM)],
        out_specs=pl.BlockSpec(memory_space=pltpu.VMEM),
        compiler_params=pltpu.CompilerParams(vmem_limit_bytes=SMALL_VMEM),
        name="inner_edge",
    )(modes)


def turn_kernel(keep_rows, modes, out_ref):
    n_modes, count = out_ref.shape
    step = count // 4
    for start in range(0, count, step):
        columns = slice(start, start + step)
        block = modes[columns, :].T
        if keep_rows % TILE_ROWS:
            out_ref[:, columns] = block
        else:
            for place, k in enumerate(sum(teams(n_modes // keep_rows), [])):
                rows = slice(place * keep_rows, (place + 1) * keep_rows)
                out_ref[rows, columns] = block[k * keep_rows : (k + 1) * keep_rows]


def turn(modes, keep_rows):
    count, n_modes = modes.shape
    return pl.pallas_call(
        functools.partial(turn_kernel, keep_rows),
        out_shape=jax.ShapeDtypeStruct((n_modes, count), modes.dtype),
        in_specs=[pl.BlockSpec(memory_space=pltpu.VMEM)],
        out_specs=pl.BlockSpec(memory_space=pltpu.VMEM),
        compiler_params=pltpu.CompilerParams(vmem_limit_bytes=SMALL_VMEM),
        cost_estimate=pl.CostEstimate(flops=0, bytes_accessed=4 * modes.size, transcendentals=0),
        name="turn",
    )(modes)


def own_kernel(blocks, nb_ref, jac, modes, turned, p_ref, t_ref, left, parts, live):
    slots, width, _ = jac.shape
    n_modes = modes.shape[1]
    mid = n_modes // 2

    base = nb_ref[1, 0]
    count = jnp.int32(0)
    for s in range(blocks, slots):
        r = nb_ref[0, s]
        live[0, count] = s
        live[1, count] = r
        live[2, count] = nb_ref[1, s] - base + 1
        count += (r >= 0).astype(jnp.int32)
    live[0, count] = 0
    live[1, count] = 0
    live[2, count] = blocks + 2

    for s in range(blocks):
        left[s + 1] = dot(turned[:, s * width : (s + 1) * width], jac[s])
    left[0] = jnp.zeros((n_modes, width), jnp.float32)
    left[blocks + 1] = jnp.zeros((n_modes, width), jnp.float32)

    def pair(k, carry):
        for j in (2 * k, 2 * k + 1):
            columns = pl.ds(pl.multiple_of(live[1, j] * width, width), width)
            left[live[2, j]] += dot(turned[:, columns], jac[live[0, j]])
        return carry

    lax.fori_loop(0, (count + 1) // 2, pair, 0)

    both = jnp.zeros((2 * n_modes, n_modes), jnp.float32)
    step = 2 if blocks % 2 == 0 else 1
    for first in range(0, blocks, step):
        for c in range(first, first + step):
            upper, lower = halves(left[c + 1])
            parts[:n_modes, c * width : (c + 1) * width] = upper
            parts[n_modes:, c * width : (c + 1) * width] = lower
        inner = slice(first * width, (first + step) * width)
        both += dot(parts[:, inner], modes[inner, :])
    p_ref[...] = both[:n_modes] + both[n_modes:]
    for side, c in enumerate((0, blocks + 1)):
        upper, lower = halves(left[c])
        for half in range(2):
            t_ref[side, half, :mid] = upper[half * mid : (half + 1) * mid]
            t_ref[side, half, mid:] = lower[half * mid : (half + 1) * mid]


def own_part(neighbours, jac_blocks, modes, turned):
    slots, width, _ = jac_blocks.shape
    rows, n_modes = modes.shape
    blocks = rows // width
    flops = 2 * n_modes * width * width * slots + 4 * rows * n_modes * n_modes
    return pl.pallas_call(
        functools.partial(own_kernel, blocks),
        out_shape=(
            jax.ShapeDtypeStruct((n_modes, n_modes), jnp.float32),
            jax.ShapeDtypeStruct((2, 2, n_modes, width), jnp.bfloat16),
        ),
        in_specs=[
            pl.BlockSpec(memory_space=pltpu.SMEM),
            pl.BlockSpec(memory_space=pltpu.VMEM),
            pl.BlockSpec(memory_space=pltpu.VMEM),
            pl.BlockSpec(memory_space=pltpu.VMEM),
        ],
        out_specs=(pl.BlockSpec(memory_space=pltpu.VMEM), pl.BlockSpec(memory_space=pltpu.VMEM)),
        scratch_shapes=[
            pltpu.VMEM((blocks + 3, n_modes, width), jnp.float32),
            pltpu.VMEM((2 * n_modes, rows), jnp.bfloat16),
            pltpu.SMEM((3, slots + 1), jnp.int32),
        ],
        compiler_params=pltpu.CompilerParams(vmem_limit_bytes=OWN_VMEM),
        cost_estimate=pl.CostEstimate(
            flops=flops, bytes_accessed=slots * width * width * 2 + rows * n_modes * 2, transcendentals=0
        ),
        name="own_part",
    )(neighbours, jac_blocks, modes, turned)


def teams(count):
    chips = range(count // 2)
    middle = [chip for chip in (count // 4, count // 4 + 1) if 0 < chip < count // 2]
    rest = [chip for chip in chips if chip not in middle]
    rings = [middle + rest, middle + rest[:-2] + rest[: -3 : -1]]
    return [[2 * chip + (chip + half) % 2 for chip in reversed(rings[half])] for half in range(2)]


def own_team():
    me = lax.axis_index("cell")
    return lax.rem(me + me // 2, 2)


def regrouped(value, axis, keep_rows):
    first, second = teams(value.shape[axis] // keep_rows)
    starts = [k * keep_rows for k in first + second]
    return jnp.concatenate([lax.slice_in_dim(value, k, k + keep_rows, axis=axis) for k in starts], axis=axis)


def join_kernel(other, p_ref, t_ref, outer_ref, inner_ref, out_ref):
    core = lax.rem(lax.axis_index("cell"), 2)
    count = out_ref.shape[0]
    half = 1 - own_team() if other else own_team()
    rows = pl.ds(pl.multiple_of(half * count, TILE_ROWS), count)
    left = jnp.concatenate([t_ref[1 - core, half], t_ref[core, half]], axis=1)
    both = dot(left, jnp.concatenate([inner_ref[...], outer_ref[...]], axis=0))
    out_ref[...] = p_ref[rows, :] + both[:count] + both[count:]


def join(other, p, t, outer, inner):
    rows = p.shape[0] // 2
    return pl.pallas_call(
        functools.partial(join_kernel, other),
        out_shape=jax.ShapeDtypeStruct((rows, p.shape[1]), jnp.float32),
        in_specs=[pl.BlockSpec(memory_space=pltpu.VMEM)] * 4,
        out_specs=pl.BlockSpec(memory_space=pltpu.VMEM),
        compiler_params=pltpu.CompilerParams(vmem_limit_bytes=SMALL_VMEM),
        cost_estimate=pl.CostEstimate(flops=8 * rows * outer.size, bytes_accessed=0, transcendentals=0),
        name="join_give" if other else "join_keep",
    )(p, t, outer, inner)


def sum_kernel(parts_ref, out_hbm, total, sem):
    total[...] = jnp.sum(parts_ref[...], axis=0)
    copy = pltpu.make_async_copy(total, out_hbm, sem)
    copy.start()
    copy.wait()


def sum_parts(parts):
    return pl.pallas_call(
        sum_kernel,
        out_shape=jax.ShapeDtypeStruct(parts.shape[1:], parts.dtype),
        in_specs=[pl.BlockSpec(memory_space=pltpu.VMEM)],
        out_specs=pl.BlockSpec(memory_space=pl.ANY),
        scratch_shapes=[pltpu.VMEM(parts.shape[1:], parts.dtype), pltpu.SemaphoreType.DMA],
        compiler_params=pltpu.CompilerParams(vmem_limit_bytes=SMALL_VMEM),
        name="sum_parts",
    )(parts)


def per_device(jac_blocks, modes, neighbours):
    width = jac_blocks.shape[1]
    rows, n_modes = modes.shape
    count = lax.axis_size("cell")
    keep_rows = n_modes // count
    across = [(i, min(max(i - 1 + 2 * (i % 2), 0), count - 1)) for i in range(count)]
    swap = [(i, i ^ 1) for i in range(count)]
    core = lax.rem(lax.axis_index("cell"), 2)
    outer_edge = lax.dynamic_slice_in_dim(modes, core * (rows - width), width)
    outer = lax.ppermute(gate(outer_edge), "cell", across)
    inner = lax.ppermute(inner_edge(modes, width), "cell", swap)
    p, t = own_part(neighbours.T, jac_blocks, modes, turn(modes, keep_rows))
    if keep_rows % TILE_ROWS:
        p = regrouped(p, 0, keep_rows)
        apart = jnp.swapaxes(t.reshape(2, 2, 2, n_modes // 2, width), 1, 2).reshape(2, 2, n_modes, width)
        apart = regrouped(apart, 2, keep_rows).reshape(2, 2, 2, n_modes // 2, width)
        t = jnp.swapaxes(apart, 1, 2).reshape(t.shape)
    got = lax.ppermute(join(True, p, t, outer, inner), "cell", swap)
    keep = join(False, p, t, outer, inner)
    pair = (keep + got).reshape(count // 2, keep_rows, n_modes)
    parts = lax.all_to_all(pair, "cell", 0, 0, axis_index_groups=teams(count))
    return sum_parts(parts)


def solution(mesh):
    placed = (P(("grp", "cell"), None, None), P(("grp", "cell"), None), P(("grp", "cell"), None))
    return jax.shard_map(
        per_device, mesh=mesh, in_specs=placed, out_specs=P(("grp", "cell"), None), check_vma=False
    )
```

```python
import functools

import jax
import jax.numpy as jnp
from jax import lax
from jax.experimental import pallas as pl
from jax.experimental.pallas import tpu as pltpu
from jax.sharding import PartitionSpec as P

OWN_VMEM = 24 * 2**20
SMALL_VMEM = 8 * 2**20
TILE_ROWS = 16
LOAD_COST = 35 * 10**8


def dot(a, b):
    return jnp.dot(a, b, preferred_element_type=jnp.float32)


def halves(value):
    upper = value.astype(jnp.bfloat16)
    return upper, (value - upper.astype(jnp.float32)).astype(jnp.bfloat16)


def gate(block):
    return pl.pallas_call(
        lambda block_ref, out_ref: None,
        out_shape=jax.ShapeDtypeStruct(block.shape, block.dtype),
        in_specs=[pl.BlockSpec(memory_space=pl.ANY)],
        out_specs=pl.BlockSpec(memory_space=pl.ANY),
        input_output_aliases={0: 0},
        compiler_params=pltpu.CompilerParams(vmem_limit_bytes=SMALL_VMEM),
        cost_estimate=pl.CostEstimate(flops=LOAD_COST, bytes_accessed=0, transcendentals=0),
        name="gate",
    )(block)


def inner_kernel(modes, out_ref):
    width = out_ref.shape[0]
    head = modes[:width, :]
    tail = modes[modes.shape[0] - width :, :]
    out_ref[...] = jnp.where(lax.rem(lax.axis_index("cell"), 2) == 0, tail, head)


def inner_edge(modes, width):
    return pl.pallas_call(
        inner_kernel,
        out_shape=jax.ShapeDtypeStruct((width, modes.shape[1]), modes.dtype),
        in_specs=[pl.BlockSpec(memory_space=pltpu.VMEM)],
        out_specs=pl.BlockSpec(memory_space=pltpu.VMEM),
        compiler_params=pltpu.CompilerParams(vmem_limit_bytes=SMALL_VMEM),
        name="inner_edge",
    )(modes)


def turn_kernel(keep_rows, modes, out_ref):
    n_modes, count = out_ref.shape
    step = count // 4
    for start in range(0, count, step):
        columns = slice(start, start + step)
        block = modes[columns, :].T
        if keep_rows % TILE_ROWS:
            out_ref[:, columns] = block
        else:
            for place, k in enumerate(sum(teams(n_modes // keep_rows), [])):
                rows = slice(place * keep_rows, (place + 1) * keep_rows)
                out_ref[rows, columns] = block[k * keep_rows : (k + 1) * keep_rows]


def turn(modes, keep_rows):
    count, n_modes = modes.shape
    return pl.pallas_call(
        functools.partial(turn_kernel, keep_rows),
        out_shape=jax.ShapeDtypeStruct((n_modes, count), modes.dtype),
        in_specs=[pl.BlockSpec(memory_space=pltpu.VMEM)],
        out_specs=pl.BlockSpec(memory_space=pltpu.VMEM),
        compiler_params=pltpu.CompilerParams(vmem_limit_bytes=SMALL_VMEM),
        cost_estimate=pl.CostEstimate(flops=0, bytes_accessed=4 * modes.size, transcendentals=0),
        name="turn",
    )(modes)


def own_kernel(blocks, nb_ref, jac, modes, turned, p_ref, t_ref, left, parts, live):
    slots, width, _ = jac.shape
    n_modes = modes.shape[1]
    mid = n_modes // 2

    base = nb_ref[1, 0]
    count = jnp.int32(0)
    for s in range(blocks, slots):
        r = nb_ref[0, s]
        live[0, count] = s
        live[1, count] = r
        live[2, count] = nb_ref[1, s] - base + 1
        count += (r >= 0).astype(jnp.int32)
    live[0, count] = 0
    live[1, count] = 0
    live[2, count] = blocks + 2

    for s in range(blocks):
        left[s + 1] = dot(turned[:, s * width : (s + 1) * width], jac[s])
    left[0] = jnp.zeros((n_modes, width), jnp.float32)
    left[blocks + 1] = jnp.zeros((n_modes, width), jnp.float32)

    def pair(k, carry):
        for j in (2 * k, 2 * k + 1):
            columns = pl.ds(pl.multiple_of(live[1, j] * width, width), width)
            left[live[2, j]] += dot(turned[:, columns], jac[live[0, j]])
        return carry

    lax.fori_loop(0, (count + 1) // 2, pair, 0)

    def split_outside(side, c):
        upper, lower = halves(left[c])
        for half in range(2):
            t_ref[side, half, :mid] = upper[half * mid : (half + 1) * mid]
            t_ref[side, half, mid:] = lower[half * mid : (half + 1) * mid]

    both = jnp.zeros((2 * n_modes, n_modes), jnp.float32)
    for c in range(blocks):
        columns = slice(c * width, (c + 1) * width)
        upper, lower = halves(left[c + 1])
        parts[:n_modes, columns] = upper
        parts[n_modes:, columns] = lower
        both += dot(parts[:, columns], modes[columns, :])
        if c < 2:
            split_outside(c, c * (blocks + 1))
    p_ref[...] = both[:n_modes] + both[n_modes:]


def own_part(neighbours, jac_blocks, modes, turned):
    slots, width, _ = jac_blocks.shape
    rows, n_modes = modes.shape
    blocks = rows // width
    flops = 2 * n_modes * width * width * slots + 4 * rows * n_modes * n_modes
    return pl.pallas_call(
        functools.partial(own_kernel, blocks),
        out_shape=(
            jax.ShapeDtypeStruct((n_modes, n_modes), jnp.float32),
            jax.ShapeDtypeStruct((2, 2, n_modes, width), jnp.bfloat16),
        ),
        in_specs=[
            pl.BlockSpec(memory_space=pltpu.SMEM),
            pl.BlockSpec(memory_space=pltpu.VMEM),
            pl.BlockSpec(memory_space=pltpu.VMEM),
            pl.BlockSpec(memory_space=pltpu.VMEM),
        ],
        out_specs=(pl.BlockSpec(memory_space=pltpu.VMEM), pl.BlockSpec(memory_space=pltpu.VMEM)),
        scratch_shapes=[
            pltpu.VMEM((blocks + 3, n_modes, width), jnp.float32),
            pltpu.VMEM((2 * n_modes, rows), jnp.bfloat16),
            pltpu.SMEM((3, slots + 1), jnp.int32),
        ],
        compiler_params=pltpu.CompilerParams(vmem_limit_bytes=OWN_VMEM),
        cost_estimate=pl.CostEstimate(
            flops=flops, bytes_accessed=slots * width * width * 2 + rows * n_modes * 2, transcendentals=0
        ),
        name="own_part",
    )(neighbours, jac_blocks, modes, turned)


def teams(count):
    chips = range(count // 2)
    middle = [chip for chip in (count // 4, count // 4 + 1) if 0 < chip < count // 2]
    rest = [chip for chip in chips if chip not in middle]
    rings = [middle + rest, middle + rest[:-2] + rest[: -3 : -1]]
    return [[2 * chip + (chip + half) % 2 for chip in reversed(rings[half])] for half in range(2)]


def own_team():
    me = lax.axis_index("cell")
    return lax.rem(me + me // 2, 2)


def regrouped(value, axis, keep_rows):
    first, second = teams(value.shape[axis] // keep_rows)
    starts = [k * keep_rows for k in first + second]
    return jnp.concatenate([lax.slice_in_dim(value, k, k + keep_rows, axis=axis) for k in starts], axis=axis)


def join_kernel(other, p_ref, t_ref, outer_ref, inner_ref, out_ref):
    core = lax.rem(lax.axis_index("cell"), 2)
    count = out_ref.shape[0]
    half = 1 - own_team() if other else own_team()
    rows = pl.ds(pl.multiple_of(half * count, TILE_ROWS), count)
    left = jnp.concatenate([t_ref[1 - core, half], t_ref[core, half]], axis=1)
    both = dot(left, jnp.concatenate([inner_ref[...], outer_ref[...]], axis=0))
    out_ref[...] = p_ref[rows, :] + both[:count] + both[count:]


def join(other, p, t, outer, inner):
    rows = p.shape[0] // 2
    return pl.pallas_call(
        functools.partial(join_kernel, other),
        out_shape=jax.ShapeDtypeStruct((rows, p.shape[1]), jnp.float32),
        in_specs=[pl.BlockSpec(memory_space=pltpu.VMEM)] * 4,
        out_specs=pl.BlockSpec(memory_space=pltpu.VMEM),
        compiler_params=pltpu.CompilerParams(vmem_limit_bytes=SMALL_VMEM),
        cost_estimate=pl.CostEstimate(flops=8 * rows * outer.size, bytes_accessed=0, transcendentals=0),
        name="join_give" if other else "join_keep",
    )(p, t, outer, inner)


def sum_kernel(parts_ref, out_hbm, total, sem):
    total[...] = jnp.sum(parts_ref[...], axis=0)
    copy = pltpu.make_async_copy(total, out_hbm, sem)
    copy.start()
    copy.wait()


def sum_parts(parts):
    return pl.pallas_call(
        sum_kernel,
        out_shape=jax.ShapeDtypeStruct(parts.shape[1:], parts.dtype),
        in_specs=[pl.BlockSpec(memory_space=pltpu.VMEM)],
        out_specs=pl.BlockSpec(memory_space=pl.ANY),
        scratch_shapes=[pltpu.VMEM(parts.shape[1:], parts.dtype), pltpu.SemaphoreType.DMA],
        compiler_params=pltpu.CompilerParams(vmem_limit_bytes=SMALL_VMEM),
        name="sum_parts",
    )(parts)


def per_device(jac_blocks, modes, neighbours):
    width = jac_blocks.shape[1]
    rows, n_modes = modes.shape
    count = lax.axis_size("cell")
    keep_rows = n_modes // count
    across = [(i, min(max(i - 1 + 2 * (i % 2), 0), count - 1)) for i in range(count)]
    swap = [(i, i ^ 1) for i in range(count)]
    core = lax.rem(lax.axis_index("cell"), 2)
    outer_edge = lax.dynamic_slice_in_dim(modes, core * (rows - width), width)
    outer = lax.ppermute(gate(outer_edge), "cell", across)
    inner = lax.ppermute(inner_edge(modes, width), "cell", swap)
    p, t = own_part(neighbours.T, jac_blocks, modes, turn(modes, keep_rows))
    if keep_rows % TILE_ROWS:
        p = regrouped(p, 0, keep_rows)
        apart = jnp.swapaxes(t.reshape(2, 2, 2, n_modes // 2, width), 1, 2).reshape(2, 2, n_modes, width)
        apart = regrouped(apart, 2, keep_rows).reshape(2, 2, 2, n_modes // 2, width)
        t = jnp.swapaxes(apart, 1, 2).reshape(t.shape)
    got = lax.ppermute(join(True, p, t, outer, inner), "cell", swap)
    keep = join(False, p, t, outer, inner)
    pair = (keep + got).reshape(count // 2, keep_rows, n_modes)
    parts = lax.all_to_all(pair, "cell", 0, 0, axis_index_groups=teams(count))
    return sum_parts(parts)


def solution(mesh):
    placed = (P(("grp", "cell"), None, None), P(("grp", "cell"), None), P(("grp", "cell"), None))
    return jax.shard_map(
        per_device, mesh=mesh, in_specs=placed, out_specs=P(("grp", "cell"), None), check_vma=False
    )
```

```python
import functools

import jax
import jax.numpy as jnp
from jax import lax
from jax.experimental import pallas as pl
from jax.experimental.pallas import tpu as pltpu
from jax.sharding import PartitionSpec as P

OWN_VMEM = 24 * 2**20
SMALL_VMEM = 8 * 2**20
TILE_ROWS = 16
LOAD_COST = 35 * 10**8


def dot(a, b):
    return jnp.dot(a, b, preferred_element_type=jnp.float32)


def halves(value):
    upper = value.astype(jnp.bfloat16)
    return upper, (value - upper.astype(jnp.float32)).astype(jnp.bfloat16)


def gate(block):
    return pl.pallas_call(
        lambda block_ref, out_ref: None,
        out_shape=jax.ShapeDtypeStruct(block.shape, block.dtype),
        in_specs=[pl.BlockSpec(memory_space=pl.ANY)],
        out_specs=pl.BlockSpec(memory_space=pl.ANY),
        input_output_aliases={0: 0},
        compiler_params=pltpu.CompilerParams(vmem_limit_bytes=SMALL_VMEM),
        cost_estimate=pl.CostEstimate(flops=LOAD_COST, bytes_accessed=0, transcendentals=0),
        name="gate",
    )(block)


def inner_kernel(modes, out_ref):
    width = out_ref.shape[0]
    head = modes[:width, :]
    tail = modes[modes.shape[0] - width :, :]
    out_ref[...] = jnp.where(lax.rem(lax.axis_index("cell"), 2) == 0, tail, head)


def inner_edge(modes, width):
    return pl.pallas_call(
        inner_kernel,
        out_shape=jax.ShapeDtypeStruct((width, modes.shape[1]), modes.dtype),
        in_specs=[pl.BlockSpec(memory_space=pltpu.VMEM)],
        out_specs=pl.BlockSpec(memory_space=pltpu.VMEM),
        compiler_params=pltpu.CompilerParams(vmem_limit_bytes=SMALL_VMEM),
        name="inner_edge",
    )(modes)


def turn_kernel(keep_rows, modes, out_ref):
    n_modes, count = out_ref.shape
    step = count // 4
    for start in range(0, count, step):
        columns = slice(start, start + step)
        block = modes[columns, :].T
        if keep_rows % TILE_ROWS:
            out_ref[:, columns] = block
        else:
            for place, k in enumerate(sum(teams(n_modes // keep_rows), [])):
                rows = slice(place * keep_rows, (place + 1) * keep_rows)
                out_ref[rows, columns] = block[k * keep_rows : (k + 1) * keep_rows]


def turn(modes, keep_rows):
    count, n_modes = modes.shape
    return pl.pallas_call(
        functools.partial(turn_kernel, keep_rows),
        out_shape=jax.ShapeDtypeStruct((n_modes, count), modes.dtype),
        in_specs=[pl.BlockSpec(memory_space=pltpu.VMEM)],
        out_specs=pl.BlockSpec(memory_space=pltpu.VMEM),
        compiler_params=pltpu.CompilerParams(vmem_limit_bytes=SMALL_VMEM),
        cost_estimate=pl.CostEstimate(flops=0, bytes_accessed=4 * modes.size, transcendentals=0),
        name="turn",
    )(modes)


def own_kernel(blocks, nb_ref, jac, modes, turned, p_ref, t_ref, left, parts, live):
    slots, width, _ = jac.shape
    n_modes = modes.shape[1]
    mid = n_modes // 2

    base = nb_ref[1, 0]
    count = jnp.int32(0)
    for s in range(blocks, slots):
        r = nb_ref[0, s]
        live[0, count] = s
        live[1, count] = r
        live[2, count] = nb_ref[1, s] - base + 1
        count += (r >= 0).astype(jnp.int32)
    live[0, count] = 0
    live[1, count] = 0
    live[2, count] = blocks + 2

    for s in range(blocks):
        left[s + 1] = dot(turned[:, s * width : (s + 1) * width], jac[s])
    left[0] = jnp.zeros((n_modes, width), jnp.float32)
    left[blocks + 1] = jnp.zeros((n_modes, width), jnp.float32)

    def pair(k, carry):
        for j in (2 * k, 2 * k + 1):
            columns = pl.ds(pl.multiple_of(live[1, j] * width, width), width)
            left[live[2, j]] += dot(turned[:, columns], jac[live[0, j]])
        return carry

    lax.fori_loop(0, (count + 1) // 2, pair, 0)

    for c in range(blocks):
        upper, lower = halves(left[c + 1])
        parts[:n_modes, c * width : (c + 1) * width] = upper
        parts[n_modes:, c * width : (c + 1) * width] = lower
    both = dot(parts[...], modes[...])
    p_ref[...] = both[:n_modes] + both[n_modes:]
    for side, c in enumerate((0, blocks + 1)):
        upper, lower = halves(left[c])
        for half in range(2):
            t_ref[side, half, :mid] = upper[half * mid : (half + 1) * mid]
            t_ref[side, half, mid:] = lower[half * mid : (half + 1) * mid]


def own_part(neighbours, jac_blocks, modes, turned):
    slots, width, _ = jac_blocks.shape
    rows, n_modes = modes.shape
    blocks = rows // width
    flops = 2 * n_modes * width * width * slots + 4 * rows * n_modes * n_modes
    return pl.pallas_call(
        functools.partial(own_kernel, blocks),
        out_shape=(
            jax.ShapeDtypeStruct((n_modes, n_modes), jnp.float32),
            jax.ShapeDtypeStruct((2, 2, n_modes, width), jnp.bfloat16),
        ),
        in_specs=[
            pl.BlockSpec(memory_space=pltpu.SMEM),
            pl.BlockSpec(memory_space=pltpu.VMEM),
            pl.BlockSpec(memory_space=pltpu.VMEM),
            pl.BlockSpec(memory_space=pltpu.VMEM),
        ],
        out_specs=(pl.BlockSpec(memory_space=pltpu.VMEM), pl.BlockSpec(memory_space=pltpu.VMEM)),
        scratch_shapes=[
            pltpu.VMEM((blocks + 3, n_modes, width), jnp.float32),
            pltpu.VMEM((2 * n_modes, rows), jnp.bfloat16),
            pltpu.SMEM((3, slots + 1), jnp.int32),
        ],
        compiler_params=pltpu.CompilerParams(vmem_limit_bytes=OWN_VMEM),
        cost_estimate=pl.CostEstimate(
            flops=flops, bytes_accessed=slots * width * width * 2 + rows * n_modes * 2, transcendentals=0
        ),
        name="own_part",
    )(neighbours, jac_blocks, modes, turned)


def teams(count):
    chips = range(count // 2)
    middle = [chip for chip in (count // 4, count // 4 + 1) if 0 < chip < count // 2]
    rest = [chip for chip in chips if chip not in middle]
    rings = [middle + rest, middle + rest[:-2] + rest[: -3 : -1]]
    return [[2 * chip + (chip + half) % 2 for chip in reversed(rings[half])] for half in range(2)]


def own_team():
    me = lax.axis_index("cell")
    return lax.rem(me + me // 2, 2)


def regrouped(value, axis, keep_rows):
    first, second = teams(value.shape[axis] // keep_rows)
    starts = [k * keep_rows for k in first + second]
    return jnp.concatenate([lax.slice_in_dim(value, k, k + keep_rows, axis=axis) for k in starts], axis=axis)


def join_kernel(other, p_ref, t_ref, outer_ref, inner_ref, out_ref):
    core = lax.rem(lax.axis_index("cell"), 2)
    count = out_ref.shape[0]
    half = 1 - own_team() if other else own_team()
    rows = pl.ds(pl.multiple_of(half * count, TILE_ROWS), count)
    left = jnp.concatenate([t_ref[1 - core, half], t_ref[core, half]], axis=1)
    both = dot(left, jnp.concatenate([inner_ref[...], outer_ref[...]], axis=0))
    out_ref[...] = p_ref[rows, :] + both[:count] + both[count:]


def join(other, p, t, outer, inner):
    rows = p.shape[0] // 2
    return pl.pallas_call(
        functools.partial(join_kernel, other),
        out_shape=jax.ShapeDtypeStruct((rows, p.shape[1]), jnp.float32),
        in_specs=[pl.BlockSpec(memory_space=pltpu.VMEM)] * 4,
        out_specs=pl.BlockSpec(memory_space=pltpu.VMEM),
        compiler_params=pltpu.CompilerParams(vmem_limit_bytes=SMALL_VMEM),
        cost_estimate=pl.CostEstimate(flops=8 * rows * outer.size, bytes_accessed=0, transcendentals=0),
        name="join_give" if other else "join_keep",
    )(p, t, outer, inner)


def sum_kernel(parts_ref, out_hbm, total, sem):
    total[...] = jnp.sum(parts_ref[...], axis=0)
    copy = pltpu.make_async_copy(total, out_hbm, sem)
    copy.start()
    copy.wait()


def sum_parts(parts):
    return pl.pallas_call(
        sum_kernel,
        out_shape=jax.ShapeDtypeStruct(parts.shape[1:], parts.dtype),
        in_specs=[pl.BlockSpec(memory_space=pltpu.VMEM)],
        out_specs=pl.BlockSpec(memory_space=pl.ANY),
        scratch_shapes=[pltpu.VMEM(parts.shape[1:], parts.dtype), pltpu.SemaphoreType.DMA],
        compiler_params=pltpu.CompilerParams(vmem_limit_bytes=SMALL_VMEM),
        name="sum_parts",
    )(parts)


def per_device(jac_blocks, modes, neighbours):
    width = jac_blocks.shape[1]
    rows, n_modes = modes.shape
    count = lax.axis_size("cell")
    keep_rows = n_modes // count
    across = [(i, min(max(i - 1 + 2 * (i % 2), 0), count - 1)) for i in range(count)]
    swap = [(i, i ^ 1) for i in range(count)]
    core = lax.rem(lax.axis_index("cell"), 2)
    outer_edge = lax.dynamic_slice_in_dim(modes, core * (rows - width), width)
    outer = lax.ppermute(gate(outer_edge), "cell", across)
    inner = lax.ppermute(inner_edge(modes, width), "cell", swap)
    p, t = own_part(neighbours.T, jac_blocks, modes, turn(modes, keep_rows))
    if keep_rows % TILE_ROWS:
        p = regrouped(p, 0, keep_rows)
        apart = jnp.swapaxes(t.reshape(2, 2, 2, n_modes // 2, width), 1, 2).reshape(2, 2, n_modes, width)
        apart = regrouped(apart, 2, keep_rows).reshape(2, 2, 2, n_modes // 2, width)
        t = jnp.swapaxes(apart, 1, 2).reshape(t.shape)
    got = lax.ppermute(join(True, p, t, outer, inner), "cell", swap)
    keep = join(False, p, t, outer, inner)
    pair = (keep + got).reshape(count // 2, keep_rows, n_modes)
    parts = lax.all_to_all(pair, "cell", 0, 0, axis_index_groups=teams(count))
    return sum_parts(parts)


def solution(mesh):
    placed = (P(("grp", "cell"), None, None), P(("grp", "cell"), None), P(("grp", "cell"), None))
    return jax.shard_map(
        per_device, mesh=mesh, in_specs=placed, out_specs=P(("grp", "cell"), None), check_vma=False
    )
```

```python
import functools

import jax
import jax.numpy as jnp
from jax import lax
from jax.experimental import pallas as pl
from jax.experimental.pallas import tpu as pltpu
from jax.sharding import PartitionSpec as P

OWN_VMEM = 24 * 2**20
SMALL_VMEM = 8 * 2**20
TILE_ROWS = 16
LOAD_COST = 35 * 10**8


def dot(a, b):
    return jnp.dot(a, b, preferred_element_type=jnp.float32)


def halves(value):
    upper = value.astype(jnp.bfloat16)
    return upper, (value - upper.astype(jnp.float32)).astype(jnp.bfloat16)


def gate(block):
    return pl.pallas_call(
        lambda block_ref, out_ref: None,
        out_shape=jax.ShapeDtypeStruct(block.shape, block.dtype),
        in_specs=[pl.BlockSpec(memory_space=pl.ANY)],
        out_specs=pl.BlockSpec(memory_space=pl.ANY),
        input_output_aliases={0: 0},
        compiler_params=pltpu.CompilerParams(vmem_limit_bytes=SMALL_VMEM),
        cost_estimate=pl.CostEstimate(flops=LOAD_COST, bytes_accessed=0, transcendentals=0),
        name="gate",
    )(block)


def inner_kernel(modes, out_ref):
    width = out_ref.shape[0]
    head = modes[:width, :]
    tail = modes[modes.shape[0] - width :, :]
    out_ref[...] = jnp.where(lax.rem(lax.axis_index("cell"), 2) == 0, tail, head)


def inner_edge(modes, width):
    return pl.pallas_call(
        inner_kernel,
        out_shape=jax.ShapeDtypeStruct((width, modes.shape[1]), modes.dtype),
        in_specs=[pl.BlockSpec(memory_space=pltpu.VMEM)],
        out_specs=pl.BlockSpec(memory_space=pltpu.VMEM),
        compiler_params=pltpu.CompilerParams(vmem_limit_bytes=SMALL_VMEM),
        name="inner_edge",
    )(modes)


def turn_kernel(keep_rows, modes, out_ref):
    n_modes, count = out_ref.shape
    step = count // 4
    for start in range(0, count, step):
        columns = slice(start, start + step)
        block = modes[columns, :].T
        if keep_rows % TILE_ROWS:
            out_ref[:, columns] = block
        else:
            for place, k in enumerate(sum(teams(n_modes // keep_rows), [])):
                rows = slice(place * keep_rows, (place + 1) * keep_rows)
                out_ref[rows, columns] = block[k * keep_rows : (k + 1) * keep_rows]


def turn(modes, keep_rows):
    count, n_modes = modes.shape
    return pl.pallas_call(
        functools.partial(turn_kernel, keep_rows),
        out_shape=jax.ShapeDtypeStruct((n_modes, count), modes.dtype),
        in_specs=[pl.BlockSpec(memory_space=pltpu.VMEM)],
        out_specs=pl.BlockSpec(memory_space=pltpu.VMEM),
        compiler_params=pltpu.CompilerParams(vmem_limit_bytes=SMALL_VMEM),
        cost_estimate=pl.CostEstimate(flops=0, bytes_accessed=4 * modes.size, transcendentals=0),
        name="turn",
    )(modes)


def own_kernel(blocks, nb_hbm, jac, modes, turned, p_ref, t_ref, left, parts, live, nb_ref, sem):
    slots, width, _ = jac.shape
    n_modes = modes.shape[1]
    mid = n_modes // 2

    fetch = pltpu.make_async_copy(nb_hbm, nb_ref, sem)
    fetch.start()
    for s in range(blocks):
        left[s + 1] = dot(turned[:, s * width : (s + 1) * width], jac[s])
    left[0] = jnp.zeros((n_modes, width), jnp.float32)
    left[blocks + 1] = jnp.zeros((n_modes, width), jnp.float32)

    fetch.wait()
    base = nb_ref[1, 0]
    count = jnp.int32(0)
    for s in range(blocks, slots):
        r = nb_ref[0, s]
        live[0, count] = s
        live[1, count] = r
        live[2, count] = nb_ref[1, s] - base + 1
        count += (r >= 0).astype(jnp.int32)
    live[0, count] = 0
    live[1, count] = 0
    live[2, count] = blocks + 2

    def pair(k, carry):
        for j in (2 * k, 2 * k + 1):
            columns = pl.ds(pl.multiple_of(live[1, j] * width, width), width)
            left[live[2, j]] += dot(turned[:, columns], jac[live[0, j]])
        return carry

    lax.fori_loop(0, (count + 1) // 2, pair, 0)

    both = jnp.zeros((2 * n_modes, n_modes), jnp.float32)
    step = 2 if blocks % 2 == 0 else 1
    for first in range(0, blocks, step):
        for c in range(first, first + step):
            upper, lower = halves(left[c + 1])
            parts[:n_modes, c * width : (c + 1) * width] = upper
            parts[n_modes:, c * width : (c + 1) * width] = lower
        inner = slice(first * width, (first + step) * width)
        both += dot(parts[:, inner], modes[inner, :])
    p_ref[...] = both[:n_modes] + both[n_modes:]
    for side, c in enumerate((0, blocks + 1)):
        upper, lower = halves(left[c])
        for half in range(2):
            t_ref[side, half, :mid] = upper[half * mid : (half + 1) * mid]
            t_ref[side, half, mid:] = lower[half * mid : (half + 1) * mid]


def own_part(neighbours, jac_blocks, modes, turned):
    slots, width, _ = jac_blocks.shape
    rows, n_modes = modes.shape
    blocks = rows // width
    flops = 2 * n_modes * width * width * slots + 4 * rows * n_modes * n_modes
    return pl.pallas_call(
        functools.partial(own_kernel, blocks),
        out_shape=(
            jax.ShapeDtypeStruct((n_modes, n_modes), jnp.float32),
            jax.ShapeDtypeStruct((2, 2, n_modes, width), jnp.bfloat16),
        ),
        in_specs=[
            pl.BlockSpec(memory_space=pltpu.HBM),
            pl.BlockSpec(memory_space=pltpu.VMEM),
            pl.BlockSpec(memory_space=pltpu.VMEM),
            pl.BlockSpec(memory_space=pltpu.VMEM),
        ],
        out_specs=(pl.BlockSpec(memory_space=pltpu.VMEM), pl.BlockSpec(memory_space=pltpu.VMEM)),
        scratch_shapes=[
            pltpu.VMEM((blocks + 3, n_modes, width), jnp.float32),
            pltpu.VMEM((2 * n_modes, rows), jnp.bfloat16),
            pltpu.SMEM((3, slots + 1), jnp.int32),
            pltpu.SMEM(neighbours.shape, jnp.int32),
            pltpu.SemaphoreType.DMA,
        ],
        compiler_params=pltpu.CompilerParams(vmem_limit_bytes=OWN_VMEM),
        cost_estimate=pl.CostEstimate(
            flops=flops, bytes_accessed=slots * width * width * 2 + rows * n_modes * 2, transcendentals=0
        ),
        name="own_part",
    )(pltpu.with_memory_space_constraint(neighbours, pltpu.HBM), jac_blocks, modes, turned)


def teams(count):
    chips = range(count // 2)
    middle = [chip for chip in (count // 4, count // 4 + 1) if 0 < chip < count // 2]
    rest = [chip for chip in chips if chip not in middle]
    rings = [middle + rest, middle + rest[:-2] + rest[: -3 : -1]]
    return [[2 * chip + (chip + half) % 2 for chip in reversed(rings[half])] for half in range(2)]


def own_team():
    me = lax.axis_index("cell")
    return lax.rem(me + me // 2, 2)


def regrouped(value, axis, keep_rows):
    first, second = teams(value.shape[axis] // keep_rows)
    starts = [k * keep_rows for k in first + second]
    return jnp.concatenate([lax.slice_in_dim(value, k, k + keep_rows, axis=axis) for k in starts], axis=axis)


def join_kernel(other, p_ref, t_ref, outer_ref, inner_ref, out_ref):
    core = lax.rem(lax.axis_index("cell"), 2)
    count = out_ref.shape[0]
    half = 1 - own_team() if other else own_team()
    rows = pl.ds(pl.multiple_of(half * count, TILE_ROWS), count)
    left = jnp.concatenate([t_ref[1 - core, half], t_ref[core, half]], axis=1)
    both = dot(left, jnp.concatenate([inner_ref[...], outer_ref[...]], axis=0))
    out_ref[...] = p_ref[rows, :] + both[:count] + both[count:]


def join(other, p, t, outer, inner):
    rows = p.shape[0] // 2
    return pl.pallas_call(
        functools.partial(join_kernel, other),
        out_shape=jax.ShapeDtypeStruct((rows, p.shape[1]), jnp.float32),
        in_specs=[pl.BlockSpec(memory_space=pltpu.VMEM)] * 4,
        out_specs=pl.BlockSpec(memory_space=pltpu.VMEM),
        compiler_params=pltpu.CompilerParams(vmem_limit_bytes=SMALL_VMEM),
        cost_estimate=pl.CostEstimate(flops=8 * rows * outer.size, bytes_accessed=0, transcendentals=0),
        name="join_give" if other else "join_keep",
    )(p, t, outer, inner)


def sum_kernel(parts_ref, out_hbm, total, sem):
    total[...] = jnp.sum(parts_ref[...], axis=0)
    copy = pltpu.make_async_copy(total, out_hbm, sem)
    copy.start()
    copy.wait()


def sum_parts(parts):
    return pl.pallas_call(
        sum_kernel,
        out_shape=jax.ShapeDtypeStruct(parts.shape[1:], parts.dtype),
        in_specs=[pl.BlockSpec(memory_space=pltpu.VMEM)],
        out_specs=pl.BlockSpec(memory_space=pl.ANY),
        scratch_shapes=[pltpu.VMEM(parts.shape[1:], parts.dtype), pltpu.SemaphoreType.DMA],
        compiler_params=pltpu.CompilerParams(vmem_limit_bytes=SMALL_VMEM),
        name="sum_parts",
    )(parts)


def per_device(jac_blocks, modes, neighbours):
    width = jac_blocks.shape[1]
    rows, n_modes = modes.shape
    count = lax.axis_size("cell")
    keep_rows = n_modes // count
    across = [(i, min(max(i - 1 + 2 * (i % 2), 0), count - 1)) for i in range(count)]
    swap = [(i, i ^ 1) for i in range(count)]
    core = lax.rem(lax.axis_index("cell"), 2)
    outer_edge = lax.dynamic_slice_in_dim(modes, core * (rows - width), width)
    outer = lax.ppermute(gate(outer_edge), "cell", across)
    inner = lax.ppermute(inner_edge(modes, width), "cell", swap)
    p, t = own_part(neighbours.T, jac_blocks, modes, turn(modes, keep_rows))
    if keep_rows % TILE_ROWS:
        p = regrouped(p, 0, keep_rows)
        apart = jnp.swapaxes(t.reshape(2, 2, 2, n_modes // 2, width), 1, 2).reshape(2, 2, n_modes, width)
        apart = regrouped(apart, 2, keep_rows).reshape(2, 2, 2, n_modes // 2, width)
        t = jnp.swapaxes(apart, 1, 2).reshape(t.shape)
    got = lax.ppermute(join(True, p, t, outer, inner), "cell", swap)
    keep = join(False, p, t, outer, inner)
    pair = (keep + got).reshape(count // 2, keep_rows, n_modes)
    parts = lax.all_to_all(pair, "cell", 0, 0, axis_index_groups=teams(count))
    return sum_parts(parts)


def solution(mesh):
    placed = (P(("grp", "cell"), None, None), P(("grp", "cell"), None), P(("grp", "cell"), None))
    return jax.shard_map(
        per_device, mesh=mesh, in_specs=placed, out_specs=P(("grp", "cell"), None), check_vma=False
    )
```

```python
import functools

import jax
import jax.numpy as jnp
from jax import lax
from jax.experimental import pallas as pl
from jax.experimental.pallas import tpu as pltpu
from jax.sharding import PartitionSpec as P

OWN_VMEM = 24 * 2**20
SMALL_VMEM = 8 * 2**20
TILE_ROWS = 16
LOAD_COST = 35 * 10**8


def dot(a, b):
    return jnp.dot(a, b, preferred_element_type=jnp.float32)


def halves(value):
    upper = value.astype(jnp.bfloat16)
    return upper, (value - upper.astype(jnp.float32)).astype(jnp.bfloat16)


def gate(block):
    return pl.pallas_call(
        lambda block_ref, out_ref: None,
        out_shape=jax.ShapeDtypeStruct(block.shape, block.dtype),
        in_specs=[pl.BlockSpec(memory_space=pl.ANY)],
        out_specs=pl.BlockSpec(memory_space=pl.ANY),
        input_output_aliases={0: 0},
        compiler_params=pltpu.CompilerParams(vmem_limit_bytes=SMALL_VMEM),
        cost_estimate=pl.CostEstimate(flops=LOAD_COST, bytes_accessed=0, transcendentals=0),
        name="gate",
    )(block)


def inner_kernel(modes, out_ref):
    width = out_ref.shape[0]
    head = modes[:width, :]
    tail = modes[modes.shape[0] - width :, :]
    out_ref[...] = jnp.where(lax.rem(lax.axis_index("cell"), 2) == 0, tail, head)


def inner_edge(modes, width):
    return pl.pallas_call(
        inner_kernel,
        out_shape=jax.ShapeDtypeStruct((width, modes.shape[1]), modes.dtype),
        in_specs=[pl.BlockSpec(memory_space=pltpu.VMEM)],
        out_specs=pl.BlockSpec(memory_space=pltpu.VMEM),
        compiler_params=pltpu.CompilerParams(vmem_limit_bytes=SMALL_VMEM),
        name="inner_edge",
    )(modes)


def turn_kernel(keep_rows, modes, out_ref):
    n_modes, count = out_ref.shape
    step = count // 4
    for start in range(0, count, step):
        columns = slice(start, start + step)
        block = modes[columns, :].T
        if keep_rows % TILE_ROWS:
            out_ref[:, columns] = block
        else:
            for place, k in enumerate(sum(teams(n_modes // keep_rows), [])):
                rows = slice(place * keep_rows, (place + 1) * keep_rows)
                out_ref[rows, columns] = block[k * keep_rows : (k + 1) * keep_rows]


def turn(modes, keep_rows):
    count, n_modes = modes.shape
    return pl.pallas_call(
        functools.partial(turn_kernel, keep_rows),
        out_shape=jax.ShapeDtypeStruct((n_modes, count), modes.dtype),
        in_specs=[pl.BlockSpec(memory_space=pltpu.VMEM)],
        out_specs=pl.BlockSpec(memory_space=pltpu.VMEM),
        compiler_params=pltpu.CompilerParams(vmem_limit_bytes=SMALL_VMEM),
        cost_estimate=pl.CostEstimate(flops=0, bytes_accessed=4 * modes.size, transcendentals=0),
        name="turn",
    )(modes)


def own_kernel(blocks, nb_hbm, jac, modes, turned, p_ref, t_ref, left, parts, live, nb_ref, sem):
    slots, width, _ = jac.shape
    n_modes = modes.shape[1]
    mid = n_modes // 2

    fetch = pltpu.make_async_copy(nb_hbm, nb_ref, sem)
    fetch.start()
    for s in range(blocks):
        left[s + 1] = dot(turned[:, s * width : (s + 1) * width], jac[s])
    left[0] = jnp.zeros((n_modes, width), jnp.float32)
    left[blocks + 1] = jnp.zeros((n_modes, width), jnp.float32)

    fetch.wait()
    base = nb_ref[1, 0]
    count = jnp.int32(0)
    for s in range(blocks, slots):
        r = nb_ref[0, s]
        live[0, count] = s
        live[1, count] = r
        live[2, count] = nb_ref[1, s] - base + 1
        count += (r >= 0).astype(jnp.int32)
    live[0, count] = 0
    live[1, count] = 0
    live[2, count] = blocks + 2

    def pair(k, carry):
        for j in (2 * k, 2 * k + 1):
            columns = pl.ds(pl.multiple_of(live[1, j] * width, width), width)
            left[live[2, j]] += dot(turned[:, columns], jac[live[0, j]])
        return carry

    lax.fori_loop(0, (count + 1) // 2, pair, 0)

    both = jnp.zeros((2 * n_modes, n_modes), jnp.float32)
    step = 2 if blocks % 2 == 0 else 1
    for first in range(0, blocks, step):
        for c in range(first, first + step):
            upper, lower = halves(left[c + 1])
            parts[:n_modes, c * width : (c + 1) * width] = upper
            parts[n_modes:, c * width : (c + 1) * width] = lower
        inner = slice(first * width, (first + step) * width)
        both += dot(parts[:, inner], modes[inner, :])
    p_ref[...] = both[:n_modes] + both[n_modes:]
    for side, c in enumerate((0, blocks + 1)):
        upper, lower = halves(left[c])
        for half in range(2):
            t_ref[side, half, :mid] = upper[half * mid : (half + 1) * mid]
            t_ref[side, half, mid:] = lower[half * mid : (half + 1) * mid]


def own_part(neighbours, jac_blocks, modes, turned):
    slots, width, _ = jac_blocks.shape
    rows, n_modes = modes.shape
    blocks = rows // width
    flops = 2 * n_modes * width * width * slots + 4 * rows * n_modes * n_modes
    return pl.pallas_call(
        functools.partial(own_kernel, blocks),
        out_shape=(
            jax.ShapeDtypeStruct((n_modes, n_modes), jnp.float32),
            jax.ShapeDtypeStruct((2, 2, n_modes, width), jnp.bfloat16),
        ),
        in_specs=[
            pl.BlockSpec(memory_space=pltpu.HBM),
            pl.BlockSpec(memory_space=pltpu.VMEM),
            pl.BlockSpec(memory_space=pltpu.VMEM),
            pl.BlockSpec(memory_space=pltpu.VMEM),
        ],
        out_specs=(pl.BlockSpec(memory_space=pltpu.VMEM), pl.BlockSpec(memory_space=pltpu.VMEM)),
        scratch_shapes=[
            pltpu.VMEM((blocks + 3, n_modes, width), jnp.float32),
            pltpu.VMEM((2 * n_modes, rows), jnp.bfloat16),
            pltpu.SMEM((3, slots + 1), jnp.int32),
            pltpu.SMEM(neighbours.shape, jnp.int32),
            pltpu.SemaphoreType.DMA,
        ],
        compiler_params=pltpu.CompilerParams(vmem_limit_bytes=OWN_VMEM),
        cost_estimate=pl.CostEstimate(
            flops=flops, bytes_accessed=slots * width * width * 2 + rows * n_modes * 2, transcendentals=0
        ),
        name="own_part",
    )(pltpu.with_memory_space_constraint(neighbours, pltpu.HBM), jac_blocks, modes, turned)


def teams(count):
    chips = range(count // 2)
    middle = [chip for chip in (count // 4, count // 4 + 1) if 0 < chip < count // 2]
    rest = [chip for chip in chips if chip not in middle]
    near = count // 8
    rings = [[chip for chip in rest if chip != near] + [near] + middle, middle + rest[:-2] + rest[: -3 : -1]]
    return [[2 * chip + (chip + half) % 2 for chip in reversed(rings[half])] for half in range(2)]


def own_team():
    me = lax.axis_index("cell")
    return lax.rem(me + me // 2, 2)


def regrouped(value, axis, keep_rows):
    first, second = teams(value.shape[axis] // keep_rows)
    starts = [k * keep_rows for k in first + second]
    return jnp.concatenate([lax.slice_in_dim(value, k, k + keep_rows, axis=axis) for k in starts], axis=axis)


def join_kernel(other, p_ref, t_ref, outer_ref, inner_ref, out_ref):
    core = lax.rem(lax.axis_index("cell"), 2)
    count = out_ref.shape[0]
    half = 1 - own_team() if other else own_team()
    rows = pl.ds(pl.multiple_of(half * count, TILE_ROWS), count)
    left = jnp.concatenate([t_ref[1 - core, half], t_ref[core, half]], axis=1)
    both = dot(left, jnp.concatenate([inner_ref[...], outer_ref[...]], axis=0))
    out_ref[...] = p_ref[rows, :] + both[:count] + both[count:]


def join(other, p, t, outer, inner):
    rows = p.shape[0] // 2
    return pl.pallas_call(
        functools.partial(join_kernel, other),
        out_shape=jax.ShapeDtypeStruct((rows, p.shape[1]), jnp.float32),
        in_specs=[pl.BlockSpec(memory_space=pltpu.VMEM)] * 4,
        out_specs=pl.BlockSpec(memory_space=pltpu.VMEM),
        compiler_params=pltpu.CompilerParams(vmem_limit_bytes=SMALL_VMEM),
        cost_estimate=pl.CostEstimate(flops=8 * rows * outer.size, bytes_accessed=0, transcendentals=0),
        name="join_give" if other else "join_keep",
    )(p, t, outer, inner)


def sum_kernel(parts_ref, out_hbm, total, sem):
    total[...] = jnp.sum(parts_ref[...], axis=0)
    copy = pltpu.make_async_copy(total, out_hbm, sem)
    copy.start()
    copy.wait()


def sum_parts(parts):
    return pl.pallas_call(
        sum_kernel,
        out_shape=jax.ShapeDtypeStruct(parts.shape[1:], parts.dtype),
        in_specs=[pl.BlockSpec(memory_space=pltpu.VMEM)],
        out_specs=pl.BlockSpec(memory_space=pl.ANY),
        scratch_shapes=[pltpu.VMEM(parts.shape[1:], parts.dtype), pltpu.SemaphoreType.DMA],
        compiler_params=pltpu.CompilerParams(vmem_limit_bytes=SMALL_VMEM),
        name="sum_parts",
    )(parts)


def per_device(jac_blocks, modes, neighbours):
    width = jac_blocks.shape[1]
    rows, n_modes = modes.shape
    count = lax.axis_size("cell")
    keep_rows = n_modes // count
    across = [(i, min(max(i - 1 + 2 * (i % 2), 0), count - 1)) for i in range(count)]
    swap = [(i, i ^ 1) for i in range(count)]
    core = lax.rem(lax.axis_index("cell"), 2)
    outer_edge = lax.dynamic_slice_in_dim(modes, core * (rows - width), width)
    outer = lax.ppermute(gate(outer_edge), "cell", across)
    inner = lax.ppermute(inner_edge(modes, width), "cell", swap)
    p, t = own_part(neighbours.T, jac_blocks, modes, turn(modes, keep_rows))
    if keep_rows % TILE_ROWS:
        p = regrouped(p, 0, keep_rows)
        apart = jnp.swapaxes(t.reshape(2, 2, 2, n_modes // 2, width), 1, 2).reshape(2, 2, n_modes, width)
        apart = regrouped(apart, 2, keep_rows).reshape(2, 2, 2, n_modes // 2, width)
        t = jnp.swapaxes(apart, 1, 2).reshape(t.shape)
    got = lax.ppermute(join(True, p, t, outer, inner), "cell", swap)
    keep = join(False, p, t, outer, inner)
    pair = (keep + got).reshape(count // 2, keep_rows, n_modes)
    parts = lax.all_to_all(pair, "cell", 0, 0, axis_index_groups=teams(count))
    return sum_parts(parts)


def solution(mesh):
    placed = (P(("grp", "cell"), None, None), P(("grp", "cell"), None), P(("grp", "cell"), None))
    return jax.shard_map(
        per_device, mesh=mesh, in_specs=placed, out_specs=P(("grp", "cell"), None), check_vma=False
    )
```
